128 devices in a mesh: dp: 16 (over y_hi, z, core), tensor: 8 (over y_lo, x).
Axes of the slice: x: 4, y: 4 (y_hi: 2, y_lo: 2; y = y_hi * 2 + y_lo), z: 4, core: 2. Of those that a mesh axis runs over, the one named last changes fastest.
Arguments:
- block_input: bfloat16 [24576, 1024], P(('dp', 'tensor')), may hold values from -6 to 6
- out_cotangent: bfloat16 [24576, 1024], P(('dp', 'tensor')), may hold values from -6 to 6
- lengths: int32 [16], P('dp'), may hold values from 1024 to 1536, as said below
- mixer_gain: float32 [1024], replicated, may hold values from 0.5 to 1.5
- query_weight: bfloat16 [1024, 1024], P('dp', 'tensor'), may hold values from -0.1875 to 0.1875
- key_weight: bfloat16 [1024, 1024], P('dp', 'tensor'), may hold values from -0.1875 to 0.1875
- value_weight: bfloat16 [1024, 2048], P('dp', 'tensor'), may hold values from -0.1875 to 0.1875
- output_gate_weight: bfloat16 [1024, 2048], P('dp', 'tensor'), may hold values from -0.1875 to 0.1875
- decay_weight: bfloat16 [1024, 8, 2], P('dp', 'tensor'), may hold values from -0.1875 to 0.1875
- query_conv: float32 [4, 1024], P(None, 'tensor'), may hold values from -3 to 3
- key_conv: float32 [4, 1024], P(None, 'tensor'), may hold values from -3 to 3
- value_conv: float32 [4, 2048], P(None, 'tensor'), may hold values from -3 to 3
- decay_log: float32 [8], P('tensor'), may hold values from -6 to -2
- decay_bias: float32 [8], P('tensor'), may hold values from -2 to 1
- head_gain: float32 [256], replicated, may hold values from 0.5 to 1.5
- out_weight: bfloat16 [2048, 1024], P('tensor', 'dp'), may hold values from -0.25 to 0.25
- ffn_gain: float32 [1024], replicated, may hold values from 0.5 to 1.5
- ffn_gate: bfloat16 [1024, 2816], P('dp', 'tensor'), may hold values from -0.1875 to 0.1875
- ffn_up: bfloat16 [1024, 2816], P('dp', 'tensor'), may hold values from -0.1875 to 0.1875
- ffn_down: bfloat16 [2816, 1024], P('tensor', 'dp'), may hold values from -0.109375 to 0.109375
Outputs:
- block_output: bfloat16 [24576, 1024], P(('dp', 'tensor'))
- input_grad: float32 [24576, 1024], P(('dp', 'tensor'))
- mixer_gain_grad: float32 [1024], replicated
- query_weight_grad: float32 [1024, 1024], P('dp', 'tensor')
- key_weight_grad: float32 [1024, 1024], P('dp', 'tensor')
- value_weight_grad: float32 [1024, 2048], P('dp', 'tensor')
- output_gate_weight_grad: float32 [1024, 2048], P('dp', 'tensor')
- decay_weight_grad: float32 [1024, 8, 2], P('dp', 'tensor')
- query_conv_grad: float32 [4, 1024], P(None, 'tensor')
- key_conv_grad: float32 [4, 1024], P(None, 'tensor')
- value_conv_grad: float32 [4, 2048], P(None, 'tensor')
- decay_log_grad: float32 [8], P('tensor')
- decay_bias_grad: float32 [8], P('tensor')
- head_gain_grad: float32 [256], replicated
- out_weight_grad: float32 [2048, 1024], P('tensor', 'dp')
- ffn_gain_grad: float32 [1024], replicated
- ffn_gate_grad: float32 [1024, 2816], P('dp', 'tensor')
- ffn_up_grad: float32 [1024, 2816], P('dp', 'tensor')
- ffn_down_grad: float32 [2816, 1024], P('tensor', 'dp')
The draws below stay inside these ranges and needn't reach their ends.
Inputs may be any that keep to these rules, and one draw needn't show every extreme that they name: lengths[g] is a multiple of 64; some group is full and some holds exactly 1024 rows.
All inputs are finite; a program needn't handle non-finite values.
Results may differ from the reference program's by a relative error of at most 0.025.
Values may be sent and summed in bfloat16 or wider, within the bound.
A program may use at most 128 MiB of HBM per device.

```python
import jax
import jax.numpy as jnp
from jax import lax

D = 1024
HEADS = 8
DK = 128
DV = 256
FF = 2816
CONV = 4
SPAN = 64
SEQ_MIN = 1024
ROWS = 1536
GROUPS = 16
TOKENS = 24576
KEYS = 1024
VALS = 2048


def draw_lengths(key, part):
    key = jax.random.fold_in(key, 11)
    first_key, second_key, third_key = jax.random.split(key, 3)
    span_count = ROWS // SPAN
    fewest = SEQ_MIN // SPAN
    counts = jax.random.randint(first_key, (GROUPS,), fewest, span_count + 1)
    full_group = jax.random.randint(second_key, (), 0, GROUPS)
    short_group = (full_group + jax.random.randint(third_key, (), 1, GROUPS)) % GROUPS
    group_ids = jnp.arange(GROUPS)
    counts = jnp.where(group_ids == full_group, span_count, counts)
    counts = jnp.where(group_ids == short_group, fewest, counts)
    return (counts * SPAN).astype(jnp.int32)


def levels(key, extent, pieces, low, top_value):
    factor_of = 1.0
    for position, shards_of in pieces:
        draws = jax.random.uniform(jax.random.fold_in(jax.random.fold_in(key, 6), position), (shards_of,), jnp.float32, low / len(pieces), top_value / len(pieces))
        factor_of = factor_of * jnp.repeat(jnp.exp(draws), extent[position] // shards_of).reshape((-1,) + (1,) * (len(extent) - 1 - position))
    return factor_of


def scatter_about(key, dims, scale, bound, pieces=(), kind=jnp.bfloat16):
    loudness = levels(key, dims, pieces, -0.22, 0.18) if pieces else 1.0
    values = jax.random.normal(key, dims, jnp.float32) * scale * loudness
    return jnp.minimum(jnp.maximum(values, -bound), bound).astype(kind)


def setup_inputs(seed: int = 0) -> dict:
    keys = jax.random.split(jax.random.key(seed), 21)
    return {
        "block_input": scatter_about(keys[0], (TOKENS, D), 1.0, 6.0, ((0, 128),)),
        "out_cotangent": scatter_about(keys[1], (TOKENS, D), 1.0, 6.0, ((0, 128),)),
        "lengths": draw_lengths(jax.random.fold_in(keys[20], 71), 0),
        "mixer_gain": jnp.clip(1.0 + 0.1 * jax.random.normal(keys[3], (D,), jnp.float32), 0.5, 1.5),
        "query_weight": scatter_about(keys[4], (D, KEYS), D ** -0.5, 0.1875, ((0, 16), (1, 8))),
        "key_weight": scatter_about(keys[5], (D, KEYS), D ** -0.5, 0.1875, ((0, 16), (1, 8))),
        "value_weight": scatter_about(keys[6], (D, VALS), D ** -0.5, 0.1875, ((0, 16), (1, 8))),
        "output_gate_weight": scatter_about(keys[7], (D, VALS), D ** -0.5, 0.1875, ((0, 16), (1, 8))),
        "decay_weight": scatter_about(keys[8], (D, HEADS, 2), D ** -0.5, 0.1875, ((0, 16), (1, 8))),
        "query_conv": scatter_about(keys[9], (CONV, KEYS), CONV ** -0.5, 3.0, ((1, 8),), jnp.float32),
        "key_conv": scatter_about(keys[10], (CONV, KEYS), CONV ** -0.5, 3.0, ((1, 8),), jnp.float32),
        "value_conv": scatter_about(keys[11], (CONV, VALS), CONV ** -0.5, 3.0, ((1, 8),), jnp.float32),
        "decay_log": jnp.clip(-6.0 + 4.0 * jax.random.uniform(keys[12], (HEADS,), jnp.float32) ** levels(keys[12], (HEADS,), ((0, 8),), -0.2, 0.2), -6.0, -2.0),
        "decay_bias": jnp.clip(-2.0 + 3.0 * jax.random.uniform(keys[13], (HEADS,), jnp.float32) ** levels(keys[13], (HEADS,), ((0, 8),), -0.2, 0.2), -2.0, 1.0),
        "head_gain": jnp.clip(1.0 + 0.1 * jax.random.normal(keys[14], (DV,), jnp.float32), 0.5, 1.5),
        "out_weight": scatter_about(keys[15], (VALS, D), (VALS // 4) ** -0.5, 0.25, ((0, 8), (1, 16))),
        "ffn_gain": jnp.clip(1.0 + 0.1 * jax.random.normal(keys[16], (D,), jnp.float32), 0.5, 1.5),
        "ffn_gate": scatter_about(keys[17], (D, FF), D ** -0.5, 0.1875, ((0, 16), (1, 8))),
        "ffn_up": scatter_about(keys[18], (D, FF), D ** -0.5, 0.1875, ((0, 16), (1, 8))),
        "ffn_down": scatter_about(keys[19], (FF, D), FF ** -0.5, 0.109375, ((0, 8), (1, 16))),
    }


norm_eps = 1e-06
gate_eps = 1e-05

@jax.custom_vjp
def low(v):
    return lax.optimization_barrier(v.astype(jnp.bfloat16)).astype(jnp.float32)

@jax.custom_vjp
def low_back(v):
    return v

def low_keep(v):
    return (low(v), None)

def low_pass(kept, grad):
    return (grad,)

def back_keep(v):
    return (v, None)

def back_low(kept, grad):
    return (low(grad),)
low.defvjp(low_keep, low_pass)
low_back.defvjp(back_keep, back_low)

def exact_dot(left_side, right_side):
    return jnp.dot(left_side, right_side, precision=lax.Precision.HIGHEST)

def rms_scale(values, scale_gain):
    return values * lax.rsqrt(lax.optimization_barrier(jnp.mean(values * values, axis=-1, keepdims=True)) + norm_eps) * scale_gain

def causal_conv(values, weight):
    row_count = values.shape[0]
    taps_count = weight.shape[0]
    padded = jnp.concatenate([jnp.zeros((taps_count - 1, values.shape[1]), values.dtype), values], axis=0)
    summed = jnp.zeros_like(values)
    for offset in range(taps_count):
        summed = summed + weight[offset] * padded[offset:offset + row_count]
    return jax.nn.silu(summed)

def unit_inverse(lower_part):
    size_now = lower_part.shape[0]
    identity = jnp.eye(size_now, dtype=lower_part.dtype)
    powered = lower_part
    inverse = identity - lower_part
    degree = 2
    while degree < size_now:
        powered = exact_dot(powered, powered)
        inverse = exact_dot(inverse, identity + powered)
        degree = degree * 2
    return inverse

def block_step(memory, block_items):
    queries, keys_in, values, decays, write_rate = block_items
    cumul_decay = jnp.cumsum(decays)
    indices = jnp.arange(decays.shape[0])
    strict_mask = indices[:, None] > indices[None, :]
    causal_mask = indices[:, None] >= indices[None, :]
    spread = cumul_decay[:, None] - cumul_decay[None, :]
    strict_ratio = jnp.where(strict_mask, jnp.exp(jnp.where(strict_mask, spread, 0.0)), 0.0)
    causal_ratio = jnp.where(causal_mask, jnp.exp(jnp.where(causal_mask, spread, 0.0)), 0.0)
    lower_part = write_rate[:, None] * exact_dot(keys_in, keys_in.T) * strict_ratio
    inverse = unit_inverse(lower_part)
    growth = jnp.exp(cumul_decay)
    target = write_rate[:, None] * (values - exact_dot(growth[:, None] * keys_in, memory.T))
    fresh = exact_dot(inverse, target)
    scores = exact_dot(queries, keys_in.T) * causal_ratio
    result = exact_dot(growth[:, None] * queries, memory.T) + exact_dot(scores, fresh)
    tail_decay = jnp.exp(cumul_decay[-1] - cumul_decay)
    memory = growth[-1] * memory + exact_dot(fresh.T, tail_decay[:, None] * keys_in)
    return (memory, result)

def delta_head(queries, keys_in, values, decays, write_rate):
    row_count = decays.shape[0]
    blocks_count = row_count // SPAN

    def into_blocks(array):
        return array.reshape((blocks_count, SPAN) + array.shape[1:])
    start_memory = jnp.zeros((DV, DK), jnp.float32)
    final_memory, results = lax.scan(jax.checkpoint(block_step), start_memory, (into_blocks(queries), into_blocks(keys_in), into_blocks(values), into_blocks(decays), into_blocks(write_rate)))
    return results.reshape(row_count, DV)

def mixer_core(query_pre, key_pre, value_pre, gate_pre, decay_pre, query_conv, key_conv, value_conv, decay_log, decay_bias, head_gain):
    row_count = query_pre.shape[0]
    head_count = query_pre.shape[1] // DK
    queries = causal_conv(query_pre, query_conv).reshape(row_count, head_count, DK)
    keys_in = causal_conv(key_pre, key_conv).reshape(row_count, head_count, DK)
    values = causal_conv(value_pre, value_conv).reshape(row_count, head_count, DV)
    queries = queries * lax.rsqrt(lax.optimization_barrier(jnp.sum(queries * queries, axis=-1, keepdims=True)) + norm_eps) * DK ** (-0.5)
    keys_in = keys_in * lax.rsqrt(lax.optimization_barrier(jnp.sum(keys_in * keys_in, axis=-1, keepdims=True)) + norm_eps)
    decays = -jnp.exp(decay_log) * jax.nn.softplus(decay_pre[:, :, 0] + decay_bias)
    write_rate = jax.nn.sigmoid(decay_pre[:, :, 1])
    outputs = jax.vmap(delta_head, in_axes=1, out_axes=1)(queries, keys_in, values, decays, write_rate)
    normed = outputs * lax.rsqrt(lax.optimization_barrier(jnp.mean(outputs * outputs, axis=-1, keepdims=True)) + gate_eps) * head_gain
    gated = normed * jax.nn.silu(gate_pre.reshape(row_count, head_count, DV))
    return gated.reshape(row_count, head_count * DV)

def group_forward(inputs, group_length, weights):
    mixer_gain, query_weight, key_weight, value_weight, output_gate_weight, decay_weight, query_conv, key_conv, value_conv, decay_log, decay_bias, head_gain, out_weight, ffn_gain, ffn_gate, ffn_up, ffn_down = weights
    live_rows = (jnp.arange(ROWS, dtype=jnp.int32) < group_length).astype(jnp.float32)[:, None]
    first = low(rms_scale(inputs, mixer_gain))
    query_pre = low_back(exact_dot(first, query_weight))
    key_pre = low_back(exact_dot(first, key_weight))
    value_pre = low_back(exact_dot(first, value_weight))
    gate_pre = low_back(exact_dot(first, output_gate_weight))
    decay_pre = low_back(jnp.einsum('rd,dhc->rhc', first, decay_weight, precision=lax.Precision.HIGHEST))
    gated = mixer_core(query_pre, key_pre, value_pre, gate_pre, decay_pre, query_conv, key_conv, value_conv, decay_log, decay_bias, head_gain)
    mixed_rows = low(gated)
    mixed = low_back(exact_dot(mixed_rows, out_weight))
    middle = inputs + live_rows * mixed
    second = low(rms_scale(middle, ffn_gain))
    gate_act = low_back(exact_dot(second, ffn_gate))
    up_act = low_back(exact_dot(second, ffn_up))
    hidden = low(jax.nn.silu(gate_act) * up_act)
    ffn_terms = low_back(exact_dot(hidden, ffn_down))
    return middle + live_rows * ffn_terms

def reference(block_input, out_cotangent, lengths, mixer_gain, query_weight, key_weight, value_weight, output_gate_weight, decay_weight, query_conv, key_conv, value_conv, decay_log, decay_bias, head_gain, out_weight, ffn_gain, ffn_gate, ffn_up, ffn_down):
    weights = tuple((item.astype(jnp.float32) for item in (mixer_gain, query_weight, key_weight, value_weight, output_gate_weight, decay_weight, query_conv, key_conv, value_conv, decay_log, decay_bias, head_gain, out_weight, ffn_gain, ffn_gate, ffn_up, ffn_down)))
    inputs = block_input.astype(jnp.float32).reshape(GROUPS, ROWS, D)
    cotangent = out_cotangent.astype(jnp.float32).reshape(GROUPS, ROWS, D)

    def group_step(totals, group_items):
        group_inputs, group_cot, group_length = group_items

        def forward_only(input_rows, weight_set):
            return group_forward(input_rows, group_length, weight_set)
        result, pullback = jax.vjp(forward_only, group_inputs, weights)
        grad_inputs, grad_weights = pullback(group_cot)
        totals = jax.tree.map(jnp.add, totals, grad_weights)
        return (totals, (result.astype(jnp.bfloat16), grad_inputs))
    zero_totals = jax.tree.map(jnp.zeros_like, weights)
    totals, (outputs, input_grads) = lax.scan(group_step, zero_totals, (inputs, cotangent, lengths))
    return (outputs.reshape(TOKENS, D), input_grads.reshape(TOKENS, D), totals[0], totals[1], totals[2], totals[3], totals[4], totals[5], totals[6], totals[7], totals[8], totals[9], totals[10], totals[11], totals[12], totals[13], totals[14], totals[15], totals[16])
```

```python
import functools

import jax
import jax.numpy as jnp
from jax import lax
from jax.experimental import pallas as pl
from jax.experimental.pallas import tpu as pltpu
from jax.sharding import PartitionSpec as P

DK = 128
DV = 256
QKV = 2 * DK + DV
D = 1024
CHUNK = 256
BATCH = 2

norm_eps = 1e-06
gate_eps = 1e-05
bf16 = jnp.bfloat16
f32 = jnp.float32


def mm(left_side, right_side, left_dim=1, right_dim=0):
    return lax.dot_general(
        left_side.astype(bf16),
        right_side.astype(bf16),
        (((left_dim,), (right_dim,)), ((), ())),
        preferred_element_type=f32,
    )


def halves(values):
    high = values.astype(bf16)
    return high, (values - high.astype(f32)).astype(bf16)


def mm3(left_pair, right_pair, left_dim=1, right_dim=0):
    (lh, ll), (rh, rl) = left_pair, right_pair
    return (
        mm(lh, rh, left_dim, right_dim)
        + mm(lh, rl, left_dim, right_dim)
        + mm(ll, rh, left_dim, right_dim)
    )


def ones_mm(ones_side, values, terms):
    total = None
    for _ in range(terms):
        high = values.astype(bf16)
        part = mm(ones_side, high)
        total = part if total is None else total + part
        values = values - high.astype(f32)
    return total


def wide(lanes):
    return jnp.concatenate([lanes, lanes], axis=1)


def row_total(values):
    return jnp.sum(values, axis=-1, keepdims=True)


def softplus(z):
    return jnp.maximum(z, 0.0) + jnp.log1p(jnp.exp(-jnp.abs(z)))


def index_pair():
    return (
        lax.broadcasted_iota(jnp.int32, (CHUNK, CHUNK), 0),
        lax.broadcasted_iota(jnp.int32, (CHUNK, CHUNK), 1),
    )


def taps_sum(conv_ref, pad_ref, start):
    total = None
    for tap in range(4):
        term = conv_ref[tap : tap + 1, :] * pad_ref[pl.ds(start + 5 + tap, CHUNK), :]
        total = term if total is None else total + term
    return total


def gates(decay_pre, write_pre, dec_ref):
    z = decay_pre + dec_ref[1:2, :]
    return z, dec_ref[0:1, :] * softplus(z), jax.nn.sigmoid(write_pre)


def cumulative(decays, causal_ones):
    total = ones_mm(causal_ones, decays, 3)
    across = jnp.transpose(total)[0:1, :]
    return total, across


def ratios(total, across, causal):
    spread = wide(total) - across
    return jnp.where(causal, jnp.exp(jnp.where(causal, spread, 0.0)), 0.0)


def mix_forward(
    first_ref, wall_ref, conv_ref, dec_ref, hg_ref, out_ref,
    proj_ref, part_ref, mixed_ref, o_ref, t_ref, u_ref, w_ref, qe_ref, a_ref, s_ref, tail_ref,
    state, pad,
):
    @pl.when(pl.program_id(0) == 0)
    def _():
        state[...] = jnp.zeros_like(state)
        pad[0:8, :] = jnp.zeros((8, QKV), f32)

    row, col = index_pair()
    causal = row >= col
    strict = row > col
    causal_ones = causal.astype(bf16)
    parts = range(BATCH)
    rows = [pl.ds(c * CHUNK, CHUNK) for c in parts]
    for c in parts:
        pre = mm(first_ref[rows[c], :], wall_ref[...])
        proj_ref[rows[c], :] = pre
        pad[pl.ds(8 + c * CHUNK, CHUNK), :] = pre[:, :QKV]
    items = []
    for c in parts:
        tail_ref[c] = pad[pl.ds(c * CHUNK, 8), :]
        act = jax.nn.silu(taps_sum(conv_ref, pad, c * CHUNK))
        q, k, v = act[:, :DK], act[:, DK : 2 * DK], act[:, 2 * DK :]
        q = q * (lax.rsqrt(row_total(q * q) + norm_eps) * DK ** (-0.5))
        k = k * lax.rsqrt(row_total(k * k) + norm_eps)
        _, decays, rate = gates(
            proj_ref[rows[c], 768:896], proj_ref[rows[c], 896:1024], dec_ref
        )
        total, across = cumulative(decays, causal_ones)
        ratio = ratios(total, across, causal)
        kk = mm(k, k, 1, 1)
        lower = jnp.where(strict, wide(rate) * kk * ratio, 0.0)
        scores = (mm(q, k, 1, 1) * ratio).astype(bf16)
        growth = jnp.exp(total)
        last = total[CHUNK - 1 : CHUNK, :]
        tail_k = (jnp.exp(last - total) * k).astype(bf16)
        items.append((q, k, v, rate, growth, jnp.exp(last), tail_k, scores, lower))
    pad[0:8, :] = pad[pl.ds(BATCH * CHUNK, 8), :]
    size = 1
    inverse = [(row == col).astype(f32) for c in parts]
    while size < CHUNK:
        same = (row // (2 * size) == col // (2 * size)) & ((row // size) % 2 == 1) & ((col // size) % 2 == 0)
        for c in parts:
            edge = jnp.where(same, items[c][8], 0.0)
            if size == 1:
                inverse[c] = inverse[c] - edge
            else:
                pair = halves(inverse[c])
                inverse[c] = inverse[c] - mm3(halves(mm3(pair, halves(edge))), pair)
        size *= 2
    eye = lax.broadcasted_iota(jnp.int32, (DK, DK), 0) == lax.broadcasted_iota(
        jnp.int32, (DK, DK), 1
    )
    later = []
    for c in parts:
        q, k, v, rate, growth, grown, tail_k, scores, _ = items[c]
        solve = inverse[c].astype(bf16)
        t_ref[c] = solve
        w = mm(solve, rate * growth * k).astype(bf16)
        u_start = mm(solve, wide(rate) * v)
        q_eff = (growth * q - mm(scores, w)).astype(bf16)
        carry = jnp.where(eye, grown, 0.0) - mm(w, tail_k, 0, 0)
        added = mm(u_start, tail_k, 0, 0)
        w_ref[c] = w
        qe_ref[c] = q_eff
        a_ref[c] = carry
        later.append((w, u_start, q_eff, scores, carry, added))
    memory = state[...]
    starts = []
    for c in parts:
        s_ref[c] = memory
        starts.append(memory)
        memory = mm(memory, later[c][4]) + later[c][5]
    state[...] = memory
    for c in parts:
        w, u_start, q_eff, scores, _, _ = later[c]
        u_ref[c] = (u_start - mm(w, starts[c], 1, 1)).astype(bf16)
        o = mm(q_eff, starts[c], 1, 1) + mm(scores, u_start)
        o_ref[rows[c], :] = o
        normed = o * lax.rsqrt(row_total(o * o) * (1.0 / DV) + gate_eps) * hg_ref[...]
        mixed = (normed * jax.nn.silu(proj_ref[rows[c], 512:768])).astype(bf16)
        mixed_ref[rows[c], :] = mixed
        part_ref[rows[c], :] = mm(mixed, out_ref[...], 1, 1).astype(bf16)


def mix_backward(
    grad_ref, out_ref, proj_ref, tail_ref, o_ref, t_ref, u_ref, w_ref, qe_ref, a_ref, s_ref,
    wall_ref, conv_ref, dec_ref, hg_ref,
    pre_ref, first_ref, conv_grad_ref, small_ref,
    dstate, padp, padg,
):
    @pl.when(pl.program_id(0) == 0)
    def _():
        dstate[...] = jnp.zeros_like(dstate)
        padg[pl.ds(BATCH * CHUNK, 8), :] = jnp.zeros((8, QKV), f32)
        conv_grad_ref[...] = jnp.zeros_like(conv_grad_ref)
        small_ref[...] = jnp.zeros_like(small_ref)

    row, col = index_pair()
    causal = row >= col
    strict = row > col
    causal_ones = causal.astype(bf16)
    strict_ones = strict.astype(bf16)
    upper_ones = (col >= row).astype(bf16)
    lane = lax.broadcasted_iota(jnp.int32, (CHUNK, DK), 1)
    parts = range(BATCH)
    rows = [pl.ds(c * CHUNK, CHUNK) for c in parts]
    padp[0:8, :] = tail_ref[0]
    for c in parts:
        padp[pl.ds(8 + c * CHUNK, CHUNK), :] = proj_ref[rows[c], :QKV]
    items = []
    for c in parts:
        act_pre = taps_sum(conv_ref, padp, c * CHUNK)
        act_sig = jax.nn.sigmoid(act_pre)
        act = act_pre * act_sig
        slope = act_sig * (1.0 + act_pre * (1.0 - act_sig))
        qc, kc, v = act[:, :DK], act[:, DK : 2 * DK], act[:, 2 * DK :]
        q_scale = lax.rsqrt(row_total(qc * qc) + norm_eps)
        k_scale = lax.rsqrt(row_total(kc * kc) + norm_eps)
        q = qc * (q_scale * DK ** (-0.5))
        k = kc * k_scale
        z, decays, rate = gates(
            proj_ref[rows[c], 768:896], proj_ref[rows[c], 896:1024], dec_ref
        )
        total, across = cumulative(decays, causal_ones)
        ratio = ratios(total, across, causal)
        key_ratio = mm(k, k, 1, 1) * ratio
        scores = mm(q, k, 1, 1) * ratio
        growth = jnp.exp(total)
        last = total[CHUNK - 1 : CHUNK, :]
        tail = jnp.exp(last - total)
        grad = mm(grad_ref[rows[c], :], out_ref[...])
        gate = proj_ref[rows[c], 512:768]
        gate_sig = jax.nn.sigmoid(gate)
        gate_act = gate * gate_sig
        o = o_ref[rows[c], :]
        o_scale = lax.rsqrt(row_total(o * o) * (1.0 / DV) + gate_eps)
        normed = o * o_scale
        gain = hg_ref[...]
        gate_grad = grad * normed * gain * gate_sig * (1.0 + gate * (1.0 - gate_sig))
        pre_ref[rows[c], 512:768] = gate_grad.astype(bf16)
        grad = grad * gate_act
        small_ref[0:1, :] += jnp.sum(grad * normed, axis=0, keepdims=True)
        grad = grad * gain
        do = o_scale * (grad - normed * (row_total(grad * normed) * (1.0 / DV)))
        do = do.astype(bf16)
        items.append(
            (slope, q, k, v, q_scale, k_scale, z, decays, rate, ratio, key_ratio, scores,
             growth, jnp.exp(last), tail, do)
        )
    ends = [None] * BATCH
    change = dstate[...]
    for c in reversed(parts):
        ends[c] = change
        change = mm(change, a_ref[c], 1, 1) + mm(items[c][15], qe_ref[c], 0, 0)
    dstate[...] = change
    for c in reversed(parts):
        (slope, q, k, v, q_scale, k_scale, z, decays, rate, ratio, key_ratio, scores,
         growth, grown, tail, do) = items[c]
        start = s_ref[c]
        end = ends[c]
        start16 = start.astype(bf16)
        end16 = end.astype(bf16)
        u = u_ref[c]
        q16, k16 = q.astype(bf16), k.astype(bf16)
        du = mm(scores, do, 0, 0) + mm(tail * k, end16, 1, 1)
        dx = mm(t_ref[c], du, 0, 0)
        dx16 = dx.astype(bf16)
        d_scores = jnp.where(causal, mm(do, u, 1, 1), 0.0)
        d_lower = jnp.where(strict, -mm(dx16, u, 1, 1), 0.0)
        score_side = (d_scores * ratio).astype(bf16)
        rate2 = wide(rate)
        growth2 = wide(growth)
        lower_keys = d_lower * key_ratio
        key_side = (d_lower * rate2 * ratio).astype(bf16)
        do_state = mm(do, start16)
        dx_state = mm(dx16, start16)
        u_state = mm(u, end16)
        key_state = mm(k16, start16, 1, 1)
        dq = growth * do_state + mm(score_side, k16)
        rate_growth = rate * growth
        dk = (
            mm(score_side, q16, 0, 0)
            + mm(key_side, k16)
            + mm(key_side, k16, 0, 0)
            - rate_growth * dx_state
            + tail * u_state
        )
        dv = rate2 * dx
        d_rate = row_total(lower_keys) + row_total(dx * (v - growth2 * key_state))
        from_growth = row_total(growth * q * do_state - rate_growth * k * dx_state)
        from_tail = row_total(tail * k * u_state)
        pairs = d_scores * scores + rate2 * lower_keys
        held = ones_mm(upper_ones, pairs, 2)
        spread_growth = ones_mm(upper_ones, jnp.broadcast_to(from_growth, (CHUNK, DK)), 2)
        spread_tail = ones_mm(strict_ones, jnp.broadcast_to(from_tail, (CHUNK, DK)), 2)
        through = jnp.sum(row_total(end * start), axis=0, keepdims=True)
        d_decay = (
            row_total(jnp.where(strict, held, 0.0))
            + spread_growth
            + spread_tail
            + grown * through
        )
        dz = d_decay * dec_ref[0:1, :] * jax.nn.sigmoid(z)
        d_write = d_rate * rate * (1.0 - rate)
        pre_ref[rows[c], 768:896] = jnp.where(
            lane == 0, dz, jnp.where(lane == 1, d_write, 0.0)
        ).astype(bf16)
        small_ref[1:2, :DK] += jnp.sum(d_decay * decays, axis=0, keepdims=True)
        small_ref[2:3, :DK] += jnp.sum(dz, axis=0, keepdims=True)
        dqc = q_scale * (DK ** (-0.5) * dq - q * (row_total(q * dq) * DK**0.5))
        dkc = k_scale * (dk - k * row_total(k * dk))
        dact = jnp.concatenate([dqc, dkc, dv], axis=1) * slope
        padg[pl.ds(c * CHUNK, CHUNK), :] = dact
        dpre = None
        for tap in range(4):
            weight = conv_ref[tap : tap + 1, :]
            term = weight * padg[pl.ds(c * CHUNK + 3 - tap, CHUNK), :]
            dpre = term if dpre is None else dpre + term
            conv_grad_ref[tap : tap + 1, :] += jnp.sum(
                dact * padp[pl.ds(c * CHUNK + 5 + tap, CHUNK), :], axis=0, keepdims=True
            )
        pre_ref[rows[c], :QKV] = dpre.astype(bf16)
        first_ref[rows[c], :] = mm(pre_ref[rows[c], :], wall_ref[...], 1, 1).astype(bf16)
    padg[pl.ds(BATCH * CHUNK, 8), :] = padg[0:8, :]


def call_forward(first_rows, wall, conv, dec, hg, out_t):
    rows = first_rows.shape[0]
    chunks = rows // CHUNK
    steps = chunks // BATCH
    tall = lambda width: pl.BlockSpec((BATCH * CHUNK, width), lambda i: (i, 0))
    fixed = lambda shape: pl.BlockSpec(shape, lambda i: (0, 0))
    per = lambda *shape: pl.BlockSpec((BATCH,) + shape, lambda i: (i, 0, 0))
    made = jax.ShapeDtypeStruct
    return pl.pallas_call(
        mix_forward,
        grid=(steps,),
        in_specs=[
            tall(D), fixed((D, 1024)), fixed((8, QKV)), fixed((8, DK)), fixed((1, DV)),
            fixed((D, DV)),
        ],
        out_specs=[
            tall(1024), tall(D), tall(DV), tall(DV), per(CHUNK, CHUNK), per(CHUNK, DV),
            per(CHUNK, DK), per(CHUNK, DK), per(DK, DK), per(DV, DK), per(8, QKV),
        ],
        out_shape=[
            made((rows, 1024), f32), made((rows, D), bf16), made((rows, DV), bf16),
            made((rows, DV), f32), made((chunks, CHUNK, CHUNK), bf16),
            made((chunks, CHUNK, DV), bf16), made((chunks, CHUNK, DK), bf16),
            made((chunks, CHUNK, DK), bf16), made((chunks, DK, DK), f32),
            made((chunks, DV, DK), f32), made((chunks, 8, QKV), f32),
        ],
        scratch_shapes=[
            pltpu.VMEM((DV, DK), f32), pltpu.VMEM((BATCH * CHUNK + 8, QKV), f32),
        ],
        compiler_params=pltpu.CompilerParams(
            dimension_semantics=("arbitrary",), vmem_limit_bytes=56 * 1024 * 1024
        ),
        cost_estimate=pl.CostEstimate(
            flops=30_000_000_000, bytes_accessed=20_000_000, transcendentals=4_000_000
        ),
        name="mix_forward",
    )(first_rows, wall, conv, dec, hg, out_t)


def call_backward(grad_rows, out_t, saved, wall, conv, dec, hg):
    proj, o, t, u, w, qe, a, s, tails = saved
    rows = grad_rows.shape[0]
    chunks = rows // CHUNK
    steps = chunks // BATCH
    tall = lambda width: pl.BlockSpec((BATCH * CHUNK, width), lambda i: (steps - 1 - i, 0))
    fixed = lambda shape: pl.BlockSpec(shape, lambda i: (0, 0))
    per = lambda *shape: pl.BlockSpec((BATCH,) + shape, lambda i: (steps - 1 - i, 0, 0))
    made = jax.ShapeDtypeStruct
    return pl.pallas_call(
        mix_backward,
        grid=(steps,),
        in_specs=[
            tall(D), fixed((D, DV)), tall(1024), per(8, QKV), tall(DV), per(CHUNK, CHUNK),
            per(CHUNK, DV), per(CHUNK, DK), per(CHUNK, DK), per(DK, DK), per(DV, DK),
            fixed((D, 896)), fixed((8, QKV)), fixed((8, DK)), fixed((1, DV)),
        ],
        out_specs=[tall(896), tall(D), fixed((8, QKV)), fixed((8, DV))],
        out_shape=[
            made((rows, 896), bf16), made((rows, D), bf16), made((8, QKV), f32),
            made((8, DV), f32),
        ],
        scratch_shapes=[
            pltpu.VMEM((DV, DK), f32), pltpu.VMEM((BATCH * CHUNK + 8, QKV), f32),
            pltpu.VMEM((BATCH * CHUNK + 8, QKV), f32),
        ],
        compiler_params=pltpu.CompilerParams(
            dimension_semantics=("arbitrary",), vmem_limit_bytes=56 * 1024 * 1024
        ),
        cost_estimate=pl.CostEstimate(
            flops=60_000_000_000, bytes_accessed=20_000_000, transcendentals=4_000_000
        ),
        name="mix_backward",
    )(grad_rows, out_t, proj, tails, o, t, u, w, qe, a, s, wall, conv, dec, hg)


def matmul(left_side, right_side):
    return jnp.dot(left_side, right_side, preferred_element_type=f32)


def contract_rows(left_side, right_side):
    return lax.dot_general(
        left_side, right_side, (((0,), (0,)), ((), ())), preferred_element_type=f32
    )


def times_transposed(left_side, right_side):
    return lax.dot_general(
        left_side, right_side, (((1,), (1,)), ((), ())), preferred_element_type=f32
    )


def rms_scale(values, scale_gain):
    return (
        values
        * lax.rsqrt(jnp.mean(values * values, axis=-1, keepdims=True) + norm_eps)
        * scale_gain
    )


def group_rows(values):
    return lax.all_gather(values, "tensor", axis=0, tiled=True)


def row_sums(values):
    return lax.psum_scatter(
        values.astype(bf16), "tensor", scatter_dimension=0, tiled=True
    ).astype(f32)


def shards(
    block_input, out_cotangent, lengths, mixer_gain, query_weight, key_weight, value_weight,
    output_gate_weight, decay_weight, query_conv, key_conv, value_conv, decay_log, decay_bias,
    head_gain, out_weight, ffn_gain, ffn_gate, ffn_up, ffn_down,
):
    inputs = block_input.astype(f32)
    cotangent = out_cotangent.astype(f32)
    local_rows = inputs.shape[0]
    tensor_index = lax.axis_index("tensor")
    tensor_size = lax.axis_size("tensor")
    position = tensor_index * local_rows + jnp.arange(local_rows, dtype=jnp.int32)
    live_rows = (position < lengths[0]).astype(f32)[:, None]
    held = local_depth = query_weight.shape[0]
    decay_flat = decay_weight.reshape(local_depth, 2)
    mixer_pack = jnp.concatenate(
        [query_weight, key_weight, value_weight, output_gate_weight,
         jnp.pad(decay_flat, ((0, 0), (0, 126))), out_weight.T],
        axis=1,
    )
    ffn_pack = jnp.concatenate([ffn_gate, ffn_up, ffn_down.T], axis=1)
    normed_one, first_back = jax.vjp(rms_scale, inputs, mixer_gain)
    first_rows = group_rows(normed_one.astype(bf16))
    mixer_full = lax.all_gather(mixer_pack, "dp", axis=0, tiled=True)
    ffn_full = lax.all_gather(ffn_pack, "dp", axis=0, tiled=True)
    wall_back = mixer_full[:, :896]
    out_t = mixer_full[:, 896:]
    wall = jnp.concatenate(
        [mixer_full[:, :768],
         jnp.broadcast_to(mixer_full[:, 768:769], (D, DK)),
         jnp.broadcast_to(mixer_full[:, 769:770], (D, DK))],
        axis=1,
    )
    ff = ffn_gate.shape[1]
    ffn_in = ffn_full[:, : 2 * ff]
    down_t = ffn_full[:, 2 * ff :]
    conv = jnp.pad(
        jnp.concatenate([query_conv, key_conv, value_conv], axis=1), ((0, 4), (0, 0))
    )
    dec = jnp.pad(
        jnp.broadcast_to(jnp.stack([-jnp.exp(decay_log[0]), decay_bias[0]])[:, None], (2, DK)),
        ((0, 6), (0, 0)),
    )
    hg = head_gain[None, :]
    proj, mixed_part, mixed_rows, o, t, u, w, qe, a, s, tails = call_forward(
        first_rows, wall, conv, dec, hg, out_t
    )
    mixed = row_sums(mixed_part)
    middle = inputs + live_rows * mixed
    normed_two, second_back = jax.vjp(rms_scale, middle, ffn_gain)
    fed_grad = group_rows((live_rows * cotangent).astype(bf16))
    second_rows = group_rows(normed_two.astype(bf16))
    acts = matmul(second_rows, ffn_in)
    gate_act, up_act = acts[:, :ff], acts[:, ff:]
    sigmoid_gate = jax.nn.sigmoid(gate_act)
    hidden = (gate_act * sigmoid_gate * up_act).astype(bf16)
    hidden_grad = matmul(fed_grad, down_t)
    gate_grad = hidden_grad * up_act * sigmoid_gate * (1.0 + gate_act * (1.0 - sigmoid_gate))
    up_grad = hidden_grad * gate_act * sigmoid_gate
    act_grads = jnp.concatenate([gate_grad.astype(bf16), up_grad.astype(bf16)], axis=1)
    second_in = row_sums(times_transposed(act_grads, ffn_in))
    ffn_terms = row_sums(times_transposed(hidden, down_t))
    block_output = (middle + live_rows * ffn_terms).astype(bf16)
    acts_wgrad = contract_rows(second_rows, act_grads)
    down_wgrad = contract_rows(fed_grad, hidden)
    middle_part, ffn_gain_grad = second_back(second_in)
    middle_grad = cotangent + middle_part
    mixed_grad = group_rows((live_rows * middle_grad).astype(bf16))
    out_wgrad = contract_rows(mixed_grad, mixed_rows)
    early = jnp.concatenate(
        [acts_wgrad.astype(bf16), down_wgrad.astype(bf16), out_wgrad.astype(bf16)], axis=1
    )
    early_sum = lax.psum_scatter(early, "dp", scatter_dimension=0, tiled=True).astype(f32)
    pre_grads, first_part, conv_grads, small = call_backward(
        mixed_grad, out_t, (proj, o, t, u, w, qe, a, s, tails), wall_back, conv, dec, hg
    )
    first_sum = row_sums(first_part)
    late = contract_rows(first_rows, pre_grads).astype(bf16)
    late_sum = lax.psum_scatter(late, "dp", scatter_dimension=0, tiled=True).astype(f32)
    input_part, mixer_gain_grad = first_back(first_sum)
    input_grad = middle_grad + input_part
    own = jnp.concatenate(
        [conv_grads[:4].reshape(-1), small[1, :DK], small[2, :DK]]
    )
    slots = jnp.zeros((tensor_size, own.shape[0]), f32)
    slots = lax.dynamic_update_slice(slots, own[None, :], (tensor_index, 0))
    everything = lax.psum(
        jnp.concatenate([slots.reshape(-1), mixer_gain_grad, ffn_gain_grad, small[0]]),
        ("dp", "tensor"),
    )
    own_sum = lax.dynamic_slice(
        everything[: slots.size].reshape(slots.shape), (tensor_index, 0), (1, own.shape[0])
    )[0]
    gains = everything[slots.size :]
    conv_sum = own_sum[: 4 * QKV].reshape(4, QKV)
    return (
        block_output,
        input_grad,
        gains[:D],
        late_sum[:, :128],
        late_sum[:, 128:256],
        late_sum[:, 256:512],
        late_sum[:, 512:768],
        late_sum[:, 768:770].reshape(held, 1, 2),
        conv_sum[:, :DK],
        conv_sum[:, DK : 2 * DK],
        conv_sum[:, 2 * DK :],
        own_sum[4 * QKV : 4 * QKV + 1],
        own_sum[4 * QKV + DK : 4 * QKV + DK + 1],
        gains[2 * D :],
        early_sum[:, 3 * ff :].T,
        gains[D : 2 * D],
        early_sum[:, :ff],
        early_sum[:, ff : 2 * ff],
        early_sum[:, 2 * ff : 3 * ff].T,
    )


def solution(mesh):
    rows = P(("dp", "tensor"), None)
    tile = P("dp", "tensor")
    taps = P(None, "tensor")
    turned = P("tensor", "dp")
    decay = P("dp", "tensor", None)
    head = P("tensor")
    return jax.shard_map(
        shards,
        mesh=mesh,
        in_specs=(
            rows, rows, P("dp"), P(), tile, tile, tile, tile, decay, taps, taps, taps, head, head,
            P(), turned, P(), tile, tile, turned,
        ),
        out_specs=(
            rows, rows, P(), tile, tile, tile, tile, decay, taps, taps, taps, head, head,
            P(), turned, P(), tile, tile, turned,
        ),
        check_vma=False,
    )
```

```python
import functools

import jax
import jax.numpy as jnp
from jax import lax
from jax.experimental import pallas as pl
from jax.experimental.pallas import tpu as pltpu
from jax.sharding import PartitionSpec as P

DK = 128
DV = 256
QKV = 2 * DK + DV
D = 1024
GATE_END = 768
PRE = 896
MIX = 1152
TENSOR = 8
DATA = 16
CHUNK = 256
BATCH = 2

norm_eps = 1e-06
gate_eps = 1e-05
bf16 = jnp.bfloat16
f32 = jnp.float32


def mm(left_side, right_side, left_dim=1, right_dim=0):
    return lax.dot_general(
        left_side.astype(bf16),
        right_side.astype(bf16),
        (((left_dim,), (right_dim,)), ((), ())),
        preferred_element_type=f32,
    )


def halves(values):
    high = values.astype(bf16)
    return high, (values - high.astype(f32)).astype(bf16)


def mm3(left_pair, right_pair, left_dim=1, right_dim=0):
    (lh, ll), (rh, rl) = left_pair, right_pair
    return (
        mm(lh, rh, left_dim, right_dim)
        + mm(lh, rl, left_dim, right_dim)
        + mm(ll, rh, left_dim, right_dim)
    )


def ones_mm(ones_side, values, terms):
    total = None
    for _ in range(terms):
        high = values.astype(bf16)
        part = mm(ones_side, high)
        total = part if total is None else total + part
        values = values - high.astype(f32)
    return total


def wide(lanes):
    return jnp.concatenate([lanes, lanes], axis=1)


def row_total(values):
    return jnp.sum(values, axis=-1, keepdims=True)


def softplus(z):
    return jnp.maximum(z, 0.0) + jnp.log1p(jnp.exp(-jnp.abs(z)))


def index_pair():
    return (
        lax.broadcasted_iota(jnp.int32, (CHUNK, CHUNK), 0),
        lax.broadcasted_iota(jnp.int32, (CHUNK, CHUNK), 1),
    )


def taps_sum(conv_ref, pad_ref, start):
    total = None
    for tap in range(4):
        term = conv_ref[tap : tap + 1, :] * pad_ref[pl.ds(start + 5 + tap, CHUNK), :]
        total = term if total is None else total + term
    return total


def gates(proj_ref, rows, dec_ref):
    both = proj_ref[rows, GATE_END:PRE]
    z = jnp.broadcast_to(both[:, 0:1], (CHUNK, DK)) + dec_ref[1:2, :]
    rate = jax.nn.sigmoid(jnp.broadcast_to(both[:, 1:2], (CHUNK, DK)))
    return z, dec_ref[0:1, :] * softplus(z), rate


def cumulative(decays, causal_ones):
    total = ones_mm(causal_ones, decays, 3)
    across = jnp.transpose(total)[0:1, :]
    return total, across


def ratios(total, across, causal):
    spread = wide(total) - across
    return jnp.where(causal, jnp.exp(jnp.where(causal, spread, 0.0)), 0.0)


def mix_forward(
    first_ref, pack_ref, conv_ref, dec_ref, hg_ref,
    proj_ref, part_ref, mixed_ref, o_ref, t_ref, u_ref, w_ref, qe_ref, a_ref, s_ref, tail_ref,
    state, pad,
):
    @pl.when(pl.program_id(0) == 0)
    def _():
        state[...] = jnp.zeros_like(state)
        pad[0:8, :] = jnp.zeros((8, QKV), f32)

    row, col = index_pair()
    causal = row >= col
    strict = row > col
    causal_ones = causal.astype(bf16)
    parts = range(BATCH)
    rows = [pl.ds(c * CHUNK, CHUNK) for c in parts]
    for c in parts:
        pre = mm(first_ref[rows[c], :], pack_ref[:, :PRE])
        proj_ref[rows[c], :] = pre
        pad[pl.ds(8 + c * CHUNK, CHUNK), :] = pre[:, :QKV]
    items = []
    for c in parts:
        tail_ref[c] = pad[pl.ds(c * CHUNK, 8), :]
        act = jax.nn.silu(taps_sum(conv_ref, pad, c * CHUNK))
        q, k, v = act[:, :DK], act[:, DK : 2 * DK], act[:, 2 * DK :]
        q = q * (lax.rsqrt(row_total(q * q) + norm_eps) * DK ** (-0.5))
        k = k * lax.rsqrt(row_total(k * k) + norm_eps)
        _, decays, rate = gates(proj_ref, rows[c], dec_ref)
        total, across = cumulative(decays, causal_ones)
        ratio = ratios(total, across, causal)
        kk = mm(k, k, 1, 1)
        lower = jnp.where(strict, wide(rate) * kk * ratio, 0.0)
        scores = (mm(q, k, 1, 1) * ratio).astype(bf16)
        growth = jnp.exp(total)
        last = total[CHUNK - 1 : CHUNK, :]
        tail_k = (jnp.exp(last - total) * k).astype(bf16)
        items.append((q, k, v, rate, growth, jnp.exp(last), tail_k, scores, lower))
    pad[0:8, :] = pad[pl.ds(BATCH * CHUNK, 8), :]
    size = 1
    inverse = [(row == col).astype(f32) for c in parts]
    while size < CHUNK:
        same = (row // (2 * size) == col // (2 * size)) & ((row // size) % 2 == 1) & ((col // size) % 2 == 0)
        for c in parts:
            edge = jnp.where(same, items[c][8], 0.0)
            if size == 1:
                inverse[c] = inverse[c] - edge
            else:
                pair = halves(inverse[c])
                inverse[c] = inverse[c] - mm3(halves(mm3(pair, halves(edge))), pair)
        size *= 2
    eye = lax.broadcasted_iota(jnp.int32, (DK, DK), 0) == lax.broadcasted_iota(
        jnp.int32, (DK, DK), 1
    )
    later = []
    for c in parts:
        q, k, v, rate, growth, grown, tail_k, scores, _ = items[c]
        solve = inverse[c].astype(bf16)
        t_ref[c] = solve
        w = mm(solve, rate * growth * k).astype(bf16)
        u_start = mm(solve, wide(rate) * v)
        q_eff = (growth * q - mm(scores, w)).astype(bf16)
        carry = jnp.where(eye, grown, 0.0) - mm(w, tail_k, 0, 0)
        added = mm(u_start, tail_k, 0, 0)
        w_ref[c] = w
        qe_ref[c] = q_eff
        a_ref[c] = carry
        later.append((w, u_start, q_eff, scores, carry, added))
    memory = state[...]
    starts = []
    for c in parts:
        s_ref[c] = memory
        starts.append(memory)
        memory = mm(memory, later[c][4]) + later[c][5]
    state[...] = memory
    for c in parts:
        w, u_start, q_eff, scores, _, _ = later[c]
        u_ref[c] = (u_start - mm(w, starts[c], 1, 1)).astype(bf16)
        o = mm(q_eff, starts[c], 1, 1) + mm(scores, u_start)
        o_ref[rows[c], :] = o
        normed = o * lax.rsqrt(row_total(o * o) * (1.0 / DV) + gate_eps) * hg_ref[...]
        mixed = (normed * jax.nn.silu(proj_ref[rows[c], QKV:GATE_END])).astype(bf16)
        mixed_ref[rows[c], :] = mixed
        part_ref[rows[c], :] = mm(mixed, pack_ref[:, PRE:MIX], 1, 1).astype(bf16)


def mix_backward(
    grad_ref, pack_ref, proj_ref, tail_ref, o_ref, t_ref, u_ref, w_ref, qe_ref, a_ref, s_ref,
    conv_ref, dec_ref, hg_ref,
    pre_ref, first_ref, conv_grad_ref, small_ref,
    dstate, padp, padg,
):
    @pl.when(pl.program_id(0) == 0)
    def _():
        dstate[...] = jnp.zeros_like(dstate)
        padg[pl.ds(BATCH * CHUNK, 8), :] = jnp.zeros((8, QKV), f32)
        conv_grad_ref[...] = jnp.zeros_like(conv_grad_ref)
        small_ref[...] = jnp.zeros_like(small_ref)

    row, col = index_pair()
    causal = row >= col
    strict = row > col
    causal_ones = causal.astype(bf16)
    strict_ones = strict.astype(bf16)
    upper_ones = (col >= row).astype(bf16)
    lane = lax.broadcasted_iota(jnp.int32, (CHUNK, DK), 1)
    parts = range(BATCH)
    rows = [pl.ds(c * CHUNK, CHUNK) for c in parts]
    padp[0:8, :] = tail_ref[0]
    for c in parts:
        padp[pl.ds(8 + c * CHUNK, CHUNK), :] = proj_ref[rows[c], :QKV]
    items = []
    for c in parts:
        act_pre = taps_sum(conv_ref, padp, c * CHUNK)
        act_sig = jax.nn.sigmoid(act_pre)
        act = act_pre * act_sig
        slope = act_sig * (1.0 + act_pre * (1.0 - act_sig))
        qc, kc, v = act[:, :DK], act[:, DK : 2 * DK], act[:, 2 * DK :]
        q_scale = lax.rsqrt(row_total(qc * qc) + norm_eps)
        k_scale = lax.rsqrt(row_total(kc * kc) + norm_eps)
        q = qc * (q_scale * DK ** (-0.5))
        k = kc * k_scale
        z, decays, rate = gates(proj_ref, rows[c], dec_ref)
        total, across = cumulative(decays, causal_ones)
        ratio = ratios(total, across, causal)
        key_ratio = mm(k, k, 1, 1) * ratio
        scores = mm(q, k, 1, 1) * ratio
        growth = jnp.exp(total)
        last = total[CHUNK - 1 : CHUNK, :]
        tail = jnp.exp(last - total)
        grad = mm(grad_ref[rows[c], :], pack_ref[:, PRE:MIX])
        gate = proj_ref[rows[c], QKV:GATE_END]
        gate_sig = jax.nn.sigmoid(gate)
        gate_act = gate * gate_sig
        o = o_ref[rows[c], :]
        o_scale = lax.rsqrt(row_total(o * o) * (1.0 / DV) + gate_eps)
        normed = o * o_scale
        gain = hg_ref[...]
        gate_grad = grad * normed * gain * gate_sig * (1.0 + gate * (1.0 - gate_sig))
        pre_ref[rows[c], QKV:GATE_END] = gate_grad.astype(bf16)
        grad = grad * gate_act
        small_ref[0:1, :] += jnp.sum(grad * normed, axis=0, keepdims=True)
        grad = grad * gain
        do = o_scale * (grad - normed * (row_total(grad * normed) * (1.0 / DV)))
        do = do.astype(bf16)
        items.append(
            (slope, q, k, v, q_scale, k_scale, z, decays, rate, ratio, key_ratio, scores,
             growth, jnp.exp(last), tail, do)
        )
    ends = [None] * BATCH
    change = dstate[...]
    for c in reversed(parts):
        ends[c] = change
        change = mm(change, a_ref[c], 1, 1) + mm(items[c][15], qe_ref[c], 0, 0)
    dstate[...] = change
    for c in reversed(parts):
        (slope, q, k, v, q_scale, k_scale, z, decays, rate, ratio, key_ratio, scores,
         growth, grown, tail, do) = items[c]
        start = s_ref[c]
        end = ends[c]
        start16 = start.astype(bf16)
        end16 = end.astype(bf16)
        u = u_ref[c]
        q16, k16 = q.astype(bf16), k.astype(bf16)
        du = mm(scores, do, 0, 0) + mm(tail * k, end16, 1, 1)
        dx = mm(t_ref[c], du, 0, 0)
        dx16 = dx.astype(bf16)
        d_scores = jnp.where(causal, mm(do, u, 1, 1), 0.0)
        d_lower = jnp.where(strict, -mm(dx16, u, 1, 1), 0.0)
        score_side = (d_scores * ratio).astype(bf16)
        rate2 = wide(rate)
        growth2 = wide(growth)
        lower_keys = d_lower * key_ratio
        key_side = (d_lower * rate2 * ratio).astype(bf16)
        do_state = mm(do, start16)
        dx_state = mm(dx16, start16)
        u_state = mm(u, end16)
        key_state = mm(k16, start16, 1, 1)
        dq = growth * do_state + mm(score_side, k16)
        rate_growth = rate * growth
        dk = (
            mm(score_side, q16, 0, 0)
            + mm(key_side, k16)
            + mm(key_side, k16, 0, 0)
            - rate_growth * dx_state
            + tail * u_state
        )
        dv = rate2 * dx
        d_rate = row_total(lower_keys) + row_total(dx * (v - growth2 * key_state))
        from_growth = row_total(growth * q * do_state - rate_growth * k * dx_state)
        from_tail = row_total(tail * k * u_state)
        pairs = d_scores * scores + rate2 * lower_keys
        held = ones_mm(upper_ones, pairs, 2)
        spread_growth = ones_mm(upper_ones, jnp.broadcast_to(from_growth, (CHUNK, DK)), 2)
        spread_tail = ones_mm(strict_ones, jnp.broadcast_to(from_tail, (CHUNK, DK)), 2)
        through = jnp.sum(row_total(end * start), axis=0, keepdims=True)
        d_decay = (
            row_total(jnp.where(strict, held, 0.0))
            + spread_growth
            + spread_tail
            + grown * through
        )
        dz = d_decay * dec_ref[0:1, :] * jax.nn.sigmoid(z)
        d_write = d_rate * rate * (1.0 - rate)
        pre_ref[rows[c], GATE_END:PRE] = jnp.where(
            lane == 0, dz, jnp.where(lane == 1, d_write, 0.0)
        ).astype(bf16)
        small_ref[1:2, :DK] += jnp.sum(d_decay * decays, axis=0, keepdims=True)
        small_ref[2:3, :DK] += jnp.sum(dz, axis=0, keepdims=True)
        dqc = q_scale * (DK ** (-0.5) * dq - q * (row_total(q * dq) * DK**0.5))
        dkc = k_scale * (dk - k * row_total(k * dk))
        dact = jnp.concatenate([dqc, dkc, dv], axis=1) * slope
        padg[pl.ds(c * CHUNK, CHUNK), :] = dact
        dpre = None
        for tap in range(4):
            weight = conv_ref[tap : tap + 1, :]
            term = weight * padg[pl.ds(c * CHUNK + 3 - tap, CHUNK), :]
            dpre = term if dpre is None else dpre + term
            conv_grad_ref[tap : tap + 1, :] += jnp.sum(
                dact * padp[pl.ds(c * CHUNK + 5 + tap, CHUNK), :], axis=0, keepdims=True
            )
        pre_ref[rows[c], :QKV] = dpre.astype(bf16)
        first_ref[rows[c], :] = mm(pre_ref[rows[c], :], pack_ref[:, :PRE], 1, 1).astype(bf16)
    padg[pl.ds(BATCH * CHUNK, 8), :] = padg[0:8, :]


def call_forward(first_rows, pack, conv, dec, hg):
    rows = first_rows.shape[0]
    chunks = rows // CHUNK
    steps = chunks // BATCH
    tall = lambda width: pl.BlockSpec((BATCH * CHUNK, width), lambda i: (i, 0))
    fixed = lambda shape: pl.BlockSpec(shape, lambda i: (0, 0))
    per = lambda *shape: pl.BlockSpec((BATCH,) + shape, lambda i: (i, 0, 0))
    made = jax.ShapeDtypeStruct
    return pl.pallas_call(
        mix_forward,
        grid=(steps,),
        in_specs=[
            tall(D), fixed((D, MIX)), fixed((8, QKV)), fixed((8, DK)), fixed((1, DV)),
        ],
        out_specs=[
            tall(PRE), tall(D), tall(DV), tall(DV), per(CHUNK, CHUNK), per(CHUNK, DV),
            per(CHUNK, DK), per(CHUNK, DK), per(DK, DK), per(DV, DK), per(8, QKV),
        ],
        out_shape=[
            made((rows, PRE), f32), made((rows, D), bf16), made((rows, DV), bf16),
            made((rows, DV), f32), made((chunks, CHUNK, CHUNK), bf16),
            made((chunks, CHUNK, DV), bf16), made((chunks, CHUNK, DK), bf16),
            made((chunks, CHUNK, DK), bf16), made((chunks, DK, DK), f32),
            made((chunks, DV, DK), f32), made((chunks, 8, QKV), f32),
        ],
        scratch_shapes=[
            pltpu.VMEM((DV, DK), f32), pltpu.VMEM((BATCH * CHUNK + 8, QKV), f32),
        ],
        compiler_params=pltpu.CompilerParams(
            dimension_semantics=("arbitrary",), vmem_limit_bytes=56 * 1024 * 1024
        ),
        cost_estimate=pl.CostEstimate(
            flops=30_000_000_000, bytes_accessed=20_000_000, transcendentals=4_000_000
        ),
        name="mix_forward",
    )(first_rows, pack, conv, dec, hg)


def call_backward(grad_rows, pack, saved, conv, dec, hg):
    proj, o, t, u, w, qe, a, s, tails = saved
    rows = grad_rows.shape[0]
    chunks = rows // CHUNK
    steps = chunks // BATCH
    tall = lambda width: pl.BlockSpec((BATCH * CHUNK, width), lambda i: (steps - 1 - i, 0))
    fixed = lambda shape: pl.BlockSpec(shape, lambda i: (0, 0))
    per = lambda *shape: pl.BlockSpec((BATCH,) + shape, lambda i: (steps - 1 - i, 0, 0))
    made = jax.ShapeDtypeStruct
    return pl.pallas_call(
        mix_backward,
        grid=(steps,),
        in_specs=[
            tall(D), fixed((D, MIX)), tall(PRE), per(8, QKV), tall(DV), per(CHUNK, CHUNK),
            per(CHUNK, DV), per(CHUNK, DK), per(CHUNK, DK), per(DK, DK), per(DV, DK),
            fixed((8, QKV)), fixed((8, DK)), fixed((1, DV)),
        ],
        out_specs=[tall(PRE), tall(D), fixed((8, QKV)), fixed((8, DV))],
        out_shape=[
            made((rows, PRE), bf16), made((rows, D), bf16), made((8, QKV), f32),
            made((8, DV), f32),
        ],
        scratch_shapes=[
            pltpu.VMEM((DV, DK), f32), pltpu.VMEM((BATCH * CHUNK + 8, QKV), f32),
            pltpu.VMEM((BATCH * CHUNK + 8, QKV), f32),
        ],
        compiler_params=pltpu.CompilerParams(
            dimension_semantics=("arbitrary",), vmem_limit_bytes=56 * 1024 * 1024
        ),
        cost_estimate=pl.CostEstimate(
            flops=60_000_000_000, bytes_accessed=20_000_000, transcendentals=4_000_000
        ),
        name="mix_backward",
    )(grad_rows, pack, proj, tails, o, t, u, w, qe, a, s, conv, dec, hg)


class Wires:
    def __init__(self, send, recv):
        self.send, self.recv, self.sent = send, recv, []

    def put(self, source, target, device):
        k = len(self.sent)
        copy = pltpu.make_async_remote_copy(
            src_ref=source,
            dst_ref=target,
            send_sem=self.send.at[k],
            recv_sem=self.recv.at[k],
            device_id=device,
            device_id_type=pl.DeviceIdType.MESH,
        )
        copy.start()
        self.sent.append(copy)
        return copy

    def flush(self):
        for copy in self.sent:
            copy.wait_send()


def on_tensor(index):
    return {"tensor": index}


def on_data(index):
    return {"dp": index}


def tensor_places():
    me = lax.axis_index("tensor")
    x, y = me % 4, me // 4
    at = lambda side, step: side * 4 + (x + step) % 4
    return {
        "me": at(y, 0), "right": at(y, 1), "far": at(y, 2), "left": at(y, 3),
        "mate": at(1 - y, 0), "mate_right": at(1 - y, 1), "mate_far": at(1 - y, 2),
        "mate_left": at(1 - y, 3),
    }


def data_places():
    me = lax.axis_index("dp")
    core, z, y = me % 2, (me // 2) % 4, me // 8
    at = lambda side, step, unit: (side * 4 + (z + step) % 4) * 2 + unit
    here = {
        "me": at(y, 0, core), "up": at(y, 1, core), "far": at(y, 2, core),
        "down": at(y, 3, core), "over": at(1 - y, 0, core), "over_up": at(1 - y, 1, core),
        "over_far": at(1 - y, 2, core), "over_down": at(1 - y, 3, core),
    }
    core_mate = {name: at(1 - y if "over" in name else y, step, 1 - core)
                 for name, step in (("me", 0), ("up", 1), ("far", 2), ("down", 3), ("over", 0),
                                    ("over_up", 1), ("over_far", 2), ("over_down", 3))}
    return here, core_mate


def greet(devices):
    barrier = pltpu.get_barrier_semaphore()
    for device in devices:
        pl.semaphore_signal(
            barrier, inc=1, device_id=device, device_id_type=pl.DeviceIdType.MESH
        )
    pl.semaphore_wait(barrier, len(devices))


def together(*steps):
    running = list(steps)
    while running:
        for item in list(running):
            try:
                next(item)
            except StopIteration:
                running.remove(item)


def block(ref, index, size, start=0, length=None):
    return ref.at[pl.ds(pl.multiple_of(index * size + start, 16), length or size)]


def gather_tensor(wires, place, own, out):
    size = own.shape[0]
    half = size // 2
    at = lambda who, part: block(out, place[who], size, part * half, half)
    send = lambda who, part, to: wires.put(at(who, part), at(who, part), on_tensor(place[to]))
    first = {}
    for part in (0, 1):
        for to in ("mate", "right", "left"):
            first[to, part] = wires.put(
                own.at[pl.ds(part * half, half)], at("me", part), on_tensor(place[to])
            )
    yield
    first["left", 0].wait_recv()
    far_low = send("right", 0, "left")
    yield
    first["mate", 0].wait_recv()
    second = [send("mate", 0, "right"), send("mate", 0, "left")]
    yield
    first["right", 0].wait_recv()
    first["right", 1].wait_recv()
    far_high = send("left", 1, "right")
    yield
    far_low.wait_recv()
    second.append(send("far", 0, "mate"))
    yield
    first["left", 1].wait_recv()
    first["mate", 1].wait_recv()
    second += [send("mate", 1, "right"), send("mate", 1, "left")]
    yield
    far_high.wait_recv()
    second.append(send("far", 1, "mate"))
    yield
    for copy in second:
        copy.wait_recv()


GATHER_TENSOR = 14


def gather_data(wires, place, core_mate, own, out):
    size = own.shape[0]
    half = size // 2
    at = lambda who: block(out, place[who], size)
    part = lambda who, i: block(out, place[who], size, i * half, half)
    send = lambda ref, to: wires.put(ref, ref, on_data(place[to]))
    share = lambda ref: wires.put(ref, ref, on_data(core_mate["me"]))
    first = {to: wires.put(own, at("me"), on_data(place[to])) for to in ("over", "up", "down")}
    shared = [wires.put(own, at("me"), on_data(core_mate["me"]))]
    yield
    first["up"].wait_recv()
    far_high = send(part("down", 1), "up")
    shared.append(share(at("down")))
    yield
    first["down"].wait_recv()
    far_low = send(part("up", 0), "down")
    shared.append(share(at("up")))
    yield
    first["over"].wait_recv()
    second = {to: send(at("over"), to) for to in ("up", "down")}
    shared.append(share(at("over")))
    yield
    far_high.wait_recv()
    shared.append(share(part("far", 1)))
    far_low.wait_recv()
    shared.append(share(part("far", 0)))
    yield
    second["up"].wait_recv()
    far_high = send(part("over_down", 1), "up")
    shared.append(share(at("over_down")))
    yield
    second["down"].wait_recv()
    far_low = send(part("over_up", 0), "down")
    shared.append(share(at("over_up")))
    yield
    far_high.wait_recv()
    shared.append(share(part("over_far", 1)))
    far_low.wait_recv()
    shared.append(share(part("over_far", 0)))
    yield
    for copy in shared:
        copy.wait_recv()


GATHER_DATA = 19


def scatter_tensor(wires, place, part_ref, slots, done):
    size = part_ref.shape[0] // TENSOR
    half = size // 2
    rows = lambda who, start=0, length=None: block(part_ref, place[who], size, start, length)
    load = lambda ref: ref[...].astype(f32)
    slot = lambda i: slots.at[i]
    piece = lambda i, p: slots.at[i, pl.ds(p * half, half)]
    put = lambda source, target, to: wires.put(source, target, on_tensor(place[to]))
    far = put(rows("mate_far"), slot(0), "mate")
    to_right = put(rows("mate_right"), slot(1), "right")
    to_left = put(rows("mate_left"), slot(2), "left")
    yield
    far.wait_recv()
    slot(3)[...] = (load(slot(0)) + load(rows("far"))).astype(bf16)
    pass_right = put(piece(3, 1), piece(4, 1), "right")
    pass_left = put(piece(3, 0), piece(4, 0), "left")
    near = [
        put(rows("right", 0, half), piece(5, 0), "right"),
        put(rows("left", half, half), piece(6, 1), "left"),
    ]
    yield
    to_right.wait_recv()
    to_left.wait_recv()
    slot(7)[...] = (load(slot(1)) + load(slot(2)) + load(rows("mate"))).astype(bf16)
    mate = put(slot(7), slot(8), "mate")
    yield
    pass_right.wait_recv()
    piece(9, 1)[...] = (load(piece(4, 1)) + load(rows("right", half, half))).astype(bf16)
    near.append(put(piece(9, 1), piece(5, 1), "right"))
    pass_left.wait_recv()
    piece(9, 0)[...] = (load(piece(4, 0)) + load(rows("left", 0, half))).astype(bf16)
    near.append(put(piece(9, 0), piece(6, 0), "left"))
    yield
    mate.wait_recv()
    for copy in near:
        copy.wait_recv()
    done(load(rows("me")) + load(slot(5)) + load(slot(6)) + load(slot(8)))


SCATTER_TENSOR = 10
SCATTER_SLOTS = 10
NAMES = ("far", "over_far", "up", "over_up", "down", "over_down", "me", "over")


def scatter_data(wires, place, core_mate, part_ref, given, added, slots, out_ref):
    size = part_ref.shape[0] // DATA
    half = size // 2
    load = lambda ref: ref[...].astype(f32)
    number = {name: i for i, name in enumerate(NAMES)}
    mine = lambda name: added.at[number[name]]
    mine_part = lambda name, p: added.at[number[name], pl.ds(p * half, half)]
    slot = lambda i: slots.at[i]
    piece = lambda i, p: slots.at[i, pl.ds(p * half, half)]
    put = lambda source, target, to: wires.put(source, target, on_data(place[to]))
    swaps = [
        wires.put(
            block(part_ref, core_mate[name], size), given.at[i], on_data(core_mate["me"])
        )
        for i, name in enumerate(NAMES)
    ]

    def add_up(name):
        i = number[name]
        swaps[i].wait_recv()
        mine(name)[...] = (load(given.at[i]) + load(block(part_ref, place[name], size))).astype(
            bf16
        )

    yield
    passed, near = [], []
    for i, side in enumerate(("", "over_")):
        add_up(side + "far")
        passed.append(
            (
                put(mine_part(side + "far", 1), piece(i, 1), "up"),
                put(mine_part(side + "far", 0), piece(i, 0), "down"),
            )
        )
    yield
    for i, side in enumerate(("", "over_")):
        add_up(side + "up")
        near.append(put(mine_part(side + "up", 0), piece(2 + i, 0), "up"))
        add_up(side + "down")
        near.append(put(mine_part(side + "down", 1), piece(4 + i, 1), "down"))
    add_up("me")
    add_up("over")
    yield
    for i, side in enumerate(("", "over_")):
        up, down = passed[i]
        up.wait_recv()
        target = mine_part(side + "up", 1)
        target[...] = (load(target) + load(piece(i, 1))).astype(bf16)
        near.append(put(target, piece(2 + i, 1), "up"))
        down.wait_recv()
        target = mine_part(side + "down", 0)
        target[...] = (load(target) + load(piece(i, 0))).astype(bf16)
        near.append(put(target, piece(4 + i, 0), "down"))
        yield
    for copy in near:
        copy.wait_recv()
    slot(6)[...] = (load(mine("over")) + load(slot(3)) + load(slot(5))).astype(bf16)
    last = put(slot(6), slot(7), "over")
    out_ref[...] = load(mine("me")) + load(slot(2)) + load(slot(4))
    yield
    last.wait_recv()
    out_ref[...] += load(slot(7))


SCATTER_DATA = 21


def rms_rows(values):
    return lax.rsqrt(row_total(values * values) * (1.0 / D) + norm_eps)


def rms_back(values, scale, gain, grad):
    shared = grad * gain
    inner = row_total(shared * values) * (1.0 / D)
    return scale * shared - values * (scale * scale * scale * inner)


TENSOR_NEAR = ("right", "left", "mate")
DATA_NEAR = ("over", "up", "down")


def start_kernel(
    x_ref, gain_ref, pack_ref, first_ref, full_ref, own, send, recv, local,
):
    place = tensor_places()
    data_place, core_mate = data_places()
    x = x_ref[...].astype(f32)
    own[...] = (x * rms_rows(x) * gain_ref[...]).astype(bf16)
    greet(
        [on_tensor(place[to]) for to in TENSOR_NEAR]
        + [on_data(data_place[to]) for to in DATA_NEAR]
        + [on_data(core_mate["me"])]
    )
    keep = [
        pltpu.make_async_copy(own, block(first_ref, place["me"], own.shape[0]), local.at[0]),
        pltpu.make_async_copy(
            pack_ref, block(full_ref, data_place["me"], pack_ref.shape[0]), local.at[1]
        ),
    ]
    for copy in keep:
        copy.start()
    wires = Wires(send, recv)
    together(
        gather_tensor(wires, place, own, first_ref),
        gather_data(wires, data_place, core_mate, pack_ref, full_ref),
    )
    wires.flush()
    for copy in keep:
        copy.wait()


def middle_kernel(
    part_ref, x_ref, live_ref, gain_ref, middle_ref, second_ref, slots, own, send, recv, local,
):
    place = tensor_places()
    greet([on_tensor(place[to]) for to in TENSOR_NEAR])
    wires = Wires(send, recv)

    def done(mixed):
        middle = x_ref[...].astype(f32) + live_ref[...] * mixed
        middle_ref[...] = middle
        own[...] = (middle * rms_rows(middle) * gain_ref[...]).astype(bf16)

    together(scatter_tensor(wires, place, part_ref, slots, done))
    keep = pltpu.make_async_copy(own, block(second_ref, place["me"], own.shape[0]), local.at[0])
    keep.start()
    together(gather_tensor(wires, place, own, second_ref))
    wires.flush()
    keep.wait()


def turn_kernel(
    part_ref, middle_ref, cot_ref, live_ref, gain_ref, grad_ref, mixed_ref, gain_grad_ref,
    slots, own, send, recv, local,
):
    place = tensor_places()
    greet([on_tensor(place[to]) for to in TENSOR_NEAR])
    wires = Wires(send, recv)

    def done(second_in):
        middle = middle_ref[...]
        scale = rms_rows(middle)
        gain_grad_ref[...] = jnp.sum(second_in * middle * scale, axis=0, keepdims=True)
        grad = cot_ref[...].astype(f32) + rms_back(middle, scale, gain_ref[...], second_in)
        grad_ref[...] = grad
        own[...] = (live_ref[...] * grad).astype(bf16)

    together(scatter_tensor(wires, place, part_ref, slots, done))
    keep = pltpu.make_async_copy(own, block(mixed_ref, place["me"], own.shape[0]), local.at[0])
    keep.start()
    together(gather_tensor(wires, place, own, mixed_ref))
    wires.flush()
    keep.wait()


def end_kernel(
    part_ref, weight_ref, x_ref, grad_ref, gain_ref, gains_ref, head_ref,
    input_ref, weight_out, gains_out, head_out,
    slots, given, added, data_slots, gain_own, gain_slots, wide_own, wide_slots, head_slots,
    send, recv,
):
    place = tensor_places()
    data_place, core_mate = data_places()
    me, data_me = place["me"], data_place["me"]
    others = [lax.rem(me + i, TENSOR) for i in range(1, TENSOR)]
    data_others = [lax.rem(data_me + i, DATA) for i in range(1, DATA)]
    greet([on_tensor(i) for i in others] + [on_data(i) for i in data_others])
    wires = Wires(send, recv)

    def done(first_in):
        x = x_ref[...].astype(f32)
        scale = rms_rows(x)
        gain_own[...] = gains_ref[...]
        gain_own[0:1, :] = jnp.sum(first_in * x * scale, axis=0, keepdims=True)
        input_ref[...] = grad_ref[...] + rms_back(x, scale, gain_ref[...], first_in)

    def gains():
        heads = [
            wires.put(head_ref, head_slots.at[i], on_data(to))
            for i, to in enumerate(data_others)
        ]
        yield
        yield
        yield
        yield from scatter_tensor(wires, place, part_ref, slots, done)
        near = [
            wires.put(gain_own, gain_slots.at[i], on_tensor(to))
            for i, to in enumerate(others)
        ]
        for copy in near:
            copy.wait_recv()
        total = gain_own[...]
        for i in range(TENSOR - 1):
            total = total + gain_slots[i]
        wide_own[...] = total
        all_data = [
            wires.put(wide_own, wide_slots.at[i], on_data(to))
            for i, to in enumerate(data_others)
        ]
        yield
        for copy in heads:
            copy.wait_recv()
        total = head_ref[...]
        for i in range(DATA - 1):
            total = total + head_slots[i]
        head_out[...] = total
        yield
        for copy in all_data:
            copy.wait_recv()
        total = wide_own[...]
        for i in range(DATA - 1):
            total = total + wide_slots[i]
        gains_out[...] = total

    together(
        scatter_data(
            wires, data_place, core_mate, weight_ref, given, added, data_slots, weight_out
        ),
        gains(),
    )
    wires.flush()


END_COPIES = SCATTER_TENSOR + SCATTER_DATA + TENSOR - 1 + 2 * (DATA - 1)


def communicate(kernel, number, outs, in_any, scratch, copies, operands, name):
    vmem = pl.BlockSpec(memory_space=pltpu.VMEM)
    return pl.pallas_call(
        kernel,
        out_shape=[jax.ShapeDtypeStruct(shape, kind) for shape, kind, _ in outs],
        in_specs=[vmem] * len(operands),
        out_specs=[pl.BlockSpec(memory_space=pl.ANY) if far else vmem for _, _, far in outs],
        scratch_shapes=scratch
        + [pltpu.SemaphoreType.DMA((copies,)), pltpu.SemaphoreType.DMA((copies,))]
        + ([pltpu.SemaphoreType.DMA((2,))] if in_any else []),
        compiler_params=pltpu.CompilerParams(
            collective_id=number, has_side_effects=True, vmem_limit_bytes=56 * 1024 * 1024
        ),
        cost_estimate=pl.CostEstimate(
            flops=30_000_000_000, bytes_accessed=20_000_000, transcendentals=0
        ),
        name=name,
    )(*operands)


def matmul(left_side, right_side):
    return jnp.dot(left_side, right_side, preferred_element_type=f32)


def contract_rows(left_side, right_side):
    return lax.dot_general(
        left_side, right_side, (((0,), (0,)), ((), ())), preferred_element_type=f32
    )


def times_transposed(left_side, right_side):
    return lax.dot_general(
        left_side, right_side, (((1,), (1,)), ((), ())), preferred_element_type=f32
    )


def group_rows(values):
    return lax.all_gather(values, "tensor", axis=0, tiled=True)


def row_sums(values):
    return lax.psum_scatter(
        values.astype(bf16), "tensor", scatter_dimension=0, tiled=True
    ).astype(f32)


def shards(
    block_input, out_cotangent, lengths, mixer_gain, query_weight, key_weight, value_weight,
    output_gate_weight, decay_weight, query_conv, key_conv, value_conv, decay_log, decay_bias,
    head_gain, out_weight, ffn_gain, ffn_gate, ffn_up, ffn_down,
):
    local_rows = block_input.shape[0]
    rows = local_rows * TENSOR
    depth = query_weight.shape[0]
    ff = ffn_gate.shape[1]
    width = MIX + 3 * ff
    position = lax.axis_index("tensor") * local_rows + jnp.arange(local_rows, dtype=jnp.int32)
    live = (position < lengths[0]).astype(f32)[:, None]
    pack = jnp.concatenate(
        [query_weight, key_weight, value_weight, output_gate_weight,
         jnp.pad(decay_weight.reshape(depth, 2), ((0, 0), (0, 126))), out_weight.T,
         ffn_gate, ffn_up, ffn_down.T],
        axis=1,
    )
    conv = jnp.pad(
        jnp.concatenate([query_conv, key_conv, value_conv], axis=1), ((0, 4), (0, 0))
    )
    dec = jnp.pad(
        jnp.broadcast_to(jnp.stack([-jnp.exp(decay_log[0]), decay_bias[0]])[:, None], (2, DK)),
        ((0, 6), (0, 0)),
    )
    hg = head_gain[None, :]
    local_block = pltpu.VMEM((local_rows, D), bf16)
    scatter_slots = pltpu.VMEM((SCATTER_SLOTS, local_rows, D), bf16)
    first_rows, full = communicate(
        start_kernel, 1, [((rows, D), bf16, True), ((D, width), bf16, True)], True,
        [local_block], GATHER_TENSOR + GATHER_DATA,
        (block_input, mixer_gain[None, :], pack), "start_gathers",
    )
    fed_grad = group_rows((live * out_cotangent.astype(f32)).astype(bf16))
    ffn_in = full[:, MIX : MIX + 2 * ff]
    down_t = full[:, MIX + 2 * ff :]
    proj, mixed_part, mixed_rows, o, t, u, w, qe, a, s, tails = call_forward(
        first_rows, full, conv, dec, hg
    )
    middle, second_rows = communicate(
        middle_kernel, 2, [((local_rows, D), f32, False), ((rows, D), bf16, True)], True,
        [scatter_slots, local_block], GATHER_TENSOR + SCATTER_TENSOR,
        (mixed_part, block_input, live, ffn_gain[None, :]), "middle_sums",
    )
    acts = matmul(second_rows, ffn_in)
    gate_act, up_act = acts[:, :ff], acts[:, ff:]
    sigmoid_gate = jax.nn.sigmoid(gate_act)
    hidden = (gate_act * sigmoid_gate * up_act).astype(bf16)
    hidden_grad = matmul(fed_grad, down_t)
    gate_grad = hidden_grad * up_act * sigmoid_gate * (1.0 + gate_act * (1.0 - sigmoid_gate))
    up_grad = hidden_grad * gate_act * sigmoid_gate
    act_grads = jnp.concatenate([gate_grad.astype(bf16), up_grad.astype(bf16)], axis=1)
    second_part = times_transposed(act_grads, ffn_in).astype(bf16)
    middle_grad, mixed_grad, ffn_gain_grad = communicate(
        turn_kernel, 3,
        [((local_rows, D), f32, False), ((rows, D), bf16, True), ((1, D), f32, False)], True,
        [scatter_slots, local_block], GATHER_TENSOR + SCATTER_TENSOR,
        (second_part, middle, out_cotangent, live, ffn_gain[None, :]), "turn_sums",
    )
    ffn_terms = row_sums(times_transposed(hidden, down_t))
    block_output = (middle + live * ffn_terms).astype(bf16)
    acts_wgrad = contract_rows(second_rows, act_grads)
    down_wgrad = contract_rows(fed_grad, hidden)
    out_wgrad = contract_rows(mixed_grad, mixed_rows)
    pre_grads, first_part, conv_grads, small = call_backward(
        mixed_grad, full, (proj, o, t, u, w, qe, a, s, tails), conv, dec, hg
    )
    pre_wgrad = contract_rows(first_rows, pre_grads)
    weight_grads = jnp.concatenate(
        [item.astype(bf16) for item in (pre_wgrad, out_wgrad, acts_wgrad, down_wgrad)], axis=1
    )
    gains = jnp.concatenate(
        [jnp.zeros((1, D), f32), ffn_gain_grad, jnp.pad(small[0:1], ((0, 0), (0, D - DV))),
         jnp.zeros((5, D), f32)],
        axis=0,
    )
    heads = jnp.concatenate(
        [conv_grads[:4], jnp.pad(small[1:3], ((0, 0), (0, QKV - DV))), jnp.zeros((2, QKV), f32)],
        axis=0,
    )
    block_rows = D // DATA
    vmem = pltpu.VMEM
    input_grad, sums, gain_sums, head_sums = communicate(
        end_kernel, 4,
        [((local_rows, D), f32, False), ((block_rows, width), f32, False),
         ((8, D), f32, False), ((8, QKV), f32, False)], False,
        [scatter_slots, vmem((8, block_rows, width), bf16), vmem((8, block_rows, width), bf16),
         vmem((8, block_rows, width), bf16), vmem((8, D), f32), vmem((TENSOR - 1, 8, D), f32),
         vmem((8, D), f32), vmem((DATA - 1, 8, D), f32), vmem((DATA - 1, 8, QKV), f32)],
        END_COPIES,
        (first_part, weight_grads, block_input, middle_grad, mixer_gain[None, :], gains, heads),
        "end_sums",
    )
    at = MIX
    return (
        block_output,
        input_grad,
        gain_sums[0],
        sums[:, :128],
        sums[:, 128:256],
        sums[:, 256:512],
        sums[:, 512:768],
        sums[:, 768:770].reshape(depth, 1, 2),
        head_sums[:4, :DK],
        head_sums[:4, DK : 2 * DK],
        head_sums[:4, 2 * DK :],
        head_sums[4, :1],
        head_sums[5, :1],
        gain_sums[2, :DV],
        sums[:, PRE:MIX].T,
        gain_sums[1],
        sums[:, at : at + ff],
        sums[:, at + ff : at + 2 * ff],
        sums[:, at + 2 * ff :].T,
    )


def solution(mesh):
    rows = P(("dp", "tensor"), None)
    tile = P("dp", "tensor")
    taps = P(None, "tensor")
    turned = P("tensor", "dp")
    decay = P("dp", "tensor", None)
    head = P("tensor")
    return jax.shard_map(
        shards,
        mesh=mesh,
        in_specs=(
            rows, rows, P("dp"), P(), tile, tile, tile, tile, decay, taps, taps, taps, head, head,
            P(), turned, P(), tile, tile, turned,
        ),
        out_specs=(
            rows, rows, P(), tile, tile, tile, tile, decay, taps, taps, taps, head, head,
            P(), turned, P(), tile, tile, turned,
        ),
        check_vma=False,
    )
```

```python
import functools

import jax
import jax.numpy as jnp
from jax import lax
from jax.experimental import pallas as pl
from jax.experimental.pallas import tpu as pltpu
from jax.sharding import PartitionSpec as P

DK = 128
DV = 256
QKV = 2 * DK + DV
D = 1024
GATE_END = 768
PRE = 896
MIX = 1152
TENSOR = 8
DATA = 16
CHUNK = 256
BATCH = 2
SPLIT = 2

norm_eps = 1e-06
gate_eps = 1e-05
bf16 = jnp.bfloat16
f32 = jnp.float32


def mm(left_side, right_side, left_dim=1, right_dim=0):
    return lax.dot_general(
        left_side.astype(bf16),
        right_side.astype(bf16),
        (((left_dim,), (right_dim,)), ((), ())),
        preferred_element_type=f32,
    )


def halves(values):
    high = values.astype(bf16)
    return high, (values - high.astype(f32)).astype(bf16)


def mm3(left_pair, right_pair, left_dim=1, right_dim=0):
    (lh, ll), (rh, rl) = left_pair, right_pair
    return (
        mm(lh, rh, left_dim, right_dim)
        + mm(lh, rl, left_dim, right_dim)
        + mm(ll, rh, left_dim, right_dim)
    )


def ones_mm(ones_side, values, terms):
    total = None
    for _ in range(terms):
        high = values.astype(bf16)
        part = mm(ones_side, high)
        total = part if total is None else total + part
        values = values - high.astype(f32)
    return total


def wide(lanes):
    return jnp.concatenate([lanes, lanes], axis=1)


def row_total(values):
    return jnp.sum(values, axis=-1, keepdims=True)


def softplus(z):
    return jnp.maximum(z, 0.0) + jnp.log1p(jnp.exp(-jnp.abs(z)))


def index_pair():
    return (
        lax.broadcasted_iota(jnp.int32, (CHUNK, CHUNK), 0),
        lax.broadcasted_iota(jnp.int32, (CHUNK, CHUNK), 1),
    )


def taps_sum(conv_ref, pad_ref, start):
    total = None
    for tap in range(4):
        term = conv_ref[tap : tap + 1, :] * pad_ref[pl.ds(start + 5 + tap, CHUNK), :]
        total = term if total is None else total + term
    return total


def gates(proj_ref, rows, dec_ref):
    both = proj_ref[rows, GATE_END:PRE]
    z = jnp.broadcast_to(both[:, 0:1], (CHUNK, DK)) + dec_ref[1:2, :]
    rate = jax.nn.sigmoid(jnp.broadcast_to(both[:, 1:2], (CHUNK, DK)))
    return z, dec_ref[0:1, :] * softplus(z), rate


def cumulative(decays, causal_ones):
    total = ones_mm(causal_ones, decays, 3)
    across = jnp.transpose(total)[0:1, :]
    return total, across


def ratios(total, across, causal):
    spread = wide(total) - across
    return jnp.where(causal, jnp.exp(jnp.where(causal, spread, 0.0)), 0.0)


def mix_forward(
    first_ref, pack_ref, conv_ref, dec_ref, hg_ref, fed_own, ffn_own,
    proj_ref, part_ref, mixed_ref, o_ref, t_ref, u_ref, w_ref, qe_ref, a_ref, s_ref, tail_ref,
    fed_ref, ffn_ref,
    state, pad, send, recv, local,
):
    step = pl.program_id(0)
    last_step = pl.num_programs(0) - 1
    place = tensor_places()
    data_place, core_mate = data_places()
    wires, moves = Wires(send, recv), Moves(local)
    keep = [
        moves.plan(fed_own, block(fed_ref, place["me"], fed_own.shape[0])),
        moves.plan(ffn_own, block(ffn_ref, data_place["me"], ffn_own.shape[0])),
    ]
    fed = gather_tensor(wires, place, fed_own, fed_ref, 0, fed_own.shape[0])
    ffn = gather_data(wires, data_place, core_mate, ffn_own, ffn_ref)

    @pl.when(step == 0)
    def _():
        greet(tensor_near(place) + data_near(data_place, core_mate))
        fed[0]()
        ffn[0]()
        start_all(keep)
        state[...] = jnp.zeros_like(state)
        pad[0:8, :] = jnp.zeros((8, QKV), f32)

    @pl.when(step == 1)
    def _():
        for stage in ffn[1:4]:
            stage()

    @pl.when(step == last_step)
    def _():
        for stage in (fed[4], fed[6], ffn[4], ffn[5]):
            stage()

    row, col = index_pair()
    causal = row >= col
    strict = row > col
    causal_ones = causal.astype(bf16)
    parts = range(BATCH)
    rows = [pl.ds(c * CHUNK, CHUNK) for c in parts]
    for c in parts:
        pre = mm(first_ref[rows[c], :], pack_ref[:, :PRE])
        proj_ref[rows[c], :] = pre
        pad[pl.ds(8 + c * CHUNK, CHUNK), :] = pre[:, :QKV]
    items = []
    for c in parts:
        tail_ref[c] = pad[pl.ds(c * CHUNK, 8), :]
        act = jax.nn.silu(taps_sum(conv_ref, pad, c * CHUNK))
        q, k, v = act[:, :DK], act[:, DK : 2 * DK], act[:, 2 * DK :]
        q = q * (lax.rsqrt(row_total(q * q) + norm_eps) * DK ** (-0.5))
        k = k * lax.rsqrt(row_total(k * k) + norm_eps)
        _, decays, rate = gates(proj_ref, rows[c], dec_ref)
        total, across = cumulative(decays, causal_ones)
        ratio = ratios(total, across, causal)
        kk = mm(k, k, 1, 1)
        lower = jnp.where(strict, wide(rate) * kk * ratio, 0.0)
        scores = (mm(q, k, 1, 1) * ratio).astype(bf16)
        growth = jnp.exp(total)
        last = total[CHUNK - 1 : CHUNK, :]
        tail_k = (jnp.exp(last - total) * k).astype(bf16)
        items.append((q, k, v, rate, growth, jnp.exp(last), tail_k, scores, lower))
    pad[0:8, :] = pad[pl.ds(BATCH * CHUNK, 8), :]
    size = 1
    inverse = [(row == col).astype(f32) for c in parts]
    while size < CHUNK:
        same = (row // (2 * size) == col // (2 * size)) & ((row // size) % 2 == 1) & ((col // size) % 2 == 0)
        for c in parts:
            edge = jnp.where(same, items[c][8], 0.0)
            if size == 1:
                inverse[c] = inverse[c] - edge
            else:
                pair = halves(inverse[c])
                inverse[c] = inverse[c] - mm3(halves(mm3(pair, halves(edge))), pair)
        size *= 2

    @pl.when(step == 1)
    def _():
        for i in (1, 3, 2, 5):
            fed[i]()

    @pl.when(step == last_step)
    def _():
        ffn[6]()

    eye = lax.broadcasted_iota(jnp.int32, (DK, DK), 0) == lax.broadcasted_iota(
        jnp.int32, (DK, DK), 1
    )
    later = []
    for c in parts:
        q, k, v, rate, growth, grown, tail_k, scores, _ = items[c]
        solve = inverse[c].astype(bf16)
        t_ref[c] = solve
        w = mm(solve, rate * growth * k).astype(bf16)
        u_start = mm(solve, wide(rate) * v)
        q_eff = (growth * q - mm(scores, w)).astype(bf16)
        carry = jnp.where(eye, grown, 0.0) - mm(w, tail_k, 0, 0)
        added = mm(u_start, tail_k, 0, 0)
        w_ref[c] = w
        qe_ref[c] = q_eff
        a_ref[c] = carry
        later.append((w, u_start, q_eff, scores, carry, added))
    memory = state[...]
    starts = []
    for c in parts:
        s_ref[c] = memory
        starts.append(memory)
        memory = mm(memory, later[c][4]) + later[c][5]
    state[...] = memory
    for c in parts:
        w, u_start, q_eff, scores, _, _ = later[c]
        u_ref[c] = (u_start - mm(w, starts[c], 1, 1)).astype(bf16)
        o = mm(q_eff, starts[c], 1, 1) + mm(scores, u_start)
        o_ref[rows[c], :] = o
        normed = o * lax.rsqrt(row_total(o * o) * (1.0 / DV) + gate_eps) * hg_ref[...]
        mixed = (normed * jax.nn.silu(proj_ref[rows[c], QKV:GATE_END])).astype(bf16)
        mixed_ref[rows[c], :] = mixed
        part_ref[rows[c], :] = mm(mixed, pack_ref[:, PRE:MIX], 1, 1).astype(bf16)

    @pl.when(step == last_step)
    def _():
        fed[7]()
        ffn[7]()
        wires.flush()
        for copy in keep:
            copy.wait()


def mix_backward(
    grad_ref, pack_ref, proj_ref, tail_ref, o_ref, t_ref, u_ref, w_ref, qe_ref, a_ref, s_ref,
    conv_ref, dec_ref, hg_ref, ffn_part, middle_ref, length_ref,
    pre_ref, first_ref, head_ref, small_ref, output_ref,
    dstate, padp, padg, slots, send, recv, local,
):
    step = pl.program_id(0)
    last_step = pl.num_programs(0) - 1
    place = tensor_places()
    wires, moves = Wires(send, recv), Moves(local)
    size = middle_ref.shape[0]

    def done(start, length, terms):
        live = live_rows(length_ref, start, length, size)
        output_ref[...] = (middle_ref[...] + live * terms).astype(bf16)

    ffn = scatter_tensor(wires, moves, place, ffn_part, slots, 0, size, done)

    @pl.when(step == 0)
    def _():
        greet(tensor_near(place))
        ffn[0]()
        dstate[...] = jnp.zeros_like(dstate)
        padg[pl.ds(BATCH * CHUNK, 8), :] = jnp.zeros((8, QKV), f32)
        head_ref[...] = jnp.zeros_like(head_ref)
        small_ref[...] = jnp.zeros_like(small_ref)

    row, col = index_pair()
    causal = row >= col
    strict = row > col
    causal_ones = causal.astype(bf16)
    strict_ones = strict.astype(bf16)
    upper_ones = (col >= row).astype(bf16)
    lane = lax.broadcasted_iota(jnp.int32, (CHUNK, DK), 1)
    parts = range(BATCH)
    rows = [pl.ds(c * CHUNK, CHUNK) for c in parts]
    padp[0:8, :] = tail_ref[0]
    for c in parts:
        padp[pl.ds(8 + c * CHUNK, CHUNK), :] = proj_ref[rows[c], :QKV]
    items = []
    for c in parts:
        act_pre = taps_sum(conv_ref, padp, c * CHUNK)
        act_sig = jax.nn.sigmoid(act_pre)
        act = act_pre * act_sig
        slope = act_sig * (1.0 + act_pre * (1.0 - act_sig))
        qc, kc, v = act[:, :DK], act[:, DK : 2 * DK], act[:, 2 * DK :]
        q_scale = lax.rsqrt(row_total(qc * qc) + norm_eps)
        k_scale = lax.rsqrt(row_total(kc * kc) + norm_eps)
        q = qc * (q_scale * DK ** (-0.5))
        k = kc * k_scale
        z, decays, rate = gates(proj_ref, rows[c], dec_ref)
        total, across = cumulative(decays, causal_ones)
        ratio = ratios(total, across, causal)
        key_ratio = mm(k, k, 1, 1) * ratio
        scores = mm(q, k, 1, 1) * ratio
        growth = jnp.exp(total)
        last = total[CHUNK - 1 : CHUNK, :]
        tail = jnp.exp(last - total)
        grad = mm(grad_ref[rows[c], :], pack_ref[:, PRE:MIX])
        gate = proj_ref[rows[c], QKV:GATE_END]
        gate_sig = jax.nn.sigmoid(gate)
        gate_act = gate * gate_sig
        o = o_ref[rows[c], :]
        o_scale = lax.rsqrt(row_total(o * o) * (1.0 / DV) + gate_eps)
        normed = o * o_scale
        gain = hg_ref[...]
        gate_grad = grad * normed * gain * gate_sig * (1.0 + gate * (1.0 - gate_sig))
        pre_ref[rows[c], QKV:GATE_END] = gate_grad.astype(bf16)
        grad = grad * gate_act
        small_ref[0:1, :] += jnp.sum(grad * normed, axis=0, keepdims=True)
        grad = grad * gain
        do = o_scale * (grad - normed * (row_total(grad * normed) * (1.0 / DV)))
        do = do.astype(bf16)
        items.append(
            (slope, q, k, v, q_scale, k_scale, z, decays, rate, ratio, key_ratio, scores,
             growth, jnp.exp(last), tail, do)
        )

    @pl.when(step == 1)
    def _():
        ffn[1]()
        ffn[2]()

    @pl.when(step == last_step)
    def _():
        ffn[3]()

    ends = [None] * BATCH
    change = dstate[...]
    for c in reversed(parts):
        ends[c] = change
        change = mm(change, a_ref[c], 1, 1) + mm(items[c][15], qe_ref[c], 0, 0)
    dstate[...] = change
    for c in reversed(parts):
        (slope, q, k, v, q_scale, k_scale, z, decays, rate, ratio, key_ratio, scores,
         growth, grown, tail, do) = items[c]
        start = s_ref[c]
        end = ends[c]
        start16 = start.astype(bf16)
        end16 = end.astype(bf16)
        u = u_ref[c]
        q16, k16 = q.astype(bf16), k.astype(bf16)
        du = mm(scores, do, 0, 0) + mm(tail * k, end16, 1, 1)
        dx = mm(t_ref[c], du, 0, 0)
        dx16 = dx.astype(bf16)
        d_scores = jnp.where(causal, mm(do, u, 1, 1), 0.0)
        d_lower = jnp.where(strict, -mm(dx16, u, 1, 1), 0.0)
        score_side = (d_scores * ratio).astype(bf16)
        rate2 = wide(rate)
        growth2 = wide(growth)
        lower_keys = d_lower * key_ratio
        key_side = (d_lower * rate2 * ratio).astype(bf16)
        do_state = mm(do, start16)
        dx_state = mm(dx16, start16)
        u_state = mm(u, end16)
        key_state = mm(k16, start16, 1, 1)
        dq = growth * do_state + mm(score_side, k16)
        rate_growth = rate * growth
        dk = (
            mm(score_side, q16, 0, 0)
            + mm(key_side, k16)
            + mm(key_side, k16, 0, 0)
            - rate_growth * dx_state
            + tail * u_state
        )
        dv = rate2 * dx
        d_rate = row_total(lower_keys) + row_total(dx * (v - growth2 * key_state))
        from_growth = row_total(growth * q * do_state - rate_growth * k * dx_state)
        from_tail = row_total(tail * k * u_state)
        pairs = d_scores * scores + rate2 * lower_keys
        held = ones_mm(upper_ones, pairs, 2)
        spread_growth = ones_mm(upper_ones, jnp.broadcast_to(from_growth, (CHUNK, DK)), 2)
        spread_tail = ones_mm(strict_ones, jnp.broadcast_to(from_tail, (CHUNK, DK)), 2)
        through = jnp.sum(row_total(end * start), axis=0, keepdims=True)
        d_decay = (
            row_total(jnp.where(strict, held, 0.0))
            + spread_growth
            + spread_tail
            + grown * through
        )
        dz = d_decay * dec_ref[0:1, :] * jax.nn.sigmoid(z)
        d_write = d_rate * rate * (1.0 - rate)
        pre_ref[rows[c], GATE_END:PRE] = jnp.where(
            lane == 0, dz, jnp.where(lane == 1, d_write, 0.0)
        ).astype(bf16)
        head_ref[4:5, :DK] += jnp.sum(d_decay * decays, axis=0, keepdims=True)
        head_ref[5:6, :DK] += jnp.sum(dz, axis=0, keepdims=True)
        dqc = q_scale * (DK ** (-0.5) * dq - q * (row_total(q * dq) * DK**0.5))
        dkc = k_scale * (dk - k * row_total(k * dk))
        dact = jnp.concatenate([dqc, dkc, dv], axis=1) * slope
        padg[pl.ds(c * CHUNK, CHUNK), :] = dact
        dpre = None
        for tap in range(4):
            weight = conv_ref[tap : tap + 1, :]
            term = weight * padg[pl.ds(c * CHUNK + 3 - tap, CHUNK), :]
            dpre = term if dpre is None else dpre + term
            head_ref[tap : tap + 1, :] += jnp.sum(
                dact * padp[pl.ds(c * CHUNK + 5 + tap, CHUNK), :], axis=0, keepdims=True
            )
        pre_ref[rows[c], :QKV] = dpre.astype(bf16)
        first_ref[rows[c], :] = mm(pre_ref[rows[c], :], pack_ref[:, :PRE], 1, 1).astype(bf16)
    padg[pl.ds(BATCH * CHUNK, 8), :] = padg[0:8, :]

    @pl.when(step == last_step)
    def _():
        ffn[4]()
        wires.flush()


def call_forward(first_rows, pack, conv, dec, hg, fed_own, ffn_own):
    rows = first_rows.shape[0]
    chunks = rows // CHUNK
    steps = chunks // BATCH
    anywhere = pl.BlockSpec(memory_space=pl.ANY)
    tall = lambda width: pl.BlockSpec((BATCH * CHUNK, width), lambda i: (i, 0))
    fixed = lambda shape: pl.BlockSpec(shape, lambda i: (0, 0))
    per = lambda *shape: pl.BlockSpec((BATCH,) + shape, lambda i: (i, 0, 0))
    made = jax.ShapeDtypeStruct
    return pl.pallas_call(
        mix_forward,
        grid=(steps,),
        in_specs=[
            tall(D), fixed((D, MIX)), fixed((8, QKV)), fixed((8, DK)), fixed((1, DV)),
            anywhere, anywhere,
        ],
        out_specs=[
            tall(PRE), tall(D), tall(DV), tall(DV), per(CHUNK, CHUNK), per(CHUNK, DV),
            per(CHUNK, DK), per(CHUNK, DK), per(DK, DK), per(DV, DK), per(8, QKV),
            anywhere, anywhere,
        ],
        out_shape=[
            made((rows, PRE), f32), made((rows, D), bf16), made((rows, DV), bf16),
            made((rows, DV), f32), made((chunks, CHUNK, CHUNK), bf16),
            made((chunks, CHUNK, DV), bf16), made((chunks, CHUNK, DK), bf16),
            made((chunks, CHUNK, DK), bf16), made((chunks, DK, DK), f32),
            made((chunks, DV, DK), f32), made((chunks, 8, QKV), f32),
            made((rows, D), bf16), made((D, ffn_own.shape[1]), bf16),
        ],
        scratch_shapes=[
            pltpu.VMEM((DV, DK), f32), pltpu.VMEM((BATCH * CHUNK + 8, QKV), f32),
            pltpu.SemaphoreType.DMA((GATHER_TENSOR + GATHER_DATA,)),
            pltpu.SemaphoreType.DMA((GATHER_TENSOR + GATHER_DATA,)),
            pltpu.SemaphoreType.DMA((2,)),
        ],
        compiler_params=pltpu.CompilerParams(
            dimension_semantics=("arbitrary",), vmem_limit_bytes=58 * 1024 * 1024,
            collective_id=5, has_side_effects=True,
        ),
        cost_estimate=pl.CostEstimate(
            flops=30_000_000_000, bytes_accessed=20_000_000, transcendentals=4_000_000
        ),
        name="mix_forward",
    )(first_rows, pack, conv, dec, hg, fed_own, ffn_own)


def call_backward(grad_rows, pack, saved, conv, dec, hg, ffn_part, middle, lengths):
    proj, o, t, u, w, qe, a, s, tails = saved
    rows = grad_rows.shape[0]
    chunks = rows // CHUNK
    steps = chunks // BATCH
    anywhere = pl.BlockSpec(memory_space=pl.ANY)
    tall = lambda width: pl.BlockSpec((BATCH * CHUNK, width), lambda i: (steps - 1 - i, 0))
    fixed = lambda shape: pl.BlockSpec(shape, lambda i: (0, 0))
    per = lambda *shape: pl.BlockSpec((BATCH,) + shape, lambda i: (steps - 1 - i, 0, 0))
    made = jax.ShapeDtypeStruct
    return pl.pallas_call(
        mix_backward,
        grid=(steps,),
        in_specs=[
            tall(D), fixed((D, MIX)), tall(PRE), per(8, QKV), tall(DV), per(CHUNK, CHUNK),
            per(CHUNK, DV), per(CHUNK, DK), per(CHUNK, DK), per(DK, DK), per(DV, DK),
            fixed((8, QKV)), fixed((8, DK)), fixed((1, DV)), anywhere, fixed(middle.shape),
            pl.BlockSpec(memory_space=pltpu.SMEM),
        ],
        out_specs=[tall(PRE), tall(D), fixed((8, QKV)), fixed((8, DV)), fixed(middle.shape)],
        out_shape=[
            made((rows, PRE), bf16), made((rows, D), bf16), made((8, QKV), f32),
            made((8, DV), f32), made(middle.shape, bf16),
        ],
        scratch_shapes=[
            pltpu.VMEM((DV, DK), f32), pltpu.VMEM((BATCH * CHUNK + 8, QKV), f32),
            pltpu.VMEM((BATCH * CHUNK + 8, QKV), f32),
            pltpu.VMEM((SLOTS,) + middle.shape, bf16),
            pltpu.SemaphoreType.DMA((SCATTER_TENSOR,)),
            pltpu.SemaphoreType.DMA((SCATTER_TENSOR,)),
            pltpu.SemaphoreType.DMA((len(HELD),)),
        ],
        compiler_params=pltpu.CompilerParams(
            dimension_semantics=("arbitrary",), vmem_limit_bytes=58 * 1024 * 1024,
            collective_id=6, has_side_effects=True,
        ),
        cost_estimate=pl.CostEstimate(
            flops=60_000_000_000, bytes_accessed=20_000_000, transcendentals=4_000_000
        ),
        name="mix_backward",
    )(
        grad_rows, pack, proj, tails, o, t, u, w, qe, a, s, conv, dec, hg, ffn_part, middle,
        lengths,
    )


class Wires:
    def __init__(self, send, recv):
        self.send, self.recv, self.copies = send, recv, []

    def plan(self, source, target, device):
        k = len(self.copies)
        copy = pltpu.make_async_remote_copy(
            src_ref=source,
            dst_ref=target,
            send_sem=self.send.at[k],
            recv_sem=self.recv.at[k],
            device_id=device,
            device_id_type=pl.DeviceIdType.MESH,
        )
        self.copies.append(copy)
        return copy

    def flush(self):
        for copy in self.copies:
            copy.wait_send()


class Moves:
    def __init__(self, sems):
        self.sems, self.copies = sems, []

    def plan(self, source, target):
        copy = pltpu.make_async_copy(source, target, self.sems.at[len(self.copies)])
        self.copies.append(copy)
        return copy


def on_tensor(index):
    return {"tensor": index}


def on_data(index):
    return {"dp": index}


def tensor_places():
    me = lax.axis_index("tensor")
    x, y = me % 4, me // 4
    at = lambda side, step: side * 4 + (x + step) % 4
    return {
        "me": at(y, 0), "right": at(y, 1), "far": at(y, 2), "left": at(y, 3),
        "mate": at(1 - y, 0), "mate_right": at(1 - y, 1), "mate_far": at(1 - y, 2),
        "mate_left": at(1 - y, 3),
    }


NAMES = ("far", "over_far", "up", "over_up", "down", "over_down", "me", "over")
Z_STEP = {"far": 2, "up": 1, "down": 3, "me": 0}


def data_places():
    me = lax.axis_index("dp")
    core, z, y = me % 2, (me // 2) % 4, me // 8
    here, core_mate = {}, {}
    for name in NAMES:
        side = 1 - y if name.startswith("over") else y
        step = Z_STEP.get(name.replace("over_", "").replace("over", "me"))
        base = (side * 4 + (z + step) % 4) * 2
        here[name], core_mate[name] = base + core, base + 1 - core
    return here, core_mate


def greet(devices):
    barrier = pltpu.get_barrier_semaphore()
    for device in devices:
        pl.semaphore_signal(
            barrier, inc=1, device_id=device, device_id_type=pl.DeviceIdType.MESH
        )
    pl.semaphore_wait(barrier, len(devices))


def tensor_near(place):
    return [on_tensor(place[to]) for to in ("right", "left", "mate")]


def data_near(place, core_mate):
    return [on_data(place[to]) for to in ("over", "up", "down")] + [on_data(core_mate["me"])]


def together(*lists):
    for i in range(max(len(stages) for stages in lists)):
        for stages in lists:
            if i < len(stages):
                stages[i]()


def block(ref, index, size, start=0, length=None):
    return ref.at[pl.ds(pl.multiple_of(index * size + start, 16), length or size)]


def start_all(copies):
    for copy in copies:
        copy.start()


def await_all(copies):
    for copy in copies:
        copy.wait_recv()


def gather_tensor(wires, place, own, out, start, length):
    size = out.shape[0] // TENSOR
    half = length // 2
    at = lambda who, part: block(out, place[who], size, start + part * half, half)
    send = lambda who, part, to: wires.plan(at(who, part), at(who, part), on_tensor(place[to]))
    first = {
        (to, part): wires.plan(
            own.at[pl.ds(start + part * half, half)], at("me", part), on_tensor(place[to])
        )
        for part in (0, 1)
        for to in ("mate", "right", "left")
    }
    far_low, far_high = send("right", 0, "left"), send("left", 1, "right")
    second = [[send("mate", part, "right"), send("mate", part, "left")] for part in (0, 1)]
    last = [send("far", part, "mate") for part in (0, 1)]

    def begin():
        start_all(first.values())

    def low():
        first["left", 0].wait_recv()
        far_low.start()

    def mate_low():
        first["mate", 0].wait_recv()
        start_all(second[0])

    def high():
        first["right", 0].wait_recv()
        first["right", 1].wait_recv()
        far_high.start()

    def last_low():
        far_low.wait_recv()
        last[0].start()

    def mate_high():
        first["left", 1].wait_recv()
        first["mate", 1].wait_recv()
        start_all(second[1])

    def last_high():
        far_high.wait_recv()
        last[1].start()

    def finish():
        await_all(second[0] + second[1] + last)

    return [begin, low, mate_low, high, last_low, mate_high, last_high, finish]


GATHER_TENSOR = 14


def gather_data(wires, place, core_mate, own, out):
    size = own.shape[0]
    half = size // 2
    at = lambda who: block(out, place[who], size)
    part = lambda who, i: block(out, place[who], size, i * half, half)
    send = lambda ref, to: wires.plan(ref, ref, on_data(place[to]))
    share = lambda ref: wires.plan(ref, ref, on_data(core_mate["me"]))
    first = {to: wires.plan(own, at("me"), on_data(place[to])) for to in ("over", "up", "down")}
    own_share = wires.plan(own, at("me"), on_data(core_mate["me"]))
    far_high, far_low = send(part("down", 1), "up"), send(part("up", 0), "down")
    second = {to: send(at("over"), to) for to in ("up", "down")}
    over_high, over_low = send(part("over_down", 1), "up"), send(part("over_up", 0), "down")
    shared = {who: share(at(who)) for who in ("up", "down", "over", "over_up", "over_down")}
    halves_shared = {
        (who, i): share(part(who, i)) for who in ("far", "over_far") for i in (0, 1)
    }

    def begin():
        start_all(list(first.values()) + [own_share])

    def one():
        first["up"].wait_recv()
        start_all([far_high, shared["down"]])

    def two():
        first["down"].wait_recv()
        start_all([far_low, shared["up"]])

    def three():
        first["over"].wait_recv()
        start_all([second["up"], second["down"], shared["over"]])

    def four():
        far_high.wait_recv()
        halves_shared["far", 1].start()
        far_low.wait_recv()
        halves_shared["far", 0].start()

    def five():
        second["up"].wait_recv()
        start_all([over_high, shared["over_down"]])
        second["down"].wait_recv()
        start_all([over_low, shared["over_up"]])

    def six():
        over_high.wait_recv()
        halves_shared["over_far", 1].start()
        over_low.wait_recv()
        halves_shared["over_far", 0].start()

    def finish():
        await_all([own_share] + list(shared.values()) + list(halves_shared.values()))

    return [begin, one, two, three, four, five, six, finish]


GATHER_DATA = 19
HELD = ("far", "mate", "right", "left", "me")


def scatter_tensor(wires, moves, place, part_ref, slots, start, length, done):
    size = part_ref.shape[0] // TENSOR
    half = length // 2
    rows = lambda who, at=0, count=length: block(part_ref, place[who], size, start + at, count)
    slot = lambda i: slots.at[i, pl.ds(start, length)]
    piece = lambda i, p: slots.at[i, pl.ds(start + p * half, half)]
    load = lambda ref: ref[...].astype(f32)
    send = lambda source, target, to: wires.plan(source, target, on_tensor(place[to]))
    held = {who: moves.plan(rows(who), slot(10 + i)) for i, who in enumerate(HELD)}
    mine = lambda who: load(slot(10 + HELD.index(who)))
    mine_part = lambda who, p: load(piece(10 + HELD.index(who), p))
    far = send(rows("mate_far"), slot(0), "mate")
    to_right = send(rows("mate_right"), slot(1), "right")
    to_left = send(rows("mate_left"), slot(2), "left")
    pass_right = send(piece(3, 1), piece(4, 1), "right")
    pass_left = send(piece(3, 0), piece(4, 0), "left")
    near = [
        send(rows("right", 0, half), piece(5, 0), "right"),
        send(rows("left", half, half), piece(6, 1), "left"),
    ]
    mate = send(slot(7), slot(8), "mate")
    near_late = [
        send(piece(9, 1), piece(5, 1), "right"),
        send(piece(9, 0), piece(6, 0), "left"),
    ]

    def begin():
        start_all([far, to_right, to_left])
        start_all(held.values())

    def pass_on():
        held["far"].wait()
        far.wait_recv()
        slot(3)[...] = (load(slot(0)) + mine("far")).astype(bf16)
        start_all([pass_right, pass_left])
        start_all(near)

    def to_mate():
        held["mate"].wait()
        to_right.wait_recv()
        to_left.wait_recv()
        slot(7)[...] = (load(slot(1)) + load(slot(2)) + mine("mate")).astype(bf16)
        mate.start()

    def to_near():
        held["right"].wait()
        pass_right.wait_recv()
        piece(9, 1)[...] = (load(piece(4, 1)) + mine_part("right", 1)).astype(bf16)
        near_late[0].start()
        held["left"].wait()
        pass_left.wait_recv()
        piece(9, 0)[...] = (load(piece(4, 0)) + mine_part("left", 0)).astype(bf16)
        near_late[1].start()

    def finish():
        held["me"].wait()
        await_all(near + near_late + [mate])
        done(start, length, mine("me") + load(slot(5)) + load(slot(6)) + load(slot(8)))

    return [begin, pass_on, to_mate, to_near, finish]


SCATTER_TENSOR = 10
SLOTS = 15


def scatter_data(wires, place, core_mate, part_ref, given, added, slots, out_ref):
    size = part_ref.shape[0] // DATA
    half = size // 2
    load = lambda ref: ref[...].astype(f32)
    number = {name: i for i, name in enumerate(NAMES)}
    mine = lambda name: added.at[number[name]]
    mine_part = lambda name, p: added.at[number[name], pl.ds(p * half, half)]
    slot = lambda i: slots.at[i]
    piece = lambda i, p: slots.at[i, pl.ds(p * half, half)]
    send = lambda source, target, to: wires.plan(source, target, on_data(place[to]))
    swaps = [
        wires.plan(
            block(part_ref, core_mate[name], size), given.at[i], on_data(core_mate["me"])
        )
        for i, name in enumerate(NAMES)
    ]
    sides = ("", "over_")
    passed = [
        (
            send(mine_part(side + "far", 1), piece(i, 1), "up"),
            send(mine_part(side + "far", 0), piece(i, 0), "down"),
        )
        for i, side in enumerate(sides)
    ]
    near = [
        (
            send(mine_part(side + "up", 0), piece(2 + i, 0), "up"),
            send(mine_part(side + "down", 1), piece(4 + i, 1), "down"),
        )
        for i, side in enumerate(sides)
    ]
    near_late = [
        (
            send(mine_part(side + "up", 1), piece(2 + i, 1), "up"),
            send(mine_part(side + "down", 0), piece(4 + i, 0), "down"),
        )
        for i, side in enumerate(sides)
    ]
    last = send(slot(6), slot(7), "over")

    def add_up(name):
        swaps[number[name]].wait_recv()
        total = load(given.at[number[name]]) + load(block(part_ref, place[name], size))
        mine(name)[...] = total.astype(bf16)

    def begin():
        start_all(swaps)

    def fars():
        for i in (1, 0):
            add_up(sides[i] + "far")
            start_all(passed[i])

    def nears():
        for i in (1, 0):
            add_up(sides[i] + "up")
            add_up(sides[i] + "down")
            start_all(near[i])
        add_up("me")
        add_up("over")

    def joins():
        for i in (1, 0):
            side = sides[i]
            for k, target in enumerate((mine_part(side + "up", 1), mine_part(side + "down", 0))):
                passed[i][k].wait_recv()
                target[...] = (load(target) + load(piece(i, 1 - k))).astype(bf16)
                near_late[i][k].start()

    def cross():
        await_all(near[1] + near_late[1])
        slot(6)[...] = (load(mine("over")) + load(slot(3)) + load(slot(5))).astype(bf16)
        last.start()

    def own():
        await_all(near[0] + near_late[0])
        out_ref[...] = load(mine("me")) + load(slot(2)) + load(slot(4))

    def finish():
        last.wait_recv()
        out_ref[...] += load(slot(7))

    return [begin, fars, nears, joins, cross, own, finish]


SCATTER_DATA = 21


def rms_rows(values):
    return lax.rsqrt(row_total(values * values) * (1.0 / D) + norm_eps)


def rms_back(values, scale, gain, grad):
    shared = grad * gain
    inner = row_total(shared * values) * (1.0 / D)
    return scale * shared - values * (scale * scale * scale * inner)


def live_rows(length_ref, start, length, size):
    first = lax.axis_index("tensor") * size + start
    rows = first + lax.broadcasted_iota(jnp.int32, (length, 1), 0)
    return (rows < length_ref[0]).astype(f32)


def fold(ref, first, line):
    for i in range(line.shape[1] // DK):
        ref[first + i : first + i + 1, :] = line[:, i * DK : (i + 1) * DK]


def start_kernel(
    length_ref, x_ref, cot_ref, gain_ref, q_ref, k_ref, v_ref, g_ref, decay_ref, out_w_ref,
    gate_ref, up_ref, down_ref, qc_ref, kc_ref, vc_ref, log_ref, bias_ref,
    first_ref, full_ref, fed_ref, ffn_ref, conv_ref, dec_ref,
    own, pack, send, recv, local,
):
    place = tensor_places()
    data_place, core_mate = data_places()
    x = x_ref[...].astype(f32)
    own[...] = (x * rms_rows(x) * gain_ref[...]).astype(bf16)
    turn = lambda ref: jnp.transpose(ref[...].astype(f32)).astype(bf16)
    pack[:, :DK] = q_ref[...]
    pack[:, DK : 2 * DK] = k_ref[...]
    pack[:, 2 * DK : QKV] = v_ref[...]
    pack[:, QKV:GATE_END] = g_ref[...]
    pack[:, GATE_END:PRE] = jnp.zeros((pack.shape[0], PRE - GATE_END), bf16)
    pack[:, GATE_END : GATE_END + 2] = decay_ref[...]
    pack[:, PRE:MIX] = turn(out_w_ref)
    greet(tensor_near(place) + data_near(data_place, core_mate))
    moves = Moves(local)
    wires = Wires(send, recv)
    keep = [
        moves.plan(own, block(first_ref, place["me"], own.shape[0])),
        moves.plan(pack, block(full_ref, data_place["me"], pack.shape[0])),
    ]
    size = own.shape[0]
    half = size // SPLIT
    parts = [
        gather_tensor(wires, place, own, first_ref, i * half, half) for i in range(SPLIT)
    ] + [gather_data(wires, data_place, core_mate, pack, full_ref)]
    for stages in parts:
        stages[0]()
    start_all(keep)
    fed_ref[...] = (cot_ref[...].astype(f32) * live_rows(length_ref, 0, size, size)).astype(bf16)
    ff = gate_ref.shape[1]
    ffn_ref[:, :ff] = gate_ref[...]
    ffn_ref[:, ff : 2 * ff] = up_ref[...]
    ffn_ref[:, 2 * ff :] = turn(down_ref)
    conv_ref[...] = jnp.zeros_like(conv_ref)
    conv_ref[0:4, :DK] = qc_ref[...]
    conv_ref[0:4, DK : 2 * DK] = kc_ref[...]
    conv_ref[0:4, 2 * DK :] = vc_ref[...]
    dec_ref[...] = jnp.zeros_like(dec_ref)
    dec_ref[0:1, :] = -jnp.exp(jnp.broadcast_to(log_ref[...], (1, DK)))
    dec_ref[1:2, :] = jnp.broadcast_to(bias_ref[...], (1, DK))
    together(*[stages[1:] for stages in parts])
    wires.flush()
    for copy in keep:
        copy.wait()


def flow(wires, moves, place, part_ref, slots, own, out_ref, done):
    size = own.shape[0]
    length = size // SPLIT
    parts = []
    for i in range(SPLIT):
        scatter = scatter_tensor(
            wires, moves, place, part_ref, slots, i * length, length, done
        )
        gather = gather_tensor(wires, place, own, out_ref, i * length, length)
        keep = moves.plan(
            own.at[pl.ds(i * length, length)],
            block(out_ref, place["me"], size, i * length, length),
        )

        def join(last=scatter[-1], begin=gather[0], keep=keep):
            last()
            begin()
            keep.start()

        parts.append(
            scatter[:-1] + [join] + gather[1:-1]
            + [lambda finish=gather[-1], keep=keep: (finish(), keep.wait())]
        )
    return parts


FLOW_COPIES = GATHER_TENSOR + SCATTER_TENSOR
FLOW_MOVES = len(HELD) + 1


def middle_kernel(
    part_ref, x_ref, gain_ref, length_ref, middle_ref, second_ref, slots, own, send, recv, local,
):
    place = tensor_places()
    greet(tensor_near(place))
    wires, moves = Wires(send, recv), Moves(local)

    def done(start, length, mixed):
        rows = pl.ds(start, length)
        live = live_rows(length_ref, start, length, own.shape[0])
        middle = x_ref[rows, :].astype(f32) + live * mixed
        middle_ref[rows, :] = middle
        own[rows, :] = (middle * rms_rows(middle) * gain_ref[...]).astype(bf16)

    together(*flow(wires, moves, place, part_ref, slots, own, second_ref, done))
    wires.flush()


def turn_kernel(
    part_ref, middle_ref, cot_ref, gain_ref, length_ref, second_any, acts_any, hidden_any,
    fed_any, ffn_any,
    grad_ref, mixed_ref, gain_grad_ref, ffn_part_any, wgrad_any,
    slots, own, gain_acc, second, acts, hidden, fed, ffn, ffn_part, wgrad, send, recv, local,
):
    place = tensor_places()
    greet(tensor_near(place))
    wires, moves = Wires(send, recv), Moves(local)
    gain_acc[...] = jnp.zeros_like(gain_acc)

    def done(start, length, second_in):
        rows = pl.ds(start, length)
        middle = middle_ref[rows, :]
        scale = rms_rows(middle)
        gain_acc[0:1, :] += jnp.sum(second_in * middle * scale, axis=0, keepdims=True)
        grad = cot_ref[rows, :].astype(f32) + rms_back(middle, scale, gain_ref[...], second_in)
        grad_ref[rows, :] = grad
        own[rows, :] = (live_rows(length_ref, start, length, own.shape[0]) * grad).astype(bf16)

    parts = flow(wires, moves, place, part_ref, slots, own, mixed_ref, done)
    for stages in parts:
        stages[0]()
    loads = [
        moves.plan(source, target)
        for source, target in (
            (hidden_any, hidden), (ffn_any, ffn), (second_any, second), (acts_any, acts),
            (fed_any, fed),
        )
    ]
    start_all(loads)
    ff = hidden.shape[1]
    stores = [moves.plan(ffn_part, ffn_part_any), moves.plan(wgrad, wgrad_any)]
    work = []
    tile = 256
    for i in range(second.shape[0] // tile):

        def rows_work(i=i):
            if i == 0:
                loads[0].wait()
                loads[1].wait()
            at = pl.ds(i * tile, tile)
            ffn_part[at, :] = mm(hidden[at, :], ffn[:, 2 * ff :], 1, 1).astype(bf16)
            if (i + 1) * tile == second.shape[0]:
                stores[0].start()

        work.append(rows_work)
    for i in range(D // tile):

        def acts_work(i=i):
            if i == 0:
                loads[2].wait()
                loads[3].wait()
            at = pl.ds(i * tile, tile)
            wgrad[at, : 2 * ff] = mm(second[:, at], acts[...], 0, 0).astype(bf16)

        def down_work(i=i):
            if i == 0:
                loads[4].wait()
            at = pl.ds(i * tile, tile)
            wgrad[at, 2 * ff :] = mm(fed[:, at], hidden[...], 0, 0).astype(bf16)
            if (i + 1) * tile == D:
                stores[1].start()

        work += [acts_work, down_work]
    count = len(parts[0]) - 1
    spread = [[] for _ in range(count)]
    for i, item in enumerate(work):
        spread[min(count - 1, i * (count - 2) // len(work))].append(item)
    together(
        *[stages[1:] for stages in parts],
        [lambda group=group: [item() for item in group] for group in spread],
    )
    fold(gain_grad_ref, 0, gain_acc[0:1, :])
    wires.flush()
    for copy in stores:
        copy.wait()


def ffn_kernel(second_ref, fed_ref, ffn_ref, part_ref, acts_ref, hidden_ref):
    ff = hidden_ref.shape[1]
    acts = mm(second_ref[...], ffn_ref[:, : 2 * ff])
    gate, up = acts[:, :ff], acts[:, ff:]
    hidden_grad = mm(fed_ref[...], ffn_ref[:, 2 * ff :])
    sig = jax.nn.sigmoid(gate)
    act = gate * sig
    hidden_ref[...] = (act * up).astype(bf16)
    acts_ref[:, :ff] = (hidden_grad * up * sig * (1.0 + gate * (1.0 - sig))).astype(bf16)
    acts_ref[:, ff:] = (hidden_grad * act).astype(bf16)
    part_ref[...] = mm(acts_ref[...], ffn_ref[:, : 2 * ff], 1, 1).astype(bf16)


def end_kernel(
    part_ref, x_ref, grad_ref, gain_ref, ffn_gain_ref, small_ref, head_ref, early_ref,
    first_any, pre_any, mixed_grad_any, mixed_any,
    input_ref, early_out, late_out, gains_out, head_out,
    slots, first, pre, mixed_grad, mixed, late, given, added, data_slots,
    late_given, late_added, late_slots, gain_acc, gain_own, gain_slots, wide_own, wide_slots,
    head_slots, send, recv, local,
):
    place = tensor_places()
    data_place, core_mate = data_places()
    me, data_me = place["me"], data_place["me"]
    others = [lax.rem(me + i, TENSOR) for i in range(1, TENSOR)]
    data_others = [lax.rem(data_me + i, DATA) for i in range(1, DATA)]
    greet([on_tensor(i) for i in others] + [on_data(i) for i in data_others])
    wires, moves = Wires(send, recv), Moves(local)
    gain_acc[...] = jnp.zeros_like(gain_acc)
    length = x_ref.shape[0] // SPLIT

    def done(start, length, first_in):
        rows = pl.ds(start, length)
        x = x_ref[rows, :].astype(f32)
        scale = rms_rows(x)
        gain_acc[0:1, :] += jnp.sum(first_in * x * scale, axis=0, keepdims=True)
        input_ref[rows, :] = grad_ref[rows, :] + rms_back(x, scale, gain_ref[...], first_in)

    flows = [
        scatter_tensor(wires, moves, place, part_ref, slots, i * length, length, done)
        for i in range(SPLIT)
    ]
    early = scatter_data(
        wires, data_place, core_mate, early_ref, given, added, data_slots, early_out
    )
    later = scatter_data(
        wires, data_place, core_mate, late, late_given, late_added, late_slots, late_out
    )
    heads = [
        wires.plan(head_ref, head_slots.at[i], on_data(to)) for i, to in enumerate(data_others)
    ]
    near = [
        wires.plan(gain_own, gain_slots.at[i], on_tensor(to)) for i, to in enumerate(others)
    ]
    wide_ones = [
        wires.plan(wide_own, wide_slots.at[i], on_data(to)) for i, to in enumerate(data_others)
    ]
    loads = [
        moves.plan(source, target)
        for source, target in (
            (pre_any, pre), (first_any, first), (mixed_any, mixed), (mixed_grad_any, mixed_grad),
        )
    ]
    for stages in flows:
        stages[0]()
    early[0]()
    start_all(loads)
    tile = 256

    def make_late(i):
        if i == 0:
            for copy in loads:
                copy.wait()
        at = pl.ds(i * tile, tile)
        late[at, :PRE] = mm(first[:, at], pre[...], 0, 0).astype(bf16)
        late[at, PRE:] = mm(mixed_grad[:, at], mixed[...], 0, 0).astype(bf16)

    tiles = D // tile
    make_late(0)
    early[1]()
    make_late(1)
    for stages in flows:
        stages[1]()
    make_late(2)
    early[2]()
    make_late(3)
    later[0]()
    start_all(heads)
    for stages in flows:
        stages[2]()
    early[3]()
    for stages in flows:
        stages[3]()
    later[1]()
    later[2]()
    early[4]()
    early[5]()
    for stages in flows:
        stages[4]()
    gain_own[...] = jnp.zeros_like(gain_own)
    fold(gain_own, 0, gain_acc[0:1, :])
    gain_own[8:16, :] = ffn_gain_ref[...]
    fold(gain_own, 16, small_ref[0:1, :])
    start_all(near)
    later[3]()
    early[6]()
    await_all(near)
    total = gain_own[...]
    for i in range(TENSOR - 1):
        total = total + gain_slots[i]
    wide_own[...] = total
    start_all(wide_ones)
    later[4]()
    await_all(heads)
    total = head_ref[...]
    for i in range(DATA - 1):
        total = total + head_slots[i]
    head_out[...] = total
    later[5]()
    await_all(wide_ones)
    total = wide_own[...]
    for i in range(DATA - 1):
        total = total + wide_slots[i]
    gains_out[...] = total
    later[6]()
    wires.flush()


END_COPIES = SCATTER_TENSOR * 2 + SCATTER_DATA * 2 + TENSOR - 1 + 2 * (DATA - 1)
GAINS = 24


def finish_kernel(
    output_ref, input_ref, early_ref, late_ref, gains_ref, head_ref,
    output, input_grad, mixer_gain, query, key, value, gate, decay, query_conv, key_conv,
    value_conv, decay_log, decay_bias, head_gain, out_weight, ffn_gain, ffn_gate, ffn_up,
    ffn_down,
):
    output[...] = output_ref[...]
    input_grad[...] = input_ref[...]
    mixer_gain[...] = gains_ref[0:8, :]
    ffn_gain[...] = gains_ref[8:16, :]
    head_gain[...] = gains_ref[16:18, :]
    query[...] = late_ref[:, :DK]
    key[...] = late_ref[:, DK : 2 * DK]
    value[...] = late_ref[:, 2 * DK : QKV]
    gate[...] = late_ref[:, QKV:GATE_END]
    decay[...] = late_ref[:, GATE_END : GATE_END + 2]
    out_weight[...] = jnp.transpose(late_ref[:, PRE:MIX])
    ff = ffn_gate.shape[1]
    ffn_gate[...] = early_ref[:, :ff]
    ffn_up[...] = early_ref[:, ff : 2 * ff]
    ffn_down[...] = jnp.transpose(early_ref[:, 2 * ff :])
    query_conv[...] = head_ref[0:4, :DK]
    key_conv[...] = head_ref[0:4, DK : 2 * DK]
    value_conv[...] = head_ref[0:4, 2 * DK :]
    decay_log[...] = head_ref[4:5, 0:1]
    decay_bias[...] = head_ref[5:6, 0:1]


V, H, S = "vmem", "any", "smem"
SPECS = {
    V: lambda: pl.BlockSpec(memory_space=pltpu.VMEM),
    H: lambda: pl.BlockSpec(memory_space=pl.ANY),
    S: lambda: pl.BlockSpec(memory_space=pltpu.SMEM),
}


def communicate(kernel, number, ins, outs, scratch, copies, moves, name):
    sems = [pltpu.SemaphoreType.DMA((count,)) for count in (copies, copies, moves)]
    return pl.pallas_call(
        kernel,
        out_shape=[jax.ShapeDtypeStruct(shape, kind) for shape, kind, _ in outs],
        in_specs=[SPECS[space]() for _, space in ins],
        out_specs=[SPECS[space]() for _, _, space in outs],
        scratch_shapes=[pltpu.VMEM(shape, kind) for shape, kind in scratch] + sems,
        compiler_params=pltpu.CompilerParams(
            collective_id=number, has_side_effects=True, vmem_limit_bytes=58 * 1024 * 1024
        ),
        name=name,
    )(*[item for item, _ in ins])


def call_ffn(second_rows, fed_rows, ffn_full):
    rows = second_rows.shape[0]
    ff = ffn_full.shape[1] // 3
    step = 512
    tall = lambda width: pl.BlockSpec((step, width), lambda i: (i, 0))
    made = jax.ShapeDtypeStruct
    return pl.pallas_call(
        ffn_kernel,
        grid=(rows // step,),
        in_specs=[tall(D), tall(D), pl.BlockSpec(ffn_full.shape, lambda i: (0, 0))],
        out_specs=[tall(D), tall(2 * ff), tall(ff)],
        out_shape=[made((rows, D), bf16), made((rows, 2 * ff), bf16), made((rows, ff), bf16)],
        compiler_params=pltpu.CompilerParams(
            dimension_semantics=("arbitrary",), vmem_limit_bytes=58 * 1024 * 1024
        ),
        name="ffn",
    )(second_rows, fed_rows, ffn_full)


def shards(
    block_input, out_cotangent, lengths, mixer_gain, query_weight, key_weight, value_weight,
    output_gate_weight, decay_weight, query_conv, key_conv, value_conv, decay_log, decay_bias,
    head_gain, out_weight, ffn_gain, ffn_gate, ffn_up, ffn_down,
):
    size = block_input.shape[0]
    rows = size * TENSOR
    depth = query_weight.shape[0]
    ff = ffn_gate.shape[1]
    line = lambda item: item.reshape(1, -1)
    vmem = lambda *items: [(item, V) for item in items]
    hbm = lambda *items: [(item, H) for item in items]
    length = [(lengths, S)]
    slots = ((SLOTS, size, D), bf16)
    own = ((size, D), bf16)
    first_rows, full, fed_own, ffn_own, conv, dec = communicate(
        start_kernel, 1,
        length + vmem(
            block_input, out_cotangent, line(mixer_gain), query_weight, key_weight, value_weight,
            output_gate_weight, decay_weight.reshape(depth, 2), out_weight, ffn_gate, ffn_up,
            ffn_down, query_conv, key_conv, value_conv, line(decay_log), line(decay_bias),
        ),
        [((rows, D), bf16, H), ((D, MIX), bf16, H), ((size, D), bf16, V),
         ((depth, 3 * ff), bf16, V), ((8, QKV), f32, V), ((8, DK), f32, V)],
        [own, ((depth, MIX), bf16)], GATHER_TENSOR * SPLIT + GATHER_DATA, 2, "start_gathers",
    )
    hg = line(head_gain)
    forward = call_forward(first_rows, full, conv, dec, hg, fed_own, ffn_own)
    proj, mixed_part, mixed_rows, o, t, u, w, qe, a, s, tails, fed_rows, ffn_full = forward
    middle, second_rows = communicate(
        middle_kernel, 2,
        hbm(mixed_part) + vmem(block_input, line(ffn_gain)) + length,
        [((size, D), f32, V), ((rows, D), bf16, H)],
        [slots, own], FLOW_COPIES * SPLIT, FLOW_MOVES * SPLIT, "middle_sums",
    )
    second_part, acts, hidden = call_ffn(second_rows, fed_rows, ffn_full)
    middle_grad, mixed_grad, ffn_gain_grad, ffn_part, ffn_wgrad = communicate(
        turn_kernel, 3,
        hbm(second_part) + vmem(middle, out_cotangent, line(ffn_gain)) + length
        + hbm(second_rows, acts, hidden, fed_rows, ffn_full),
        [((size, D), f32, V), ((rows, D), bf16, H), ((8, DK), f32, V), ((rows, D), bf16, H),
         ((D, 3 * ff), bf16, H)],
        [slots, own, ((8, D), f32), ((rows, D), bf16), ((rows, 2 * ff), bf16),
         ((rows, ff), bf16), ((rows, D), bf16), ((D, 3 * ff), bf16), ((rows, D), bf16),
         ((D, 3 * ff), bf16)],
        FLOW_COPIES * SPLIT, FLOW_MOVES * SPLIT + 7, "turn_sums",
    )
    pre_grads, first_part, head_grads, small, block_output = call_backward(
        mixed_grad, full, (proj, o, t, u, w, qe, a, s, tails), conv, dec, hg, ffn_part, middle,
        lengths,
    )
    block_rows = D // DATA
    early_block, late_block = ((8, block_rows, 3 * ff), bf16), ((8, block_rows, MIX), bf16)
    input_grad, early, late, gains, heads = communicate(
        end_kernel, 4,
        hbm(first_part)
        + vmem(block_input, middle_grad, line(mixer_gain), ffn_gain_grad, small, head_grads,
               ffn_wgrad)
        + hbm(first_rows, pre_grads, mixed_grad, mixed_rows),
        [((size, D), f32, V), ((block_rows, 3 * ff), f32, V), ((block_rows, MIX), f32, V),
         ((GAINS, DK), f32, V), ((8, QKV), f32, V)],
        [slots, ((rows, D), bf16), ((rows, PRE), bf16), ((rows, D), bf16), ((rows, DV), bf16),
         ((D, MIX), bf16)] + [early_block] * 3 + [late_block] * 3
        + [((8, D), f32), ((GAINS, DK), f32), ((TENSOR - 1, GAINS, DK), f32),
           ((GAINS, DK), f32), ((DATA - 1, GAINS, DK), f32), ((DATA - 1, 8, QKV), f32)],
        END_COPIES, len(HELD) * SPLIT + 4, "end_sums",
    )
    made = lambda *shape: jax.ShapeDtypeStruct(shape, f32)
    whole = lambda count: [pl.BlockSpec(memory_space=pltpu.VMEM)] * count
    outs = pl.pallas_call(
        finish_kernel,
        in_specs=whole(6),
        out_specs=whole(19),
        out_shape=[
            jax.ShapeDtypeStruct((size, D), bf16), made(size, D), made(8, DK), made(depth, DK),
            made(depth, DK), made(depth, DV), made(depth, DV), made(depth, 2), made(4, DK),
            made(4, DK), made(4, DV), made(1, 1), made(1, 1), made(2, DK), made(DV, depth),
            made(8, DK), made(depth, ff), made(depth, ff), made(ff, depth),
        ],
        compiler_params=pltpu.CompilerParams(vmem_limit_bytes=58 * 1024 * 1024),
        name="finish",
    )(block_output, input_grad, early, late, gains, heads)
    shapes = {2: (D,), 7: (depth, 1, 2), 11: (1,), 12: (1,), 13: (DV,), 15: (D,)}
    return tuple(
        item.reshape(shapes[i]) if i in shapes else item for i, item in enumerate(outs)
    )


def solution(mesh):
    rows = P(("dp", "tensor"), None)
    tile = P("dp", "tensor")
    taps = P(None, "tensor")
    turned = P("tensor", "dp")
    decay = P("dp", "tensor", None)
    head = P("tensor")
    return jax.shard_map(
        shards,
        mesh=mesh,
        in_specs=(
            rows, rows, P("dp"), P(), tile, tile, tile, tile, decay, taps, taps, taps, head, head,
            P(), turned, P(), tile, tile, turned,
        ),
        out_specs=(
            rows, rows, P(), tile, tile, tile, tile, decay, taps, taps, taps, head, head,
            P(), turned, P(), tile, tile, turned,
        ),
        check_vma=False,
    )
```

```python
import functools

import jax
import jax.numpy as jnp
from jax import lax
from jax.experimental import pallas as pl
from jax.experimental.pallas import tpu as pltpu
from jax.sharding import PartitionSpec as P

DK = 128
DV = 256
QKV = 2 * DK + DV
D = 1024
GATE_END = 768
PRE = 896
MIX = 1152
TENSOR = 8
RING = 4
DATA = 16
CHUNK = 256
BATCH = 2
SPLIT = 2

FED = "fed"
FFN = "ffn"
TOP = "top"
MIDDLE = "middle"
X_ME = "x_me"
ME = "me"
ARBITRARY = "arbitrary"
AT_TENSOR = "tensor"
DP = "dp"
RIGHT = "right"
FAR = "far"
LEFT = "left"
MATE = "mate"
MATE_RIGHT = "mate_right"
MATE_FAR = "mate_far"
MATE_LEFT = "mate_left"
OVER_FAR = "over_far"
UP = "up"
OVER_UP = "over_up"
DOWN = "down"
OVER_DOWN = "over_down"
OVER = "over"
OVER_STEM = "over_"
X_STEM = "x_"

norm_eps = 1e-06
gate_eps = 1e-05
bf16 = jnp.bfloat16
f32 = jnp.float32


def mm(left_side, right_side, left_dim=1, right_dim=0):
    return lax.dot_general(
        left_side.astype(bf16),
        right_side.astype(bf16),
        (((left_dim,), (right_dim,)), ((), ())),
        preferred_element_type=f32,
    )


def halves(values):
    high = values.astype(bf16)
    return high, (values - high.astype(f32)).astype(bf16)


def mm3(left_pair, right_pair, left_dim=1, right_dim=0):
    (lh, ll), (rh, rl) = left_pair, right_pair
    return (
        mm(lh, rh, left_dim, right_dim)
        + mm(lh, rl, left_dim, right_dim)
        + mm(ll, rh, left_dim, right_dim)
    )


def ones_mm(ones_side, values, terms):
    total = None
    for _ in range(terms):
        high = values.astype(bf16)
        part = mm(ones_side, high)
        total = part if total is None else total + part
        values = values - high.astype(f32)
    return total


def wide(lanes):
    return jnp.concatenate([lanes, lanes], axis=1)


def row_total(values):
    return jnp.sum(values, axis=-1, keepdims=True)


def softplus(z):
    return jnp.maximum(z, 0.0) + jnp.log1p(jnp.exp(-jnp.abs(z)))


def index_pair():
    return (
        lax.broadcasted_iota(jnp.int32, (CHUNK, CHUNK), 0),
        lax.broadcasted_iota(jnp.int32, (CHUNK, CHUNK), 1),
    )


def taps_sum(conv_ref, pad_ref, start):
    total = None
    for tap in range(4):
        term = conv_ref[tap : tap + 1, :] * pad_ref[pl.ds(start + 5 + tap, CHUNK), :]
        total = term if total is None else total + term
    return total


def gates(proj_ref, rows, dec_ref):
    both = proj_ref[rows, GATE_END:PRE]
    z = jnp.broadcast_to(both[:, 0:1], (CHUNK, DK)) + dec_ref[1:2, :]
    rate = jax.nn.sigmoid(jnp.broadcast_to(both[:, 1:2], (CHUNK, DK)))
    return z, dec_ref[0:1, :] * softplus(z), rate


def cumulative(decays, causal_ones):
    total = ones_mm(causal_ones, decays, 3)
    across = jnp.transpose(total)[0:1, :]
    return total, across


def ratios(total, across, causal):
    spread = wide(total) - across
    return jnp.where(causal, jnp.exp(jnp.where(causal, spread, 0.0)), 0.0)


KINDS = (FED, FFN)
FORWARD_PLAN = {
    (0, TOP): ((FFN, 0), (FED, 0)),
    (0, MIDDLE): ((FFN, 1), (FFN, 2), (FFN, 3)),
    (1, MIDDLE): ((FED, 1), (FED, 2), (FFN, 4), (FFN, 5)),
    (2, TOP): ((FFN, 6),),
}


def mix_forward(
    first_ref, pack_ref, conv_ref, dec_ref, hg_ref, fed_own, ffn_own,
    proj_ref, part_ref, mixed_ref, o_ref, t_ref, u_ref, qe_ref, a_ref, s_ref, tail_ref,
    fed_ref, ffn_ref,
    state, pad, send, recv, local,
):
    step = pl.program_id(0)
    last_step = pl.num_programs(0) - 1
    place = tensor_places()
    data_place, core_mate = data_places()
    wires = {
        FED: Wires(send, recv),
        FFN: Wires(send, recv, GATHER_RING),
    }
    moves = Moves(local)
    keep = [
        moves.plan(fed_own, block(fed_ref, place[X_ME], fed_own.shape[0])),
        moves.plan(ffn_own, block(ffn_ref, data_place[ME], ffn_own.shape[0])),
    ]
    stages = {
        FED: gather_ring(wires[FED], place, fed_own, fed_ref, 0, fed_own.shape[0]),
        FFN: gather_data(wires[FFN], data_place, core_mate, ffn_own, ffn_ref),
    }

    def advance(point):
        for at in range(3):
            todo = [stages[kind][i] for kind, i in FORWARD_PLAN.get((at, point), ())]
            if todo:

                @pl.when(step == at)
                def _():
                    for stage in todo:
                        stage()

    @pl.when(step == 0)
    def _():
        greet(ring_near(place) + data_near(data_place, core_mate))
        start_all(keep)
        state[...] = jnp.zeros_like(state)
        pad[0:8, :] = jnp.zeros((8, QKV), f32)

    advance(TOP)
    row, col = index_pair()
    causal = row >= col
    strict = row > col
    causal_ones = causal.astype(bf16)
    parts = range(BATCH)
    rows = [pl.ds(c * CHUNK, CHUNK) for c in parts]
    for c in parts:
        pre = mm(first_ref[rows[c], :], pack_ref[:, :PRE])
        proj_ref[rows[c], :] = pre
        pad[pl.ds(8 + c * CHUNK, CHUNK), :] = pre[:, :QKV]
    items = []
    for c in parts:
        tail_ref[c] = pad[pl.ds(c * CHUNK, 8), :]
        act = jax.nn.silu(taps_sum(conv_ref, pad, c * CHUNK))
        q, k, v = act[:, :DK], act[:, DK : 2 * DK], act[:, 2 * DK :]
        q = q * (lax.rsqrt(row_total(q * q) + norm_eps) * DK ** (-0.5))
        k = k * lax.rsqrt(row_total(k * k) + norm_eps)
        _, decays, rate = gates(proj_ref, rows[c], dec_ref)
        total, across = cumulative(decays, causal_ones)
        ratio = ratios(total, across, causal)
        k_pair = halves(k)
        kk = mm3(k_pair, k_pair, 1, 1)
        lower = jnp.where(strict, wide(rate) * kk * ratio, 0.0)
        scores = halves(mm3(halves(q), k_pair, 1, 1) * ratio)
        growth = jnp.exp(total)
        last = total[CHUNK - 1 : CHUNK, :]
        tail_k = halves(jnp.exp(last - total) * k)
        items.append((q, k, v, rate, growth, jnp.exp(last), tail_k, scores, lower))
    pad[0:8, :] = pad[pl.ds(BATCH * CHUNK, 8), :]
    size = 1
    inverse = [(row == col).astype(f32) for c in parts]
    while size < CHUNK:
        same = (row // (2 * size) == col // (2 * size)) & ((row // size) % 2 == 1) & ((col // size) % 2 == 0)
        for c in parts:
            edge = jnp.where(same, items[c][8], 0.0)
            if size == 1:
                inverse[c] = inverse[c] - edge
            else:
                pair = halves(inverse[c])
                inverse[c] = inverse[c] - mm3(halves(mm3(pair, halves(edge))), pair)
        size *= 2
    advance(MIDDLE)
    eye = lax.broadcasted_iota(jnp.int32, (DK, DK), 0) == lax.broadcasted_iota(
        jnp.int32, (DK, DK), 1
    )
    later = []
    for c in parts:
        q, k, v, rate, growth, grown, tail_k, scores, _ = items[c]
        t_ref[c] = inverse[c]
        solve = halves(inverse[c])
        w = halves(mm3(solve, halves(rate * growth * k)))
        u_start = mm3(solve, halves(wide(rate) * v))
        u_pair = halves(u_start)
        q_eff = growth * q - mm3(scores, w)
        carry = jnp.where(eye, grown, 0.0) - mm3(w, tail_k, 0, 0)
        added = mm3(u_pair, tail_k, 0, 0)
        qe_ref[c] = q_eff
        a_ref[c] = carry
        later.append((w, u_start, u_pair, halves(q_eff), scores, halves(carry), added))
    memory = state[...]
    starts = []
    for c in parts:
        s_ref[c] = memory
        starts.append(halves(memory))
        memory = mm3(starts[c], later[c][5]) + later[c][6]
    state[...] = memory
    for c in parts:
        w, u_start, u_pair, q_eff, scores, _, _ = later[c]
        u_ref[c] = u_start - mm3(w, starts[c], 1, 1)
        o = mm3(q_eff, starts[c], 1, 1) + mm3(scores, u_pair)
        o_ref[rows[c], :] = o
        normed = o * lax.rsqrt(row_total(o * o) * (1.0 / DV) + gate_eps) * hg_ref[...]
        mixed = (normed * jax.nn.silu(proj_ref[rows[c], QKV:GATE_END])).astype(bf16)
        mixed_ref[rows[c], :] = mixed
        part_ref[rows[c], :] = mm(mixed, pack_ref[:, PRE:MIX], 1, 1).astype(bf16)

    @pl.when(step == last_step)
    def _():
        for kind in KINDS:
            stages[kind][-1]()
            wires[kind].flush()
        for copy in keep:
            copy.wait()


def mix_backward(
    grad_ref, pack_ref, proj_ref, tail_ref, o_ref, t_ref, u_ref, qe_ref, a_ref, s_ref,
    conv_ref, dec_ref, hg_ref, ffn_part, middle_ref, length_ref,
    pre_ref, first_ref, head_ref, small_ref, output_ref,
    dstate, padp, padg, slots, send, recv, local,
):
    step = pl.program_id(0)
    last_step = pl.num_programs(0) - 1
    place = tensor_places()
    wires, moves = Wires(send, recv), Moves(local)
    size = middle_ref.shape[0]

    def done(start, length, terms):
        live = live_rows(length_ref, start, length, size)
        output_ref[...] = (middle_ref[...] + live * terms).astype(bf16)

    ffn = scatter_ring(wires, moves, place, ffn_part, slots, 0, size, done)

    @pl.when(step == 0)
    def _():
        greet(ring_near(place))
        ffn[0]()
        dstate[...] = jnp.zeros_like(dstate)
        padg[pl.ds(BATCH * CHUNK, 8), :] = jnp.zeros((8, QKV), f32)
        head_ref[...] = jnp.zeros_like(head_ref)
        small_ref[...] = jnp.zeros_like(small_ref)

    row, col = index_pair()
    causal = row >= col
    strict = row > col
    causal_ones = causal.astype(bf16)
    strict_ones = strict.astype(bf16)
    upper_ones = (col >= row).astype(bf16)
    lane = lax.broadcasted_iota(jnp.int32, (CHUNK, DK), 1)
    parts = range(BATCH)
    rows = [pl.ds(c * CHUNK, CHUNK) for c in parts]
    padp[0:8, :] = tail_ref[0]
    for c in parts:
        padp[pl.ds(8 + c * CHUNK, CHUNK), :] = proj_ref[rows[c], :QKV]
    items = []
    for c in parts:
        act_pre = taps_sum(conv_ref, padp, c * CHUNK)
        act_sig = jax.nn.sigmoid(act_pre)
        act = act_pre * act_sig
        slope = act_sig * (1.0 + act_pre * (1.0 - act_sig))
        qc, kc, v = act[:, :DK], act[:, DK : 2 * DK], act[:, 2 * DK :]
        q_scale = lax.rsqrt(row_total(qc * qc) + norm_eps)
        k_scale = lax.rsqrt(row_total(kc * kc) + norm_eps)
        q = qc * (q_scale * DK ** (-0.5))
        k = kc * k_scale
        z, decays, rate = gates(proj_ref, rows[c], dec_ref)
        total, across = cumulative(decays, causal_ones)
        ratio = ratios(total, across, causal)
        k_pair = halves(k)
        key_ratio = mm3(k_pair, k_pair, 1, 1) * ratio
        scores = mm3(halves(q), k_pair, 1, 1) * ratio
        growth = jnp.exp(total)
        last = total[CHUNK - 1 : CHUNK, :]
        tail = jnp.exp(last - total)
        grad = mm(grad_ref[rows[c], :], pack_ref[:, PRE:MIX])
        gate = proj_ref[rows[c], QKV:GATE_END]
        gate_sig = jax.nn.sigmoid(gate)
        gate_act = gate * gate_sig
        o = o_ref[rows[c], :]
        o_scale = lax.rsqrt(row_total(o * o) * (1.0 / DV) + gate_eps)
        normed = o * o_scale
        gain = hg_ref[...]
        gate_grad = grad * normed * gain * gate_sig * (1.0 + gate * (1.0 - gate_sig))
        pre_ref[rows[c], QKV:GATE_END] = gate_grad.astype(bf16)
        grad = grad * gate_act
        small_ref[0:1, :] += jnp.sum(grad * normed, axis=0, keepdims=True)
        grad = grad * gain
        do = o_scale * (grad - normed * (row_total(grad * normed) * (1.0 / DV)))
        do = halves(do)
        items.append(
            (slope, q, k, v, q_scale, k_scale, z, decays, rate, ratio, key_ratio, scores,
             growth, jnp.exp(last), tail, do)
        )

    @pl.when(step == 1)
    def _():
        ffn[1]()

    ends = [None] * BATCH
    change = dstate[...]
    for c in reversed(parts):
        ends[c] = change
        change = mm3(halves(change), halves(a_ref[c]), 1, 1) + mm3(
            items[c][15], halves(qe_ref[c]), 0, 0
        )
    dstate[...] = change
    for c in reversed(parts):
        (slope, q, k, v, q_scale, k_scale, z, decays, rate, ratio, key_ratio, scores,
         growth, grown, tail, do) = items[c]
        start = s_ref[c]
        end = ends[c]
        start_pair, end_pair = halves(start), halves(end)
        u = halves(u_ref[c])
        k_pair = halves(k)
        q16, k16 = q.astype(bf16), k_pair[0]
        du = mm3(halves(scores), do, 0, 0) + mm3(halves(tail * k), end_pair, 1, 1)
        dx = mm3(halves(t_ref[c]), halves(du), 0, 0)
        dx_pair = halves(dx)
        d_scores = jnp.where(causal, mm3(do, u, 1, 1), 0.0)
        d_lower = jnp.where(strict, -mm3(dx_pair, u, 1, 1), 0.0)
        score_side = (d_scores * ratio).astype(bf16)
        rate2 = wide(rate)
        growth2 = wide(growth)
        lower_keys = d_lower * key_ratio
        key_side = (d_lower * rate2 * ratio).astype(bf16)
        do_state = mm3(do, start_pair)
        dx_state = mm3(dx_pair, start_pair)
        u_state = mm3(u, end_pair)
        key_state = mm3(k_pair, start_pair, 1, 1)
        dq = growth * do_state + mm(score_side, k16)
        rate_growth = rate * growth
        dk = (
            mm(score_side, q16, 0, 0)
            + mm(key_side, k16)
            + mm(key_side, k16, 0, 0)
            - rate_growth * dx_state
            + tail * u_state
        )
        dv = rate2 * dx
        d_rate = row_total(lower_keys) + row_total(dx * (v - growth2 * key_state))
        from_growth = row_total(growth * q * do_state - rate_growth * k * dx_state)
        from_tail = row_total(tail * k * u_state)
        pairs = d_scores * scores + rate2 * lower_keys
        held = ones_mm(upper_ones, pairs, 2)
        spread_growth = ones_mm(upper_ones, jnp.broadcast_to(from_growth, (CHUNK, DK)), 2)
        spread_tail = ones_mm(strict_ones, jnp.broadcast_to(from_tail, (CHUNK, DK)), 2)
        through = jnp.sum(row_total(end * start), axis=0, keepdims=True)
        d_decay = (
            row_total(jnp.where(strict, held, 0.0))
            + spread_growth
            + spread_tail
            + grown * through
        )
        dz = d_decay * dec_ref[0:1, :] * jax.nn.sigmoid(z)
        d_write = d_rate * rate * (1.0 - rate)
        pre_ref[rows[c], GATE_END:PRE] = jnp.where(
            lane == 0, dz, jnp.where(lane == 1, d_write, 0.0)
        ).astype(bf16)
        head_ref[4:5, :DK] += jnp.sum(d_decay * decays, axis=0, keepdims=True)
        head_ref[5:6, :DK] += jnp.sum(dz, axis=0, keepdims=True)
        dqc = q_scale * (DK ** (-0.5) * dq - q * (row_total(q * dq) * DK**0.5))
        dkc = k_scale * (dk - k * row_total(k * dk))
        dact = jnp.concatenate([dqc, dkc, dv], axis=1) * slope
        padg[pl.ds(c * CHUNK, CHUNK), :] = dact
        dpre = None
        for tap in range(4):
            weight = conv_ref[tap : tap + 1, :]
            term = weight * padg[pl.ds(c * CHUNK + 3 - tap, CHUNK), :]
            dpre = term if dpre is None else dpre + term
            head_ref[tap : tap + 1, :] += jnp.sum(
                dact * padp[pl.ds(c * CHUNK + 5 + tap, CHUNK), :], axis=0, keepdims=True
            )
        pre_ref[rows[c], :QKV] = dpre.astype(bf16)
        first_ref[rows[c], :] = mm(pre_ref[rows[c], :], pack_ref[:, :PRE], 1, 1).astype(bf16)
    padg[pl.ds(BATCH * CHUNK, 8), :] = padg[0:8, :]

    @pl.when(step == last_step)
    def _():
        ffn[2]()
        wires.flush()


def call_forward(first_rows, pack, conv, dec, hg, fed_own, ffn_own):
    rows = first_rows.shape[0]
    chunks = rows // CHUNK
    steps = chunks // BATCH
    anywhere = pl.BlockSpec(memory_space=pl.ANY)
    tall = lambda width: pl.BlockSpec((BATCH * CHUNK, width), lambda i: (i, 0))
    fixed = lambda shape: pl.BlockSpec(shape, lambda i: (0, 0))
    per = lambda *shape: pl.BlockSpec((BATCH,) + shape, lambda i: (i, 0, 0))
    made = jax.ShapeDtypeStruct
    return pl.pallas_call(
        mix_forward,
        grid=(steps,),
        in_specs=[
            tall(D), fixed((D, MIX)), fixed((8, QKV)), fixed((8, DK)), fixed((1, DV)),
            anywhere, anywhere,
        ],
        out_specs=[
            tall(PRE), tall(D), tall(DV), tall(DV), per(CHUNK, CHUNK), per(CHUNK, DV),
            per(CHUNK, DK), per(DK, DK), per(DV, DK), per(8, QKV),
            anywhere, anywhere,
        ],
        out_shape=[
            made((rows, PRE), f32), made((rows, D), bf16), made((rows, DV), bf16),
            made((rows, DV), f32), made((chunks, CHUNK, CHUNK), f32),
            made((chunks, CHUNK, DV), f32),
            made((chunks, CHUNK, DK), f32), made((chunks, DK, DK), f32),
            made((chunks, DV, DK), f32), made((chunks, 8, QKV), f32),
            made((rows // 2, D), bf16), made((D, ffn_own.shape[1]), bf16),
        ],
        scratch_shapes=[
            pltpu.VMEM((DV, DK), f32), pltpu.VMEM((BATCH * CHUNK + 8, QKV), f32),
            pltpu.SemaphoreType.DMA((GATHER_RING + GATHER_DATA,)),
            pltpu.SemaphoreType.DMA((GATHER_RING + GATHER_DATA,)),
            pltpu.SemaphoreType.DMA((2,)),
        ],
        compiler_params=pltpu.CompilerParams(
            dimension_semantics=(ARBITRARY,), vmem_limit_bytes=58 * 1024 * 1024,
            collective_id=5, has_side_effects=True,
        ),
        cost_estimate=pl.CostEstimate(
            flops=30_000_000_000, bytes_accessed=20_000_000, transcendentals=4_000_000
        ),
        name="mix_forward",
    )(first_rows, pack, conv, dec, hg, fed_own, ffn_own)


def call_backward(grad_rows, pack, saved, conv, dec, hg, ffn_part, middle, lengths):
    proj, o, t, u, qe, a, s, tails = saved
    rows = grad_rows.shape[0]
    chunks = rows // CHUNK
    steps = chunks // BATCH
    anywhere = pl.BlockSpec(memory_space=pl.ANY)
    tall = lambda width: pl.BlockSpec((BATCH * CHUNK, width), lambda i: (steps - 1 - i, 0))
    fixed = lambda shape: pl.BlockSpec(shape, lambda i: (0, 0))
    per = lambda *shape: pl.BlockSpec((BATCH,) + shape, lambda i: (steps - 1 - i, 0, 0))
    made = jax.ShapeDtypeStruct
    return pl.pallas_call(
        mix_backward,
        grid=(steps,),
        in_specs=[
            tall(D), fixed((D, MIX)), tall(PRE), per(8, QKV), tall(DV), per(CHUNK, CHUNK),
            per(CHUNK, DV), per(CHUNK, DK), per(DK, DK), per(DV, DK),
            fixed((8, QKV)), fixed((8, DK)), fixed((1, DV)), anywhere, fixed(middle.shape),
            pl.BlockSpec(memory_space=pltpu.SMEM),
        ],
        out_specs=[tall(PRE), tall(D), fixed((8, QKV)), fixed((8, DV)), fixed(middle.shape)],
        out_shape=[
            made((rows, PRE), bf16), made((rows, D), bf16), made((8, QKV), f32),
            made((8, DV), f32), made(middle.shape, bf16),
        ],
        scratch_shapes=[
            pltpu.VMEM((DV, DK), f32), pltpu.VMEM((BATCH * CHUNK + 8, QKV), f32),
            pltpu.VMEM((BATCH * CHUNK + 8, QKV), f32),
            pltpu.VMEM((RING_SLOTS,) + middle.shape, bf16),
            pltpu.SemaphoreType.DMA((SCATTER_RING,)),
            pltpu.SemaphoreType.DMA((SCATTER_RING,)),
            pltpu.SemaphoreType.DMA((len(HELD),)),
        ],
        compiler_params=pltpu.CompilerParams(
            dimension_semantics=(ARBITRARY,), vmem_limit_bytes=58 * 1024 * 1024,
            collective_id=6, has_side_effects=True,
        ),
        cost_estimate=pl.CostEstimate(
            flops=60_000_000_000, bytes_accessed=20_000_000, transcendentals=4_000_000
        ),
        name="mix_backward",
    )(
        grad_rows, pack, proj, tails, o, t, u, qe, a, s, conv, dec, hg, ffn_part, middle,
        lengths,
    )


class Wires:
    def __init__(self, send, recv, base=0):
        self.send, self.recv, self.copies, self.base = send, recv, [], base

    def plan(self, source, target, device):
        k = self.base + len(self.copies)
        copy = pltpu.make_async_remote_copy(
            src_ref=source,
            dst_ref=target,
            send_sem=self.send.at[k],
            recv_sem=self.recv.at[k],
            device_id=device,
            device_id_type=pl.DeviceIdType.MESH,
        )
        self.copies.append(copy)
        return copy

    def flush(self):
        for copy in self.copies:
            copy.wait_send()


class Moves:
    def __init__(self, sems):
        self.sems, self.copies = sems, []

    def plan(self, source, target):
        copy = pltpu.make_async_copy(source, target, self.sems.at[len(self.copies)])
        self.copies.append(copy)
        return copy


def on_tensor(index):
    return {AT_TENSOR: index}


def on_data(index):
    return {DP: index}


def tensor_places():
    me = lax.axis_index(AT_TENSOR)
    x, y = me % 4, me // 4
    at = lambda side, step: side * 4 + (x + step) % 4
    return {
        ME: at(y, 0), RIGHT: at(y, 1), FAR: at(y, 2), LEFT: at(y, 3),
        MATE: at(1 - y, 0), MATE_RIGHT: at(1 - y, 1), MATE_FAR: at(1 - y, 2),
        MATE_LEFT: at(1 - y, 3),
        X_ME: x, "x_right": (x + 1) % 4, "x_far": (x + 2) % 4, "x_left": (x + 3) % 4,
    }


NAMES = (FAR, OVER_FAR, UP, OVER_UP, DOWN, OVER_DOWN, ME, OVER)
Z_STEP = {FAR: 2, UP: 1, DOWN: 3, ME: 0}


def data_places():
    me = lax.axis_index(DP)
    core, z, y = me % 2, (me // 2) % 4, me // 8
    here, core_mate = {}, {}
    for name in NAMES:
        side = 1 - y if name.startswith(OVER) else y
        step = Z_STEP.get(name.replace(OVER_STEM, "").replace(OVER, ME))
        base = (side * 4 + (z + step) % 4) * 2
        here[name], core_mate[name] = base + core, base + 1 - core
    return here, core_mate


def greet(devices):
    barrier = pltpu.get_barrier_semaphore()
    for device in devices:
        pl.semaphore_signal(
            barrier, inc=1, device_id=device, device_id_type=pl.DeviceIdType.MESH
        )
    pl.semaphore_wait(barrier, len(devices))


def tensor_near(place):
    return [on_tensor(place[to]) for to in (RIGHT, LEFT, MATE)]


def ring_near(place):
    return [on_tensor(place[to]) for to in (RIGHT, LEFT)]


def data_near(place, core_mate):
    return [on_data(place[to]) for to in (OVER, UP, DOWN)] + [on_data(core_mate[ME])]


def together(*lists):
    for i in range(max(len(stages) for stages in lists)):
        for stages in lists:
            if i < len(stages):
                stages[i]()


def block(ref, index, size, start=0, length=None):
    return ref.at[pl.ds(pl.multiple_of(index * size + start, 16), length or size)]


def start_all(copies):
    for copy in copies:
        copy.start()


def await_all(copies):
    for copy in copies:
        copy.wait_recv()


def gather_tensor(wires, place, own, out, start, length):
    size = out.shape[0] // TENSOR
    half = length // 2
    at = lambda who, part: block(out, place[who], size, start + part * half, half)
    send = lambda who, part, to: wires.plan(at(who, part), at(who, part), on_tensor(place[to]))
    first = {
        (to, part): wires.plan(
            own.at[pl.ds(start + part * half, half)], at(ME, part), on_tensor(place[to])
        )
        for part in (0, 1)
        for to in (MATE, RIGHT, LEFT)
    }
    far_low, far_high = send(RIGHT, 0, LEFT), send(LEFT, 1, RIGHT)
    second = [[send(MATE, part, RIGHT), send(MATE, part, LEFT)] for part in (0, 1)]
    last = [send(FAR, part, MATE) for part in (0, 1)]

    def begin():
        start_all(first.values())

    def low():
        first[LEFT, 0].wait_recv()
        far_low.start()

    def mate_low():
        first[MATE, 0].wait_recv()
        start_all(second[0])

    def high():
        first[RIGHT, 0].wait_recv()
        first[RIGHT, 1].wait_recv()
        far_high.start()

    def last_low():
        far_low.wait_recv()
        last[0].start()

    def mate_high():
        first[LEFT, 1].wait_recv()
        first[MATE, 1].wait_recv()
        start_all(second[1])

    def last_high():
        far_high.wait_recv()
        last[1].start()

    def finish():
        await_all(second[0] + second[1] + last)

    return [begin, low, mate_low, high, last_low, mate_high, last_high, finish]


GATHER_TENSOR = 14


def gather_ring(wires, place, own, out, start, length):
    size = out.shape[0] // RING
    half = length // 2
    at = lambda who, part: block(out, place[X_STEM + who], size, start + part * half, half)
    send = lambda who, part, to: wires.plan(at(who, part), at(who, part), on_tensor(place[to]))
    first = {
        (to, part): wires.plan(
            own.at[pl.ds(start + part * half, half)], at(ME, part), on_tensor(place[to])
        )
        for to, part in ((LEFT, 0), (RIGHT, 1), (LEFT, 1), (RIGHT, 0))
    }
    far_low, far_high = send(RIGHT, 0, LEFT), send(LEFT, 1, RIGHT)

    def begin():
        start_all(first.values())

    def low():
        first[LEFT, 0].wait_recv()
        far_low.start()

    def high():
        first[RIGHT, 1].wait_recv()
        far_high.start()

    def finish():
        await_all([first[LEFT, 1], first[RIGHT, 0], far_low, far_high])

    return [begin, low, high, finish]


GATHER_RING = 6


def gather_data(wires, place, core_mate, own, out):
    size = own.shape[0]
    half = size // 2
    at = lambda who: block(out, place[who], size)
    part = lambda who, i: block(out, place[who], size, i * half, half)
    send = lambda ref, to: wires.plan(ref, ref, on_data(place[to]))
    share = lambda ref: wires.plan(ref, ref, on_data(core_mate[ME]))
    first = {to: wires.plan(own, at(ME), on_data(place[to])) for to in (OVER, UP, DOWN)}
    own_share = wires.plan(own, at(ME), on_data(core_mate[ME]))
    far_high, far_low = send(part(DOWN, 1), UP), send(part(UP, 0), DOWN)
    second = {to: send(at(OVER), to) for to in (UP, DOWN)}
    over_high, over_low = send(part(OVER_DOWN, 1), UP), send(part(OVER_UP, 0), DOWN)
    shared = {who: share(at(who)) for who in (UP, DOWN, OVER, OVER_UP, OVER_DOWN)}
    halves_shared = {
        (who, i): share(part(who, i)) for who in (FAR, OVER_FAR) for i in (0, 1)
    }

    def begin():
        start_all(list(first.values()) + [own_share])

    def one():
        first[UP].wait_recv()
        start_all([far_high, shared[DOWN]])

    def two():
        first[DOWN].wait_recv()
        start_all([far_low, shared[UP]])

    def three():
        first[OVER].wait_recv()
        start_all([second[UP], second[DOWN], shared[OVER]])

    def four():
        far_high.wait_recv()
        halves_shared[FAR, 1].start()
        far_low.wait_recv()
        halves_shared[FAR, 0].start()

    def five():
        second[UP].wait_recv()
        start_all([over_high, shared[OVER_DOWN]])
        second[DOWN].wait_recv()
        start_all([over_low, shared[OVER_UP]])

    def six():
        over_high.wait_recv()
        halves_shared[OVER_FAR, 1].start()
        over_low.wait_recv()
        halves_shared[OVER_FAR, 0].start()

    def finish():
        await_all([own_share] + list(shared.values()) + list(halves_shared.values()))

    return [begin, one, two, three, four, five, six, finish]


GATHER_DATA = 19
HELD = (FAR, MATE, RIGHT, LEFT, ME)


def scatter_tensor(wires, moves, place, part_ref, slots, start, length, done):
    size = part_ref.shape[0] // TENSOR
    half = length // 2
    rows = lambda who, at=0, count=length: block(part_ref, place[who], size, start + at, count)
    slot = lambda i: slots.at[i, pl.ds(start, length)]
    piece = lambda i, p: slots.at[i, pl.ds(start + p * half, half)]
    load = lambda ref: ref[...].astype(f32)
    send = lambda source, target, to: wires.plan(source, target, on_tensor(place[to]))
    held = {who: moves.plan(rows(who), slot(10 + i)) for i, who in enumerate(HELD)}
    mine = lambda who: load(slot(10 + HELD.index(who)))
    mine_part = lambda who, p: load(piece(10 + HELD.index(who), p))
    far = send(rows(MATE_FAR), slot(0), MATE)
    to_right = send(rows(MATE_RIGHT), slot(1), RIGHT)
    to_left = send(rows(MATE_LEFT), slot(2), LEFT)
    pass_right = send(piece(3, 1), piece(4, 1), RIGHT)
    pass_left = send(piece(3, 0), piece(4, 0), LEFT)
    near = [
        send(rows(RIGHT, 0, half), piece(5, 0), RIGHT),
        send(rows(LEFT, half, half), piece(6, 1), LEFT),
    ]
    mate = send(slot(7), slot(8), MATE)
    near_late = [
        send(piece(9, 1), piece(5, 1), RIGHT),
        send(piece(9, 0), piece(6, 0), LEFT),
    ]

    def begin():
        start_all([far, to_right, to_left])
        start_all(held.values())

    def pass_on():
        held[FAR].wait()
        far.wait_recv()
        slot(3)[...] = (load(slot(0)) + mine(FAR)).astype(bf16)
        start_all([pass_right, pass_left])
        start_all(near)

    def to_mate():
        held[MATE].wait()
        to_right.wait_recv()
        to_left.wait_recv()
        slot(7)[...] = (load(slot(1)) + load(slot(2)) + mine(MATE)).astype(bf16)
        mate.start()

    def to_near():
        held[RIGHT].wait()
        pass_right.wait_recv()
        piece(9, 1)[...] = (load(piece(4, 1)) + mine_part(RIGHT, 1)).astype(bf16)
        near_late[0].start()
        held[LEFT].wait()
        pass_left.wait_recv()
        piece(9, 0)[...] = (load(piece(4, 0)) + mine_part(LEFT, 0)).astype(bf16)
        near_late[1].start()

    def finish():
        held[ME].wait()
        await_all(near + near_late + [mate])
        done(start, length, mine(ME) + load(slot(5)) + load(slot(6)) + load(slot(8)))

    return [begin, pass_on, to_mate, to_near, finish]


SCATTER_TENSOR = 10
SLOTS = 15


def scatter_ring(wires, moves, place, part_ref, slots, start, length, done):
    size = part_ref.shape[0] // RING
    half = length // 2
    rows = lambda who, at, count: block(part_ref, place[X_STEM + who], size, start + at, count)
    slot = lambda i: slots.at[i, pl.ds(start, length)]
    piece = lambda i, p: slots.at[i, pl.ds(start + p * half, half)]
    load = lambda ref: ref[...].astype(f32)
    send = lambda source, target, to: wires.plan(source, target, on_tensor(place[to]))
    held = {
        who: moves.plan(rows(who, 0, length), slot(4 + i))
        for i, who in enumerate((RIGHT, LEFT, ME))
    }
    pass_right = send(rows(FAR, half, half), piece(0, 1), RIGHT)
    pass_left = send(rows(FAR, 0, half), piece(0, 0), LEFT)
    near = [
        send(rows(RIGHT, 0, half), piece(1, 0), RIGHT),
        send(rows(LEFT, half, half), piece(2, 1), LEFT),
    ]
    near_late = [
        send(piece(3, 1), piece(1, 1), RIGHT),
        send(piece(3, 0), piece(2, 0), LEFT),
    ]

    def begin():
        start_all([pass_right, pass_left] + near)
        start_all(held.values())

    def to_near():
        held[RIGHT].wait()
        pass_right.wait_recv()
        piece(3, 1)[...] = (load(piece(0, 1)) + load(piece(4, 1))).astype(bf16)
        near_late[0].start()
        held[LEFT].wait()
        pass_left.wait_recv()
        piece(3, 0)[...] = (load(piece(0, 0)) + load(piece(5, 0))).astype(bf16)
        near_late[1].start()

    def finish():
        held[ME].wait()
        await_all(near + near_late)
        done(start, length, load(slot(6)) + load(slot(1)) + load(slot(2)))

    return [begin, to_near, finish]


SCATTER_RING = 6
RING_SLOTS = 7


def scatter_data(wires, place, core_mate, part_ref, given, added, slots, out_ref):
    size = part_ref.shape[0] // DATA
    half = size // 2
    load = lambda ref: ref[...].astype(f32)
    number = {name: i for i, name in enumerate(NAMES)}
    mine = lambda name: added.at[number[name]]
    mine_part = lambda name, p: added.at[number[name], pl.ds(p * half, half)]
    slot = lambda i: slots.at[i]
    piece = lambda i, p: slots.at[i, pl.ds(p * half, half)]
    send = lambda source, target, to: wires.plan(source, target, on_data(place[to]))
    swaps = [
        wires.plan(
            block(part_ref, core_mate[name], size), given.at[i], on_data(core_mate[ME])
        )
        for i, name in enumerate(NAMES)
    ]
    sides = ("", OVER_STEM)
    passed = [
        (
            send(mine_part(side + FAR, 1), piece(i, 1), UP),
            send(mine_part(side + FAR, 0), piece(i, 0), DOWN),
        )
        for i, side in enumerate(sides)
    ]
    near = [
        (
            send(mine_part(side + UP, 0), piece(2 + i, 0), UP),
            send(mine_part(side + DOWN, 1), piece(4 + i, 1), DOWN),
        )
        for i, side in enumerate(sides)
    ]
    near_late = [
        (
            send(mine_part(side + UP, 1), piece(2 + i, 1), UP),
            send(mine_part(side + DOWN, 0), piece(4 + i, 0), DOWN),
        )
        for i, side in enumerate(sides)
    ]
    last = send(slot(6), slot(7), OVER)

    def add_up(name):
        swaps[number[name]].wait_recv()
        total = load(given.at[number[name]]) + load(block(part_ref, place[name], size))
        mine(name)[...] = total.astype(bf16)

    def begin():
        start_all(swaps)

    def fars():
        for i in (1, 0):
            add_up(sides[i] + FAR)
            start_all(passed[i])

    def nears():
        for i in (1, 0):
            add_up(sides[i] + UP)
            add_up(sides[i] + DOWN)
            start_all(near[i])
        add_up(ME)
        add_up(OVER)

    def joins():
        for i in (1, 0):
            side = sides[i]
            for k, target in enumerate((mine_part(side + UP, 1), mine_part(side + DOWN, 0))):
                passed[i][k].wait_recv()
                target[...] = (load(target) + load(piece(i, 1 - k))).astype(bf16)
                near_late[i][k].start()

    def cross():
        await_all(near[1] + near_late[1])
        slot(6)[...] = (load(mine(OVER)) + load(slot(3)) + load(slot(5))).astype(bf16)
        last.start()

    def own():
        await_all(near[0] + near_late[0])
        out_ref[...] = load(mine(ME)) + load(slot(2)) + load(slot(4))

    def finish():
        last.wait_recv()
        out_ref[...] += load(slot(7))

    return [begin, fars, nears, joins, cross, own, finish]


SCATTER_DATA = 21


def rms_rows(values):
    return lax.rsqrt(row_total(values * values) * (1.0 / D) + norm_eps)


def rms_back(values, scale, gain, grad):
    shared = grad * gain
    inner = row_total(shared * values) * (1.0 / D)
    return scale * shared - values * (scale * scale * scale * inner)


def live_rows(length_ref, start, length, size):
    first = lax.axis_index(AT_TENSOR) * size + start
    rows = first + lax.broadcasted_iota(jnp.int32, (length, 1), 0)
    return (rows < length_ref[0]).astype(f32)


def fold(ref, first, line):
    for i in range(line.shape[1] // DK):
        ref[first + i : first + i + 1, :] = line[:, i * DK : (i + 1) * DK]


def start_kernel(
    length_ref, x_ref, cot_ref, gain_ref, q_ref, k_ref, v_ref, g_ref, decay_ref, out_w_ref,
    gate_ref, up_ref, down_ref, qc_ref, kc_ref, vc_ref, log_ref, bias_ref,
    first_ref, full_ref, fed_ref, ffn_ref, alt_ref, conv_ref, dec_ref,
    own, pack, send, recv, local,
):
    place = tensor_places()
    data_place, core_mate = data_places()
    x = x_ref[...].astype(f32)
    own[...] = (x * rms_rows(x) * gain_ref[...]).astype(bf16)
    pack[:, :DK] = q_ref[...]
    pack[:, DK : 2 * DK] = k_ref[...]
    pack[:, 2 * DK : QKV] = v_ref[...]
    pack[:, QKV:GATE_END] = g_ref[...]
    decay = jnp.zeros((PRE - GATE_END - 2, pack.shape[0]), f32)
    decay = jnp.concatenate([decay_ref[...].astype(f32), decay], axis=0)
    pack[:, GATE_END:PRE] = jnp.transpose(decay).astype(bf16)
    pack[:, PRE:MIX] = out_w_ref[...]
    greet(tensor_near(place) + data_near(data_place, core_mate))
    moves = Moves(local)
    wires = Wires(send, recv)
    keep = [
        moves.plan(own, block(first_ref, place[ME], own.shape[0])),
        moves.plan(pack, block(full_ref, data_place[ME], pack.shape[0])),
    ]
    size = own.shape[0]
    half = size // SPLIT
    parts = [
        gather_tensor(wires, place, own, first_ref, i * half, half) for i in range(SPLIT)
    ] + [gather_data(wires, data_place, core_mate, pack, full_ref)]
    for stages in parts:
        stages[0]()
    start_all(keep)
    fed_ref[...] = (cot_ref[...].astype(f32) * live_rows(length_ref, 0, size, size)).astype(bf16)
    ff = gate_ref.shape[1]
    ffn_ref[:, :ff] = gate_ref[...]
    ffn_ref[:, ff : 2 * ff] = up_ref[...]
    ffn_ref[:, 2 * ff :] = down_ref[...]
    swap = wires.plan(ffn_ref, alt_ref, on_tensor(place[MATE]))
    swap.start()
    conv_ref[...] = jnp.zeros_like(conv_ref)
    conv_ref[0:4, :DK] = qc_ref[...]
    conv_ref[0:4, DK : 2 * DK] = kc_ref[...]
    conv_ref[0:4, 2 * DK :] = vc_ref[...]
    dec_ref[...] = jnp.zeros_like(dec_ref)
    dec_ref[0:1, :] = -jnp.exp(jnp.broadcast_to(log_ref[...], (1, DK)))
    dec_ref[1:2, :] = jnp.broadcast_to(bias_ref[...], (1, DK))
    together(*[stages[1:] for stages in parts])
    swap.wait_recv()
    wires.flush()
    for copy in keep:
        copy.wait()


def flow(wires, moves, place, part_ref, slots, own, out_ref, done, scatter, gather):
    size = own.shape[0]
    length = size // SPLIT
    mine = place[ME] if out_ref.shape[0] == TENSOR * size else place[X_ME]
    parts = []
    for i in range(SPLIT):
        sums = scatter(wires, moves, place, part_ref, slots, i * length, length, done)
        spread = gather(wires, place, own, out_ref, i * length, length)
        keep = moves.plan(
            own.at[pl.ds(i * length, length)], block(out_ref, mine, size, i * length, length)
        )

        def join(last=sums[-1], begin=spread[0], keep=keep):
            last()
            begin()
            keep.start()

        def finish(last=spread[-1], keep=keep):
            last()
            keep.wait()

        parts.append(sums[:-1] + [join] + spread[1:-1] + [finish])
    return parts


def middle_kernel(
    part_ref, x_ref, gain_ref, length_ref, alt_own, middle_ref, second_ref, alt_ref, slots, own,
    send, recv, local,
):
    place = tensor_places()
    data_place, core_mate = data_places()
    greet(tensor_near(place) + data_near(data_place, core_mate))
    wires, moves = Wires(send, recv), Moves(local)

    def done(start, length, mixed):
        rows = pl.ds(start, length)
        live = live_rows(length_ref, start, length, own.shape[0])
        middle = x_ref[rows, :].astype(f32) + live * mixed
        middle_ref[rows, :] = middle
        own[rows, :] = (middle * rms_rows(middle) * gain_ref[...]).astype(bf16)

    parts = flow(wires, moves, place, part_ref, slots, own, second_ref, done,
                 scatter_tensor, gather_ring)
    weights = gather_data(wires, data_place, core_mate, alt_own, alt_ref)
    keep = moves.plan(alt_own, block(alt_ref, data_place[ME], alt_own.shape[0]))

    def nothing():
        pass

    together(*parts, weights[:1] + [keep.start] + weights[1:-1] + [nothing, weights[-1]])
    keep.wait()
    wires.flush()


def turn_kernel(
    part_ref, middle_ref, cot_ref, gain_ref, length_ref, second_any, fed_any, acts_any,
    hidden_any, ffn_any, alt_acts_any, alt_hidden_any, alt_any,
    grad_ref, mixed_ref, gain_grad_ref, ffn_part_any, early_out,
    slots, own, gain_acc, second, fed, acts, hidden, ffn, alt_acts, alt_hidden, alt, ffn_part,
    wgrad, alt_wgrad, given, added, data_slots, alt_given, alt_added, alt_slots, alt_out,
    swap_own, swap_slot, send, recv, local,
):
    place = tensor_places()
    data_place, core_mate = data_places()
    greet(tensor_near(place) + data_near(data_place, core_mate))
    wires, moves = Wires(send, recv), Moves(local)
    gain_acc[...] = jnp.zeros_like(gain_acc)

    def done(start, length, second_in):
        rows = pl.ds(start, length)
        middle = middle_ref[rows, :]
        scale = rms_rows(middle)
        gain_acc[0:1, :] += jnp.sum(second_in * middle * scale, axis=0, keepdims=True)
        grad = cot_ref[rows, :].astype(f32) + rms_back(middle, scale, gain_ref[...], second_in)
        grad_ref[rows, :] = grad
        own[rows, :] = (live_rows(length_ref, start, length, own.shape[0]) * grad).astype(bf16)

    parts = flow(wires, moves, place, part_ref, slots, own, mixed_ref, done,
                 scatter_ring, gather_tensor)
    mine = scatter_data(
        wires, data_place, core_mate, wgrad, given, added, data_slots, early_out
    )
    other = scatter_data(
        wires, data_place, core_mate, alt_wgrad, alt_given, alt_added, alt_slots, alt_out
    )
    swap = wires.plan(swap_own, swap_slot, on_tensor(place[MATE]))
    loads = [
        moves.plan(source, target)
        for source, target in (
            (second_any, second), (alt_acts_any, alt_acts), (fed_any, fed),
            (alt_hidden_any, alt_hidden), (acts_any, acts), (hidden_any, hidden), (ffn_any, ffn),
            (alt_any, alt),
        )
    ]
    store = moves.plan(ffn_part, ffn_part_any)
    ff = hidden.shape[1]
    tile = 256

    def weight_work(target, acts_side, hidden_side, i):
        at = pl.ds(i * tile, tile)
        target[at, : 2 * ff] = mm(second[:, at], acts_side[...], 0, 0).astype(bf16)
        target[at, 2 * ff :] = mm(fed[:, at], hidden_side[...], 0, 0).astype(bf16)

    def everywhere(i):
        for stages in parts:
            stages[i]()

    everywhere(0)
    start_all(loads)
    for copy in loads[:4]:
        copy.wait()
    tiles = D // tile
    for i in range(tiles):
        weight_work(alt_wgrad, alt_acts, alt_hidden, i)
    other[0]()
    for copy in loads[4:6]:
        copy.wait()
    weight_work(wgrad, acts, hidden, 0)
    everywhere(1)
    other[1]()
    for i in range(1, tiles):
        weight_work(wgrad, acts, hidden, i)
    mine[0]()
    other[2]()
    parts[0][2]()
    mine[1]()
    parts[1][2]()
    mine[2]()
    for copy in loads[6:]:
        copy.wait()
    for i in range(ffn_part.shape[0] // tile):
        at = pl.ds(i * tile, tile)
        terms = mm(hidden[at, :], ffn[:, 2 * ff :], 1, 1)
        terms = terms + mm(alt_hidden[at, :], alt[:, 2 * ff :], 1, 1)
        ffn_part[at, :] = terms.astype(bf16)
    store.start()
    everywhere(3)
    everywhere(4)
    other[3]()
    everywhere(5)
    mine[3]()
    everywhere(6)
    other[4]()
    everywhere(7)
    mine[4]()
    other[5]()
    everywhere(8)
    other[6]()
    swap_own[...] = alt_out[...].astype(bf16)
    swap.start()
    mine[5]()
    mine[6]()
    everywhere(9)
    fold(gain_grad_ref, 0, gain_acc[0:1, :])
    swap.wait_recv()
    early_out[...] += swap_slot[...].astype(f32)
    wires.flush()
    store.wait()


def ffn_kernel(
    second_ref, fed_ref, ffn_ref, alt_ref, part_ref, acts_ref, hidden_ref, alt_acts_ref,
    alt_hidden_ref,
):
    ff = hidden_ref.shape[1]
    total = None
    for weights, acts_out, hidden_out in (
        (ffn_ref, acts_ref, hidden_ref), (alt_ref, alt_acts_ref, alt_hidden_ref),
    ):
        acts = mm(second_ref[...], weights[:, : 2 * ff])
        gate, up = acts[:, :ff], acts[:, ff:]
        hidden_grad = mm(fed_ref[...], weights[:, 2 * ff :])
        sig = jax.nn.sigmoid(gate)
        act = gate * sig
        hidden_out[...] = (act * up).astype(bf16)
        acts_out[:, :ff] = (hidden_grad * up * sig * (1.0 + gate * (1.0 - sig))).astype(bf16)
        acts_out[:, ff:] = (hidden_grad * act).astype(bf16)
        part = mm(acts_out[...], weights[:, : 2 * ff], 1, 1)
        total = part if total is None else total + part
    part_ref[...] = total.astype(bf16)


def end_kernel(
    part_ref, x_ref, grad_ref, gain_ref, ffn_gain_ref, small_ref, head_ref, first_any, pre_any, mixed_grad_any, mixed_any,
    input_ref, late_out, gains_out, head_out,
    slots, first, pre, mixed_grad, mixed, part, late, late_given, late_added, late_slots, gain_acc, gain_own, gain_slots, wide_own, wide_slots,
    head_slots, send, recv, local,
):
    place = tensor_places()
    data_place, core_mate = data_places()
    me, data_me = place[ME], data_place[ME]
    others = [lax.rem(me + i, TENSOR) for i in range(1, TENSOR)]
    data_others = [lax.rem(data_me + i, DATA) for i in range(1, DATA)]
    greet([on_tensor(i) for i in others] + [on_data(i) for i in data_others])
    wires, moves = Wires(send, recv), Moves(local)
    gain_acc[...] = jnp.zeros_like(gain_acc)
    length = x_ref.shape[0] // SPLIT

    def done(start, length, first_in):
        rows = pl.ds(start, length)
        x = x_ref[rows, :].astype(f32)
        scale = rms_rows(x)
        input_ref[rows, :] = grad_ref[rows, :] + rms_back(x, scale, gain_ref[...], first_in)

    flows = [
        scatter_tensor(wires, moves, place, part_ref, slots, i * length, length, done)
        for i in range(SPLIT)
    ]
    later = scatter_data(
        wires, data_place, core_mate, late, late_given, late_added, late_slots, late_out
    )
    heads = [
        wires.plan(head_ref, head_slots.at[i], on_data(to)) for i, to in enumerate(data_others)
    ]
    near = [
        wires.plan(gain_own, gain_slots.at[i], on_tensor(to)) for i, to in enumerate(others)
    ]
    wide_ones = [
        wires.plan(wide_own, wide_slots.at[i], on_data(to)) for i, to in enumerate(data_others)
    ]
    loads = [
        moves.plan(source, target)
        for source, target in (
            (pre_any, pre), (first_any, first), (mixed_any, mixed), (mixed_grad_any, mixed_grad),
            (part_ref, part),
        )
    ]

    def everywhere(i):
        for stages in flows:
            stages[i]()

    everywhere(0)
    start_all(loads)
    tile = 256

    def make_late(i):
        at = pl.ds(i * tile, tile)
        late[at, :PRE] = mm(first[:, at], pre[...], 0, 0).astype(bf16)
        late[at, PRE:] = mm(mixed_grad[:, at], mixed[...], 0, 0).astype(bf16)

    for copy in loads:
        copy.wait()
    make_late(0)
    make_late(1)
    everywhere(1)
    make_late(2)
    make_late(3)
    later[0]()
    start_all(heads)
    for i in range(first.shape[0] // 256):
        at = pl.ds(i * 256, 256)
        normed = first[at, :].astype(f32) * part[at, :].astype(f32)
        gain_acc[0:1, :] += jnp.sum(normed, axis=0, keepdims=True)
    gain_own[...] = jnp.zeros_like(gain_own)
    fold(gain_own, 0, gain_acc[0:1, :] / gain_ref[...])
    gain_own[8:16, :] = ffn_gain_ref[...]
    fold(gain_own, 16, small_ref[0:1, :])
    start_all(near)
    everywhere(2)
    later[1]()
    later[2]()
    await_all(near)
    total = gain_own[...]
    for i in range(TENSOR - 1):
        total = total + gain_slots[i]
    wide_own[...] = total
    start_all(wide_ones)
    everywhere(3)
    later[3]()
    await_all(heads)
    total = head_ref[...]
    for i in range(DATA - 1):
        total = total + head_slots[i]
    head_out[...] = total
    later[4]()
    await_all(wide_ones)
    total = wide_own[...]
    for i in range(DATA - 1):
        total = total + wide_slots[i]
    gains_out[...] = total
    later[5]()
    everywhere(4)
    later[6]()
    wires.flush()


END_COPIES = SCATTER_TENSOR * SPLIT + SCATTER_DATA + TENSOR - 1 + 2 * (DATA - 1)
GAINS = 24


def finish_kernel(
    output_ref, input_ref, early_ref, late_ref, gains_ref, head_ref,
    output, input_grad, mixer_gain, query, key, value, gate, decay, query_conv, key_conv,
    value_conv, decay_log, decay_bias, head_gain, out_weight, ffn_gain, ffn_gate, ffn_up,
    ffn_down,
):
    output[...] = output_ref[...]
    input_grad[...] = input_ref[...]
    mixer_gain[...] = gains_ref[0:8, :]
    ffn_gain[...] = gains_ref[8:16, :]
    head_gain[...] = gains_ref[16:18, :]
    query[...] = late_ref[:, :DK]
    key[...] = late_ref[:, DK : 2 * DK]
    value[...] = late_ref[:, 2 * DK : QKV]
    gate[...] = late_ref[:, QKV:GATE_END]
    decay[...] = jnp.transpose(late_ref[:, GATE_END:PRE])[0:2, :]
    out_weight[...] = late_ref[:, PRE:MIX]
    ff = ffn_gate.shape[1]
    ffn_gate[...] = early_ref[:, :ff]
    ffn_up[...] = early_ref[:, ff : 2 * ff]
    ffn_down[...] = early_ref[:, 2 * ff :]
    query_conv[...] = head_ref[0:4, :DK]
    key_conv[...] = head_ref[0:4, DK : 2 * DK]
    value_conv[...] = head_ref[0:4, 2 * DK :]
    decay_log[...] = head_ref[4:5, 0:1]
    decay_bias[...] = head_ref[5:6, 0:1]


V, H, S = "vmem", "any", "smem"
SPECS = {
    V: lambda: pl.BlockSpec(memory_space=pltpu.VMEM),
    H: lambda: pl.BlockSpec(memory_space=pl.ANY),
    S: lambda: pl.BlockSpec(memory_space=pltpu.SMEM),
}


def communicate(kernel, number, ins, outs, scratch, copies, moves, name):
    sems = [pltpu.SemaphoreType.DMA((count,)) for count in (copies, copies, moves)]
    return pl.pallas_call(
        kernel,
        out_shape=[jax.ShapeDtypeStruct(shape, kind) for shape, kind, _ in outs],
        in_specs=[SPECS[space]() for _, space in ins],
        out_specs=[SPECS[space]() for _, _, space in outs],
        scratch_shapes=[pltpu.VMEM(shape, kind) for shape, kind in scratch] + sems,
        compiler_params=pltpu.CompilerParams(
            collective_id=number, has_side_effects=True, vmem_limit_bytes=58 * 1024 * 1024
        ),
        name=name,
    )(*[item for item, _ in ins])


def call_ffn(second_rows, fed_rows, ffn_full, alt_full):
    rows = second_rows.shape[0]
    ff = ffn_full.shape[1] // 3
    step = 256
    tall = lambda width: pl.BlockSpec((step, width), lambda i: (i, 0))
    fixed = pl.BlockSpec(ffn_full.shape, lambda i: (0, 0))
    made = lambda width: jax.ShapeDtypeStruct((rows, width), bf16)
    return pl.pallas_call(
        ffn_kernel,
        grid=(rows // step,),
        in_specs=[tall(D), tall(D), fixed, fixed],
        out_specs=[tall(D), tall(2 * ff), tall(ff), tall(2 * ff), tall(ff)],
        out_shape=[made(D), made(2 * ff), made(ff), made(2 * ff), made(ff)],
        compiler_params=pltpu.CompilerParams(
            dimension_semantics=(ARBITRARY,), vmem_limit_bytes=58 * 1024 * 1024
        ),
        name=FFN,
    )(second_rows, fed_rows, ffn_full, alt_full)


def shards(
    block_input, out_cotangent, lengths, mixer_gain, query_weight, key_weight, value_weight,
    output_gate_weight, decay_weight, query_conv, key_conv, value_conv, decay_log, decay_bias,
    head_gain, out_weight, ffn_gain, ffn_gate, ffn_up, ffn_down,
):
    size = block_input.shape[0]
    rows = size * TENSOR
    depth = query_weight.shape[0]
    ff = ffn_gate.shape[1]
    line = lambda item: item.reshape(1, -1)
    vmem = lambda *items: [(item, V) for item in items]
    hbm = lambda *items: [(item, H) for item in items]
    length = [(lengths, S)]
    slots = ((SLOTS, size, D), bf16)
    own = ((size, D), bf16)
    first_rows, full, fed_own, ffn_own, alt_own, conv, dec = communicate(
        start_kernel, 1,
        length + vmem(
            block_input, out_cotangent, line(mixer_gain), query_weight, key_weight, value_weight,
            output_gate_weight, decay_weight.reshape(depth, 2).T, out_weight.T, ffn_gate, ffn_up,
            ffn_down.T, query_conv, key_conv, value_conv, line(decay_log), line(decay_bias),
        ),
        [((rows, D), bf16, H), ((D, MIX), bf16, H), ((size, D), bf16, V),
         ((depth, 3 * ff), bf16, V), ((depth, 3 * ff), bf16, V), ((8, QKV), f32, V),
         ((8, DK), f32, V)],
        [own, ((depth, MIX), bf16)], GATHER_TENSOR * SPLIT + GATHER_DATA + 1, 2, "start_gathers",
    )
    hg = line(head_gain)
    forward = call_forward(first_rows, full, conv, dec, hg, fed_own, ffn_own)
    proj, mixed_part, mixed_rows, o, t, u, qe, a, s, tails, fed_rows, ffn_full = forward
    middle, second_rows, alt_full = communicate(
        middle_kernel, 2,
        hbm(mixed_part) + vmem(block_input, line(ffn_gain)) + length + hbm(alt_own),
        [((size, D), f32, V), ((rows // 2, D), bf16, H), ((D, 3 * ff), bf16, H)],
        [slots, own], (GATHER_RING + SCATTER_TENSOR) * SPLIT + GATHER_DATA,
        (len(HELD) + 1) * SPLIT + 1, "middle_sums",
    )
    second_part, acts, hidden, alt_acts, alt_hidden = call_ffn(
        second_rows, fed_rows, ffn_full, alt_full
    )
    block_rows = D // DATA
    half_rows = rows // 2
    early_block, late_block = ((8, block_rows, 3 * ff), bf16), ((8, block_rows, MIX), bf16)
    early_row, early_all = (block_rows, 3 * ff), ((D, 3 * ff), bf16)
    middle_grad, mixed_grad, ffn_gain_grad, ffn_part, early = communicate(
        turn_kernel, 3,
        hbm(second_part) + vmem(middle, out_cotangent, line(ffn_gain)) + length
        + hbm(second_rows, fed_rows, acts, hidden, ffn_full, alt_acts, alt_hidden, alt_full),
        [((size, D), f32, V), ((rows, D), bf16, H), ((8, DK), f32, V),
         ((half_rows, D), bf16, H), (early_row, f32, V)],
        [((RING_SLOTS, size, D), bf16), own, ((8, D), f32)] + [((half_rows, D), bf16)] * 2
        + [((half_rows, 2 * ff), bf16), ((half_rows, ff), bf16), early_all] * 2
        + [((half_rows, D), bf16), early_all, early_all] + [early_block] * 6
        + [(early_row, f32), (early_row, bf16), (early_row, bf16)],
        (GATHER_TENSOR + SCATTER_RING) * SPLIT + 2 * SCATTER_DATA + 1, 4 * SPLIT + 9,
        "turn_sums",
    )
    pre_grads, first_part, head_grads, small, block_output = call_backward(
        mixed_grad, full, (proj, o, t, u, qe, a, s, tails), conv, dec, hg, ffn_part, middle,
        lengths,
    )
    input_grad, late, gains, heads = communicate(
        end_kernel, 4,
        hbm(first_part)
        + vmem(block_input, middle_grad, line(mixer_gain), ffn_gain_grad, small, head_grads)
        + hbm(first_rows, pre_grads, mixed_grad, mixed_rows),
        [((size, D), f32, V), ((block_rows, MIX), f32, V), ((GAINS, DK), f32, V),
         ((8, QKV), f32, V)],
        [slots, ((rows, D), bf16), ((rows, PRE), bf16), ((rows, D), bf16), ((rows, DV), bf16),
         ((rows, D), bf16), ((D, MIX), bf16)] + [late_block] * 3
        + [((8, D), f32), ((GAINS, DK), f32), ((TENSOR - 1, GAINS, DK), f32),
           ((GAINS, DK), f32), ((DATA - 1, GAINS, DK), f32), ((DATA - 1, 8, QKV), f32)],
        END_COPIES, len(HELD) * SPLIT + 5, "end_sums",
    )
    made = lambda *shape: jax.ShapeDtypeStruct(shape, f32)
    whole = lambda count: [pl.BlockSpec(memory_space=pltpu.VMEM)] * count
    outs = pl.pallas_call(
        finish_kernel,
        in_specs=whole(6),
        out_specs=whole(19),
        out_shape=[
            jax.ShapeDtypeStruct((size, D), bf16), made(size, D), made(8, DK), made(depth, DK),
            made(depth, DK), made(depth, DV), made(depth, DV), made(2, depth), made(4, DK),
            made(4, DK), made(4, DV), made(1, 1), made(1, 1), made(2, DK), made(depth, DV),
            made(8, DK), made(depth, ff), made(depth, ff), made(depth, ff),
        ],
        compiler_params=pltpu.CompilerParams(vmem_limit_bytes=58 * 1024 * 1024),
        name="finish",
    )(block_output, input_grad, early, late, gains, heads)
    outs = [item.T if i in (7, 14, 18) else item for i, item in enumerate(outs)]
    shapes = {2: (D,), 7: (depth, 1, 2), 11: (1,), 12: (1,), 13: (DV,), 15: (D,)}
    return tuple(
        item.reshape(shapes[i]) if i in shapes else item for i, item in enumerate(outs)
    )


def solution(mesh):
    rows = P((DP, AT_TENSOR), None)
    tile = P(DP, AT_TENSOR)
    taps = P(None, AT_TENSOR)
    turned = P(AT_TENSOR, DP)
    decay = P(DP, AT_TENSOR, None)
    head = P(AT_TENSOR)
    return jax.shard_map(
        shards,
        mesh=mesh,
        in_specs=(
            rows, rows, P(DP), P(), tile, tile, tile, tile, decay, taps, taps, taps, head, head,
            P(), turned, P(), tile, tile, turned,
        ),
        out_specs=(
            rows, rows, P(), tile, tile, tile, tile, decay, taps, taps, taps, head, head,
            P(), turned, P(), tile, tile, turned,
        ),
        check_vma=False,
    )
```

```python
import functools

import jax
import jax.numpy as jnp
from jax import lax
from jax.experimental import pallas as pl
from jax.experimental.pallas import tpu as pltpu
from jax.sharding import PartitionSpec as P

DK = 128
DV = 256
QKV = 2 * DK + DV
D = 1024
GATE_END = 768
PRE = 896
MIX = 1152
TENSOR = 8
RING = 4
DATA = 16
CHUNK = 256
BATCH = 2
SPLIT = 2

FED = "fed"
FFN = "ffn"
TOP = "top"
MIDDLE = "middle"
X_ME = "x_me"
ME = "me"
ARBITRARY = "arbitrary"
AT_TENSOR = "tensor"
DP = "dp"
RIGHT = "right"
FAR = "far"
LEFT = "left"
MATE = "mate"
MATE_RIGHT = "mate_right"
MATE_FAR = "mate_far"
MATE_LEFT = "mate_left"
OVER_FAR = "over_far"
UP = "up"
OVER_UP = "over_up"
DOWN = "down"
OVER_DOWN = "over_down"
OVER = "over"
OVER_STEM = "over_"
X_STEM = "x_"

norm_eps = 1e-06
gate_eps = 1e-05
bf16 = jnp.bfloat16
f32 = jnp.float32


def mm(left_side, right_side, left_dim=1, right_dim=0):
    return lax.dot_general(
        left_side.astype(bf16),
        right_side.astype(bf16),
        (((left_dim,), (right_dim,)), ((), ())),
        preferred_element_type=f32,
    )


def halves(values):
    high = values.astype(bf16)
    return high, (values - high.astype(f32)).astype(bf16)


def mm3(left_pair, right_pair, left_dim=1, right_dim=0):
    (lh, ll), (rh, rl) = left_pair, right_pair
    return (
        mm(lh, rh, left_dim, right_dim)
        + mm(lh, rl, left_dim, right_dim)
        + mm(ll, rh, left_dim, right_dim)
    )


def ones_mm(ones_side, values, terms):
    total = None
    for _ in range(terms):
        high = values.astype(bf16)
        part = mm(ones_side, high)
        total = part if total is None else total + part
        values = values - high.astype(f32)
    return total


def wide(lanes):
    return jnp.concatenate([lanes, lanes], axis=1)


def row_total(values):
    return jnp.sum(values, axis=-1, keepdims=True)


def softplus(z):
    return jnp.maximum(z, 0.0) + jnp.log1p(jnp.exp(-jnp.abs(z)))


def index_pair():
    return (
        lax.broadcasted_iota(jnp.int32, (CHUNK, CHUNK), 0),
        lax.broadcasted_iota(jnp.int32, (CHUNK, CHUNK), 1),
    )


def taps_sum(conv_ref, pad_ref, start):
    total = None
    for tap in range(4):
        term = conv_ref[tap : tap + 1, :] * pad_ref[pl.ds(start + 5 + tap, CHUNK), :]
        total = term if total is None else total + term
    return total


def gates(proj_ref, rows, dec_ref):
    both = proj_ref[rows, GATE_END:PRE]
    z = jnp.broadcast_to(both[:, 0:1], (CHUNK, DK)) + dec_ref[1:2, :]
    rate = jax.nn.sigmoid(jnp.broadcast_to(both[:, 1:2], (CHUNK, DK)))
    return z, dec_ref[0:1, :] * softplus(z), rate


def cumulative(decays, causal_ones):
    total = ones_mm(causal_ones, decays, 3)
    across = jnp.transpose(total)[0:1, :]
    return total, across


def ratios(total, across, causal):
    spread = wide(total) - across
    return jnp.where(causal, jnp.exp(jnp.where(causal, spread, 0.0)), 0.0)


KINDS = (FED, FFN)
FORWARD_PLAN = {
    (0, TOP): ((FFN, 0), (FED, 0)),
    (0, MIDDLE): ((FFN, 1), (FFN, 2), (FFN, 3)),
    (1, MIDDLE): ((FED, 1), (FED, 2), (FFN, 4), (FFN, 5)),
    (2, TOP): ((FFN, 6),),
}


def mix_forward(
    first_ref, pack_ref, conv_ref, dec_ref, hg_ref, fed_own, ffn_own,
    proj_ref, part_ref, mixed_ref, o_ref, t_ref, u_ref, qe_ref, a_ref, s_ref, tail_ref,
    fed_ref, ffn_ref,
    state, pad, send, recv, local,
):
    step = pl.program_id(0)
    last_step = pl.num_programs(0) - 1
    place = tensor_places()
    data_place, core_mate = data_places()
    wires = {
        FED: Wires(send, recv),
        FFN: Wires(send, recv, GATHER_RING),
    }
    moves = Moves(local)
    keep = [
        moves.plan(fed_own, block(fed_ref, place[X_ME], fed_own.shape[0])),
        moves.plan(ffn_own, block(ffn_ref, data_place[ME], ffn_own.shape[0])),
    ]
    stages = {
        FED: gather_ring(wires[FED], place, fed_own, fed_ref, 0, fed_own.shape[0]),
        FFN: gather_data(wires[FFN], data_place, core_mate, ffn_own, ffn_ref),
    }

    def advance(point):
        for at in range(3):
            todo = [stages[kind][i] for kind, i in FORWARD_PLAN.get((at, point), ())]
            if todo:

                @pl.when(step == at)
                def _():
                    for stage in todo:
                        stage()

    @pl.when(step == 0)
    def _():
        greet(ring_near(place) + data_near(data_place, core_mate))
        start_all(keep)
        state[...] = jnp.zeros_like(state)
        pad[0:8, :] = jnp.zeros((8, QKV), f32)

    advance(TOP)
    row, col = index_pair()
    causal = row >= col
    strict = row > col
    causal_ones = causal.astype(bf16)
    parts = range(BATCH)
    rows = [pl.ds(c * CHUNK, CHUNK) for c in parts]
    for c in parts:
        pre = mm(first_ref[rows[c], :], pack_ref[:, :PRE])
        proj_ref[rows[c], :] = pre
        pad[pl.ds(8 + c * CHUNK, CHUNK), :] = pre[:, :QKV]
    items = []
    for c in parts:
        tail_ref[c] = pad[pl.ds(c * CHUNK, 8), :]
        act = jax.nn.silu(taps_sum(conv_ref, pad, c * CHUNK))
        q, k, v = act[:, :DK], act[:, DK : 2 * DK], act[:, 2 * DK :]
        q = q * (lax.rsqrt(row_total(q * q) + norm_eps) * DK ** (-0.5))
        k = k * lax.rsqrt(row_total(k * k) + norm_eps)
        _, decays, rate = gates(proj_ref, rows[c], dec_ref)
        total, across = cumulative(decays, causal_ones)
        ratio = ratios(total, across, causal)
        k_pair = halves(k)
        kk = mm3(k_pair, k_pair, 1, 1)
        lower = jnp.where(strict, wide(rate) * kk * ratio, 0.0)
        scores = halves(mm3(halves(q), k_pair, 1, 1) * ratio)
        growth = jnp.exp(total)
        last = total[CHUNK - 1 : CHUNK, :]
        tail_k = halves(jnp.exp(last - total) * k)
        items.append((q, k, v, rate, growth, jnp.exp(last), tail_k, scores, lower))
    pad[0:8, :] = pad[pl.ds(BATCH * CHUNK, 8), :]
    size = 1
    inverse = [(row == col).astype(f32) for c in parts]
    while size < CHUNK:
        same = (row // (2 * size) == col // (2 * size)) & ((row // size) % 2 == 1) & ((col // size) % 2 == 0)
        for c in parts:
            edge = jnp.where(same, items[c][8], 0.0)
            if size == 1:
                inverse[c] = inverse[c] - edge
            else:
                pair = halves(inverse[c])
                inverse[c] = inverse[c] - mm3(halves(mm3(pair, halves(edge))), pair)
        size *= 2
    advance(MIDDLE)
    eye = lax.broadcasted_iota(jnp.int32, (DK, DK), 0) == lax.broadcasted_iota(
        jnp.int32, (DK, DK), 1
    )
    later = []
    for c in parts:
        q, k, v, rate, growth, grown, tail_k, scores, _ = items[c]
        t_ref[c] = inverse[c]
        solve = halves(inverse[c])
        w = halves(mm3(solve, halves(rate * growth * k)))
        u_start = mm3(solve, halves(wide(rate) * v))
        u_pair = halves(u_start)
        q_eff = growth * q - mm3(scores, w)
        carry = jnp.where(eye, grown, 0.0) - mm3(w, tail_k, 0, 0)
        added = mm3(u_pair, tail_k, 0, 0)
        qe_ref[c] = q_eff
        a_ref[c] = carry
        later.append((w, u_start, u_pair, halves(q_eff), scores, halves(carry), added))
    memory = state[...]
    starts = []
    for c in parts:
        s_ref[c] = memory
        starts.append(halves(memory))
        memory = mm3(starts[c], later[c][5]) + later[c][6]
    state[...] = memory
    for c in parts:
        w, u_start, u_pair, q_eff, scores, _, _ = later[c]
        u_ref[c] = u_start - mm3(w, starts[c], 1, 1)
        o = mm3(q_eff, starts[c], 1, 1) + mm3(scores, u_pair)
        o_ref[rows[c], :] = o
        normed = o * lax.rsqrt(row_total(o * o) * (1.0 / DV) + gate_eps) * hg_ref[...]
        mixed = (normed * jax.nn.silu(proj_ref[rows[c], QKV:GATE_END])).astype(bf16)
        mixed_ref[rows[c], :] = mixed
        part_ref[rows[c], :] = mm(mixed, pack_ref[:, PRE:MIX], 1, 1).astype(bf16)

    @pl.when(step == last_step)
    def _():
        for kind in KINDS:
            stages[kind][-1]()
            wires[kind].flush()
        for copy in keep:
            copy.wait()


def mix_backward(
    grad_ref, pack_ref, proj_ref, tail_ref, o_ref, t_ref, u_ref, qe_ref, a_ref, s_ref,
    conv_ref, dec_ref, hg_ref, ffn_part, middle_ref, length_ref,
    pre_ref, first_ref, head_ref, small_ref, output_ref,
    dstate, padp, padg, slots, send, recv, local,
):
    step = pl.program_id(0)
    last_step = pl.num_programs(0) - 1
    place = tensor_places()
    wires, moves = Wires(send, recv), Moves(local)
    size = middle_ref.shape[0]

    def done(start, length, terms):
        live = live_rows(length_ref, start, length, size)
        output_ref[...] = (middle_ref[...] + live * terms).astype(bf16)

    ffn = scatter_ring(wires, moves, place, ffn_part, slots, 0, size, done)

    @pl.when(step == 0)
    def _():
        greet(ring_near(place))
        ffn[0]()
        dstate[...] = jnp.zeros_like(dstate)
        padg[pl.ds(BATCH * CHUNK, 8), :] = jnp.zeros((8, QKV), f32)
        head_ref[...] = jnp.zeros_like(head_ref)
        small_ref[...] = jnp.zeros_like(small_ref)

    row, col = index_pair()
    causal = row >= col
    strict = row > col
    causal_ones = causal.astype(bf16)
    strict_ones = strict.astype(bf16)
    upper_ones = (col >= row).astype(bf16)
    lane = lax.broadcasted_iota(jnp.int32, (CHUNK, DK), 1)
    parts = range(BATCH)
    rows = [pl.ds(c * CHUNK, CHUNK) for c in parts]
    padp[0:8, :] = tail_ref[0]
    for c in parts:
        padp[pl.ds(8 + c * CHUNK, CHUNK), :] = proj_ref[rows[c], :QKV]
    items = []
    for c in parts:
        act_pre = taps_sum(conv_ref, padp, c * CHUNK)
        act_sig = jax.nn.sigmoid(act_pre)
        act = act_pre * act_sig
        slope = act_sig * (1.0 + act_pre * (1.0 - act_sig))
        qc, kc, v = act[:, :DK], act[:, DK : 2 * DK], act[:, 2 * DK :]
        q_scale = lax.rsqrt(row_total(qc * qc) + norm_eps)
        k_scale = lax.rsqrt(row_total(kc * kc) + norm_eps)
        q = qc * (q_scale * DK ** (-0.5))
        k = kc * k_scale
        z, decays, rate = gates(proj_ref, rows[c], dec_ref)
        total, across = cumulative(decays, causal_ones)
        ratio = ratios(total, across, causal)
        k_pair = halves(k)
        key_ratio = mm3(k_pair, k_pair, 1, 1) * ratio
        scores = mm3(halves(q), k_pair, 1, 1) * ratio
        growth = jnp.exp(total)
        last = total[CHUNK - 1 : CHUNK, :]
        tail = jnp.exp(last - total)
        grad = mm(grad_ref[rows[c], :], pack_ref[:, PRE:MIX])
        gate = proj_ref[rows[c], QKV:GATE_END]
        gate_sig = jax.nn.sigmoid(gate)
        gate_act = gate * gate_sig
        o = o_ref[rows[c], :]
        o_scale = lax.rsqrt(row_total(o * o) * (1.0 / DV) + gate_eps)
        normed = o * o_scale
        gain = hg_ref[...]
        gate_grad = grad * normed * gain * gate_sig * (1.0 + gate * (1.0 - gate_sig))
        pre_ref[rows[c], QKV:GATE_END] = gate_grad.astype(bf16)
        grad = grad * gate_act
        small_ref[0:1, :] += jnp.sum(grad * normed, axis=0, keepdims=True)
        grad = grad * gain
        do = o_scale * (grad - normed * (row_total(grad * normed) * (1.0 / DV)))
        do = halves(do)
        items.append(
            (slope, q, k, v, q_scale, k_scale, z, decays, rate, ratio, key_ratio, scores,
             growth, jnp.exp(last), tail, do)
        )

    @pl.when(step == 1)
    def _():
        ffn[1]()

    ends = [None] * BATCH
    change = dstate[...]
    for c in reversed(parts):
        ends[c] = change
        change = mm3(halves(change), halves(a_ref[c]), 1, 1) + mm3(
            items[c][15], halves(qe_ref[c]), 0, 0
        )
    dstate[...] = change
    for c in reversed(parts):
        (slope, q, k, v, q_scale, k_scale, z, decays, rate, ratio, key_ratio, scores,
         growth, grown, tail, do) = items[c]
        start = s_ref[c]
        end = ends[c]
        start_pair, end_pair = halves(start), halves(end)
        u = halves(u_ref[c])
        k_pair = halves(k)
        q16, k16 = q.astype(bf16), k_pair[0]
        du = mm3(halves(scores), do, 0, 0) + mm3(halves(tail * k), end_pair, 1, 1)
        dx = mm3(halves(t_ref[c]), halves(du), 0, 0)
        dx_pair = halves(dx)
        d_scores = jnp.where(causal, mm3(do, u, 1, 1), 0.0)
        d_lower = jnp.where(strict, -mm3(dx_pair, u, 1, 1), 0.0)
        score_side = (d_scores * ratio).astype(bf16)
        rate2 = wide(rate)
        growth2 = wide(growth)
        lower_keys = d_lower * key_ratio
        key_side = (d_lower * rate2 * ratio).astype(bf16)
        do_state = mm3(do, start_pair)
        dx_state = mm3(dx_pair, start_pair)
        u_state = mm3(u, end_pair)
        key_state = mm3(k_pair, start_pair, 1, 1)
        dq = growth * do_state + mm(score_side, k16)
        rate_growth = rate * growth
        dk = (
            mm(score_side, q16, 0, 0)
            + mm(key_side, k16)
            + mm(key_side, k16, 0, 0)
            - rate_growth * dx_state
            + tail * u_state
        )
        dv = rate2 * dx
        d_rate = row_total(lower_keys) + row_total(dx * (v - growth2 * key_state))
        from_growth = row_total(growth * q * do_state - rate_growth * k * dx_state)
        from_tail = row_total(tail * k * u_state)
        pairs = d_scores * scores + rate2 * lower_keys
        held = ones_mm(upper_ones, pairs, 2)
        spread_growth = ones_mm(upper_ones, jnp.broadcast_to(from_growth, (CHUNK, DK)), 2)
        spread_tail = ones_mm(strict_ones, jnp.broadcast_to(from_tail, (CHUNK, DK)), 2)
        through = jnp.sum(row_total(end * start), axis=0, keepdims=True)
        d_decay = (
            row_total(jnp.where(strict, held, 0.0))
            + spread_growth
            + spread_tail
            + grown * through
        )
        dz = d_decay * dec_ref[0:1, :] * jax.nn.sigmoid(z)
        d_write = d_rate * rate * (1.0 - rate)
        pre_ref[rows[c], GATE_END:PRE] = jnp.where(
            lane == 0, dz, jnp.where(lane == 1, d_write, 0.0)
        ).astype(bf16)
        head_ref[4:5, :DK] += jnp.sum(d_decay * decays, axis=0, keepdims=True)
        head_ref[5:6, :DK] += jnp.sum(dz, axis=0, keepdims=True)
        dqc = q_scale * (DK ** (-0.5) * dq - q * (row_total(q * dq) * DK**0.5))
        dkc = k_scale * (dk - k * row_total(k * dk))
        dact = jnp.concatenate([dqc, dkc, dv], axis=1) * slope
        padg[pl.ds(c * CHUNK, CHUNK), :] = dact
        dpre = None
        for tap in range(4):
            weight = conv_ref[tap : tap + 1, :]
            term = weight * padg[pl.ds(c * CHUNK + 3 - tap, CHUNK), :]
            dpre = term if dpre is None else dpre + term
            head_ref[tap : tap + 1, :] += jnp.sum(
                dact * padp[pl.ds(c * CHUNK + 5 + tap, CHUNK), :], axis=0, keepdims=True
            )
        pre_ref[rows[c], :QKV] = dpre.astype(bf16)
        first_ref[rows[c], :] = mm(pre_ref[rows[c], :], pack_ref[:, :PRE], 1, 1).astype(bf16)
    padg[pl.ds(BATCH * CHUNK, 8), :] = padg[0:8, :]

    @pl.when(step == last_step)
    def _():
        ffn[2]()
        wires.flush()


def call_forward(first_rows, pack, conv, dec, hg, fed_own, ffn_own):
    rows = first_rows.shape[0]
    chunks = rows // CHUNK
    steps = chunks // BATCH
    anywhere = pl.BlockSpec(memory_space=pl.ANY)
    tall = lambda width: pl.BlockSpec((BATCH * CHUNK, width), lambda i: (i, 0))
    fixed = lambda shape: pl.BlockSpec(shape, lambda i: (0, 0))
    per = lambda *shape: pl.BlockSpec((BATCH,) + shape, lambda i: (i, 0, 0))
    made = jax.ShapeDtypeStruct
    return pl.pallas_call(
        mix_forward,
        grid=(steps,),
        in_specs=[
            tall(D), fixed((D, MIX)), fixed((8, QKV)), fixed((8, DK)), fixed((1, DV)),
            anywhere, anywhere,
        ],
        out_specs=[
            tall(PRE), tall(D), tall(DV), tall(DV), per(CHUNK, CHUNK), per(CHUNK, DV),
            per(CHUNK, DK), per(DK, DK), per(DV, DK), per(8, QKV),
            anywhere, anywhere,
        ],
        out_shape=[
            made((rows, PRE), f32), made((rows, D), bf16), made((rows, DV), bf16),
            made((rows, DV), f32), made((chunks, CHUNK, CHUNK), f32),
            made((chunks, CHUNK, DV), f32),
            made((chunks, CHUNK, DK), f32), made((chunks, DK, DK), f32),
            made((chunks, DV, DK), f32), made((chunks, 8, QKV), f32),
            made((rows // 2, D), bf16), made((D, ffn_own.shape[1]), bf16),
        ],
        scratch_shapes=[
            pltpu.VMEM((DV, DK), f32), pltpu.VMEM((BATCH * CHUNK + 8, QKV), f32),
            pltpu.SemaphoreType.DMA((GATHER_RING + GATHER_DATA,)),
            pltpu.SemaphoreType.DMA((GATHER_RING + GATHER_DATA,)),
            pltpu.SemaphoreType.DMA((2,)),
        ],
        compiler_params=pltpu.CompilerParams(
            dimension_semantics=(ARBITRARY,), vmem_limit_bytes=58 * 1024 * 1024,
            collective_id=5, has_side_effects=True,
        ),
        cost_estimate=pl.CostEstimate(
            flops=30_000_000_000, bytes_accessed=20_000_000, transcendentals=4_000_000
        ),
        name="mix_forward",
    )(first_rows, pack, conv, dec, hg, fed_own, ffn_own)


def call_backward(grad_rows, pack, saved, conv, dec, hg, ffn_part, middle, lengths):
    proj, o, t, u, qe, a, s, tails = saved
    rows = grad_rows.shape[0]
    chunks = rows // CHUNK
    steps = chunks // BATCH
    anywhere = pl.BlockSpec(memory_space=pl.ANY)
    tall = lambda width: pl.BlockSpec((BATCH * CHUNK, width), lambda i: (steps - 1 - i, 0))
    fixed = lambda shape: pl.BlockSpec(shape, lambda i: (0, 0))
    per = lambda *shape: pl.BlockSpec((BATCH,) + shape, lambda i: (steps - 1 - i, 0, 0))
    made = jax.ShapeDtypeStruct
    return pl.pallas_call(
        mix_backward,
        grid=(steps,),
        in_specs=[
            tall(D), fixed((D, MIX)), tall(PRE), per(8, QKV), tall(DV), per(CHUNK, CHUNK),
            per(CHUNK, DV), per(CHUNK, DK), per(DK, DK), per(DV, DK),
            fixed((8, QKV)), fixed((8, DK)), fixed((1, DV)), anywhere, fixed(middle.shape),
            pl.BlockSpec(memory_space=pltpu.SMEM),
        ],
        out_specs=[tall(PRE), tall(D), fixed((8, QKV)), fixed((8, DV)), fixed(middle.shape)],
        out_shape=[
            made((rows, PRE), bf16), made((rows, D), bf16), made((8, QKV), f32),
            made((8, DV), f32), made(middle.shape, bf16),
        ],
        scratch_shapes=[
            pltpu.VMEM((DV, DK), f32), pltpu.VMEM((BATCH * CHUNK + 8, QKV), f32),
            pltpu.VMEM((BATCH * CHUNK + 8, QKV), f32),
            pltpu.VMEM((RING_SLOTS,) + middle.shape, bf16),
            pltpu.SemaphoreType.DMA((SCATTER_RING,)),
            pltpu.SemaphoreType.DMA((SCATTER_RING,)),
            pltpu.SemaphoreType.DMA((len(HELD),)),
        ],
        compiler_params=pltpu.CompilerParams(
            dimension_semantics=(ARBITRARY,), vmem_limit_bytes=58 * 1024 * 1024,
            collective_id=6, has_side_effects=True,
        ),
        cost_estimate=pl.CostEstimate(
            flops=60_000_000_000, bytes_accessed=20_000_000, transcendentals=4_000_000
        ),
        name="mix_backward",
    )(
        grad_rows, pack, proj, tails, o, t, u, qe, a, s, conv, dec, hg, ffn_part, middle,
        lengths,
    )


class Wires:
    def __init__(self, send, recv, base=0):
        self.send, self.recv, self.copies, self.base = send, recv, [], base

    def plan(self, source, target, device):
        k = self.base + len(self.copies)
        copy = pltpu.make_async_remote_copy(
            src_ref=source,
            dst_ref=target,
            send_sem=self.send.at[k],
            recv_sem=self.recv.at[k],
            device_id=device,
            device_id_type=pl.DeviceIdType.MESH,
        )
        self.copies.append(copy)
        return copy

    def flush(self):
        for copy in self.copies:
            copy.wait_send()


class Moves:
    def __init__(self, sems):
        self.sems, self.copies = sems, []

    def plan(self, source, target):
        copy = pltpu.make_async_copy(source, target, self.sems.at[len(self.copies)])
        self.copies.append(copy)
        return copy


def on_tensor(index):
    return {AT_TENSOR: index}


def on_data(index):
    return {DP: index}


def tensor_places():
    me = lax.axis_index(AT_TENSOR)
    x, y = me % 4, me // 4
    at = lambda side, step: side * 4 + (x + step) % 4
    return {
        ME: at(y, 0), RIGHT: at(y, 1), FAR: at(y, 2), LEFT: at(y, 3),
        MATE: at(1 - y, 0), MATE_RIGHT: at(1 - y, 1), MATE_FAR: at(1 - y, 2),
        MATE_LEFT: at(1 - y, 3),
        X_ME: x, "x_right": (x + 1) % 4, "x_far": (x + 2) % 4, "x_left": (x + 3) % 4,
    }


NAMES = (FAR, OVER_FAR, UP, OVER_UP, DOWN, OVER_DOWN, ME, OVER)
Z_STEP = {FAR: 2, UP: 1, DOWN: 3, ME: 0}


def data_places():
    me = lax.axis_index(DP)
    core, z, y = me % 2, (me // 2) % 4, me // 8
    here, core_mate = {}, {}
    for name in NAMES:
        side = 1 - y if name.startswith(OVER) else y
        step = Z_STEP.get(name.replace(OVER_STEM, "").replace(OVER, ME))
        base = (side * 4 + (z + step) % 4) * 2
        here[name], core_mate[name] = base + core, base + 1 - core
    return here, core_mate


def greet(devices):
    barrier = pltpu.get_barrier_semaphore()
    for device in devices:
        pl.semaphore_signal(
            barrier, inc=1, device_id=device, device_id_type=pl.DeviceIdType.MESH
        )
    pl.semaphore_wait(barrier, len(devices))


def tensor_near(place):
    return [on_tensor(place[to]) for to in (RIGHT, LEFT, MATE)]


def ring_near(place):
    return [on_tensor(place[to]) for to in (RIGHT, LEFT)]


def data_near(place, core_mate):
    return [on_data(place[to]) for to in (OVER, UP, DOWN)] + [on_data(core_mate[ME])]


def together(*lists):
    for i in range(max(len(stages) for stages in lists)):
        for stages in lists:
            if i < len(stages):
                stages[i]()


def block(ref, index, size, start=0, length=None):
    return ref.at[pl.ds(pl.multiple_of(index * size + start, 16), length or size)]


def start_all(copies):
    for copy in copies:
        copy.start()


def await_all(copies):
    for copy in copies:
        copy.wait_recv()


def gather_tensor(wires, place, own, out, start, length):
    size = out.shape[0] // TENSOR
    half = length // 2
    at = lambda who, part: block(out, place[who], size, start + part * half, half)
    send = lambda who, part, to: wires.plan(at(who, part), at(who, part), on_tensor(place[to]))
    first = {
        (to, part): wires.plan(
            own.at[pl.ds(start + part * half, half)], at(ME, part), on_tensor(place[to])
        )
        for part in (0, 1)
        for to in (MATE, RIGHT, LEFT)
    }
    far_low, far_high = send(RIGHT, 0, LEFT), send(LEFT, 1, RIGHT)
    second = [[send(MATE, part, RIGHT), send(MATE, part, LEFT)] for part in (0, 1)]
    last = [send(FAR, part, MATE) for part in (0, 1)]

    def begin():
        start_all(first.values())

    def low():
        first[LEFT, 0].wait_recv()
        far_low.start()

    def mate_low():
        first[MATE, 0].wait_recv()
        start_all(second[0])

    def high():
        first[RIGHT, 0].wait_recv()
        first[RIGHT, 1].wait_recv()
        far_high.start()

    def last_low():
        far_low.wait_recv()
        last[0].start()

    def mate_high():
        first[LEFT, 1].wait_recv()
        first[MATE, 1].wait_recv()
        start_all(second[1])

    def last_high():
        far_high.wait_recv()
        last[1].start()

    def finish():
        await_all(second[0] + second[1] + last)

    return [begin, low, mate_low, high, last_low, mate_high, last_high, finish]


GATHER_TENSOR = 14


def gather_ring(wires, place, own, out, start, length):
    size = out.shape[0] // RING
    half = length // 2
    at = lambda who, part: block(out, place[X_STEM + who], size, start + part * half, half)
    send = lambda who, part, to: wires.plan(at(who, part), at(who, part), on_tensor(place[to]))
    first = {
        (to, part): wires.plan(
            own.at[pl.ds(start + part * half, half)], at(ME, part), on_tensor(place[to])
        )
        for to, part in ((LEFT, 0), (RIGHT, 1), (LEFT, 1), (RIGHT, 0))
    }
    far_low, far_high = send(RIGHT, 0, LEFT), send(LEFT, 1, RIGHT)

    def begin():
        start_all(first.values())

    def low():
        first[LEFT, 0].wait_recv()
        far_low.start()

    def high():
        first[RIGHT, 1].wait_recv()
        far_high.start()

    def finish():
        await_all([first[LEFT, 1], first[RIGHT, 0], far_low, far_high])

    return [begin, low, high, finish]


GATHER_RING = 6


def gather_data(wires, place, core_mate, own, out):
    size = own.shape[0]
    half = size // 2
    at = lambda who: block(out, place[who], size)
    part = lambda who, i: block(out, place[who], size, i * half, half)
    send = lambda ref, to: wires.plan(ref, ref, on_data(place[to]))
    share = lambda ref: wires.plan(ref, ref, on_data(core_mate[ME]))
    first = {to: wires.plan(own, at(ME), on_data(place[to])) for to in (OVER, UP, DOWN)}
    own_share = wires.plan(own, at(ME), on_data(core_mate[ME]))
    far_high, far_low = send(part(DOWN, 1), UP), send(part(UP, 0), DOWN)
    second = {to: send(at(OVER), to) for to in (UP, DOWN)}
    over_high, over_low = send(part(OVER_DOWN, 1), UP), send(part(OVER_UP, 0), DOWN)
    shared = {who: share(at(who)) for who in (UP, DOWN, OVER, OVER_UP, OVER_DOWN)}
    halves_shared = {
        (who, i): share(part(who, i)) for who in (FAR, OVER_FAR) for i in (0, 1)
    }

    def begin():
        start_all(list(first.values()) + [own_share])

    def one():
        first[UP].wait_recv()
        start_all([far_high, shared[DOWN]])

    def two():
        first[DOWN].wait_recv()
        start_all([far_low, shared[UP]])

    def three():
        first[OVER].wait_recv()
        start_all([second[UP], second[DOWN], shared[OVER]])

    def four():
        far_high.wait_recv()
        halves_shared[FAR, 1].start()
        far_low.wait_recv()
        halves_shared[FAR, 0].start()

    def five():
        second[UP].wait_recv()
        start_all([over_high, shared[OVER_DOWN]])
        second[DOWN].wait_recv()
        start_all([over_low, shared[OVER_UP]])

    def six():
        over_high.wait_recv()
        halves_shared[OVER_FAR, 1].start()
        over_low.wait_recv()
        halves_shared[OVER_FAR, 0].start()

    def finish():
        await_all([own_share] + list(shared.values()) + list(halves_shared.values()))

    return [begin, one, two, three, four, five, six, finish]


GATHER_DATA = 19
HELD = (FAR, MATE, RIGHT, LEFT, ME)


def scatter_tensor(wires, moves, place, part_ref, slots, start, length, done):
    size = part_ref.shape[0] // TENSOR
    half = length // 2
    rows = lambda who, at=0, count=length: block(part_ref, place[who], size, start + at, count)
    slot = lambda i: slots.at[i, pl.ds(start, length)]
    piece = lambda i, p: slots.at[i, pl.ds(start + p * half, half)]
    load = lambda ref: ref[...].astype(f32)
    send = lambda source, target, to: wires.plan(source, target, on_tensor(place[to]))
    held = {who: moves.plan(rows(who), slot(10 + i)) for i, who in enumerate(HELD)}
    mine = lambda who: load(slot(10 + HELD.index(who)))
    mine_part = lambda who, p: load(piece(10 + HELD.index(who), p))
    far = send(rows(MATE_FAR), slot(0), MATE)
    to_right = send(rows(MATE_RIGHT), slot(1), RIGHT)
    to_left = send(rows(MATE_LEFT), slot(2), LEFT)
    pass_right = send(piece(3, 1), piece(4, 1), RIGHT)
    pass_left = send(piece(3, 0), piece(4, 0), LEFT)
    near = [
        send(rows(RIGHT, 0, half), piece(5, 0), RIGHT),
        send(rows(LEFT, half, half), piece(6, 1), LEFT),
    ]
    mate = send(slot(7), slot(8), MATE)
    near_late = [
        send(piece(9, 1), piece(5, 1), RIGHT),
        send(piece(9, 0), piece(6, 0), LEFT),
    ]

    def begin():
        start_all([far, to_right, to_left])
        start_all(held.values())

    def pass_on():
        held[FAR].wait()
        far.wait_recv()
        slot(3)[...] = (load(slot(0)) + mine(FAR)).astype(bf16)
        start_all([pass_right, pass_left])
        start_all(near)

    def to_mate():
        held[MATE].wait()
        to_right.wait_recv()
        to_left.wait_recv()
        slot(7)[...] = (load(slot(1)) + load(slot(2)) + mine(MATE)).astype(bf16)
        mate.start()

    def to_near():
        held[RIGHT].wait()
        pass_right.wait_recv()
        piece(9, 1)[...] = (load(piece(4, 1)) + mine_part(RIGHT, 1)).astype(bf16)
        near_late[0].start()
        held[LEFT].wait()
        pass_left.wait_recv()
        piece(9, 0)[...] = (load(piece(4, 0)) + mine_part(LEFT, 0)).astype(bf16)
        near_late[1].start()

    def finish():
        held[ME].wait()
        await_all(near + near_late + [mate])
        done(start, length, mine(ME) + load(slot(5)) + load(slot(6)) + load(slot(8)))

    return [begin, pass_on, to_mate, to_near, finish]


SCATTER_TENSOR = 10
SLOTS = 15


def scatter_ring(wires, moves, place, part_ref, slots, start, length, done):
    size = part_ref.shape[0] // RING
    half = length // 2
    rows = lambda who, at, count: block(part_ref, place[X_STEM + who], size, start + at, count)
    slot = lambda i: slots.at[i, pl.ds(start, length)]
    piece = lambda i, p: slots.at[i, pl.ds(start + p * half, half)]
    load = lambda ref: ref[...].astype(f32)
    send = lambda source, target, to: wires.plan(source, target, on_tensor(place[to]))
    held = {
        who: moves.plan(rows(who, 0, length), slot(4 + i))
        for i, who in enumerate((RIGHT, LEFT, ME))
    }
    pass_right = send(rows(FAR, half, half), piece(0, 1), RIGHT)
    pass_left = send(rows(FAR, 0, half), piece(0, 0), LEFT)
    near = [
        send(rows(RIGHT, 0, half), piece(1, 0), RIGHT),
        send(rows(LEFT, half, half), piece(2, 1), LEFT),
    ]
    near_late = [
        send(piece(3, 1), piece(1, 1), RIGHT),
        send(piece(3, 0), piece(2, 0), LEFT),
    ]

    def begin():
        start_all([pass_right, pass_left] + near)
        start_all(held.values())

    def to_near():
        held[RIGHT].wait()
        pass_right.wait_recv()
        piece(3, 1)[...] = (load(piece(0, 1)) + load(piece(4, 1))).astype(bf16)
        near_late[0].start()
        held[LEFT].wait()
        pass_left.wait_recv()
        piece(3, 0)[...] = (load(piece(0, 0)) + load(piece(5, 0))).astype(bf16)
        near_late[1].start()

    def finish():
        held[ME].wait()
        await_all(near + near_late)
        done(start, length, load(slot(6)) + load(slot(1)) + load(slot(2)))

    return [begin, to_near, finish]


SCATTER_RING = 6
RING_SLOTS = 7


def scatter_data(wires, place, core_mate, part_ref, given, added, slots, out_ref):
    size = part_ref.shape[0] // DATA
    half = size // 2
    load = lambda ref: ref[...].astype(f32)
    number = {name: i for i, name in enumerate(NAMES)}
    mine = lambda name: added.at[number[name]]
    mine_part = lambda name, p: added.at[number[name], pl.ds(p * half, half)]
    slot = lambda i: slots.at[i]
    piece = lambda i, p: slots.at[i, pl.ds(p * half, half)]
    send = lambda source, target, to: wires.plan(source, target, on_data(place[to]))
    swaps = [
        wires.plan(
            block(part_ref, core_mate[name], size), given.at[i], on_data(core_mate[ME])
        )
        for i, name in enumerate(NAMES)
    ]
    sides = ("", OVER_STEM)
    passed = [
        (
            send(mine_part(side + FAR, 1), piece(i, 1), UP),
            send(mine_part(side + FAR, 0), piece(i, 0), DOWN),
        )
        for i, side in enumerate(sides)
    ]
    near = [
        (
            send(mine_part(side + UP, 0), piece(2 + i, 0), UP),
            send(mine_part(side + DOWN, 1), piece(4 + i, 1), DOWN),
        )
        for i, side in enumerate(sides)
    ]
    near_late = [
        (
            send(mine_part(side + UP, 1), piece(2 + i, 1), UP),
            send(mine_part(side + DOWN, 0), piece(4 + i, 0), DOWN),
        )
        for i, side in enumerate(sides)
    ]
    last = send(slot(6), slot(7), OVER)

    def add_up(name):
        swaps[number[name]].wait_recv()
        total = load(given.at[number[name]]) + load(block(part_ref, place[name], size))
        mine(name)[...] = total.astype(bf16)

    def begin():
        start_all(swaps)

    def fars():
        for i in (1, 0):
            add_up(sides[i] + FAR)
            start_all(passed[i])

    def nears():
        for i in (1, 0):
            add_up(sides[i] + UP)
            add_up(sides[i] + DOWN)
            start_all(near[i])
        add_up(ME)
        add_up(OVER)

    def joins():
        for i in (1, 0):
            side = sides[i]
            for k, target in enumerate((mine_part(side + UP, 1), mine_part(side + DOWN, 0))):
                passed[i][k].wait_recv()
                target[...] = (load(target) + load(piece(i, 1 - k))).astype(bf16)
                near_late[i][k].start()

    def cross():
        await_all(near[1] + near_late[1])
        slot(6)[...] = (load(mine(OVER)) + load(slot(3)) + load(slot(5))).astype(bf16)
        last.start()

    def own():
        await_all(near[0] + near_late[0])
        out_ref[...] = load(mine(ME)) + load(slot(2)) + load(slot(4))

    def finish():
        last.wait_recv()
        out_ref[...] += load(slot(7))

    return [begin, fars, nears, joins, cross, own, finish]


SCATTER_DATA = 21


def rms_rows(values):
    return lax.rsqrt(row_total(values * values) * (1.0 / D) + norm_eps)


def rms_back(values, scale, gain, grad):
    shared = grad * gain
    inner = row_total(shared * values) * (1.0 / D)
    return scale * shared - values * (scale * scale * scale * inner)


def live_rows(length_ref, start, length, size):
    first = lax.axis_index(AT_TENSOR) * size + start
    rows = first + lax.broadcasted_iota(jnp.int32, (length, 1), 0)
    return (rows < length_ref[0]).astype(f32)


def fold(ref, first, line):
    for i in range(line.shape[1] // DK):
        ref[first + i : first + i + 1, :] = line[:, i * DK : (i + 1) * DK]


def start_kernel(
    length_ref, x_ref, cot_ref, gain_ref, q_ref, k_ref, v_ref, g_ref, decay_ref, out_w_ref,
    gate_ref, up_ref, down_ref, qc_ref, kc_ref, vc_ref, log_ref, bias_ref,
    first_ref, full_ref, fed_ref, ffn_ref, alt_ref, conv_ref, dec_ref,
    own, pack, send, recv, local,
):
    place = tensor_places()
    data_place, core_mate = data_places()
    x = x_ref[...].astype(f32)
    own[...] = (x * rms_rows(x) * gain_ref[...]).astype(bf16)
    pack[:, :DK] = q_ref[...]
    pack[:, DK : 2 * DK] = k_ref[...]
    pack[:, 2 * DK : QKV] = v_ref[...]
    pack[:, QKV:GATE_END] = g_ref[...]
    decay = jnp.zeros((PRE - GATE_END - 2, pack.shape[0]), f32)
    decay = jnp.concatenate([decay_ref[...].astype(f32), decay], axis=0)
    pack[:, GATE_END:PRE] = jnp.transpose(decay).astype(bf16)
    pack[:, PRE:MIX] = out_w_ref[...]
    greet(tensor_near(place) + data_near(data_place, core_mate))
    moves = Moves(local)
    wires = Wires(send, recv)
    keep = [
        moves.plan(own, block(first_ref, place[ME], own.shape[0])),
        moves.plan(pack, block(full_ref, data_place[ME], pack.shape[0])),
    ]
    size = own.shape[0]
    half = size // SPLIT
    parts = [
        gather_tensor(wires, place, own, first_ref, i * half, half) for i in range(SPLIT)
    ] + [gather_data(wires, data_place, core_mate, pack, full_ref)]
    for stages in parts:
        stages[0]()
    start_all(keep)
    fed_ref[...] = (cot_ref[...].astype(f32) * live_rows(length_ref, 0, size, size)).astype(bf16)
    ff = gate_ref.shape[1]
    ffn_ref[:, :ff] = gate_ref[...]
    ffn_ref[:, ff : 2 * ff] = up_ref[...]
    ffn_ref[:, 2 * ff :] = down_ref[...]
    swap = wires.plan(ffn_ref, alt_ref, on_tensor(place[MATE]))
    swap.start()
    conv_ref[...] = jnp.zeros_like(conv_ref)
    conv_ref[0:4, :DK] = qc_ref[...]
    conv_ref[0:4, DK : 2 * DK] = kc_ref[...]
    conv_ref[0:4, 2 * DK :] = vc_ref[...]
    dec_ref[...] = jnp.zeros_like(dec_ref)
    dec_ref[0:1, :] = -jnp.exp(jnp.broadcast_to(log_ref[...], (1, DK)))
    dec_ref[1:2, :] = jnp.broadcast_to(bias_ref[...], (1, DK))
    together(*[stages[1:] for stages in parts])
    swap.wait_recv()
    wires.flush()
    for copy in keep:
        copy.wait()


def flow(wires, moves, place, part_ref, slots, own, out_ref, done, scatter, gather):
    size = own.shape[0]
    length = size // SPLIT
    mine = place[ME] if out_ref.shape[0] == TENSOR * size else place[X_ME]
    parts = []
    for i in range(SPLIT):
        sums = scatter(wires, moves, place, part_ref, slots, i * length, length, done)
        spread = gather(wires, place, own, out_ref, i * length, length)
        keep = moves.plan(
            own.at[pl.ds(i * length, length)], block(out_ref, mine, size, i * length, length)
        )

        def join(last=sums[-1], begin=spread[0], keep=keep):
            last()
            begin()
            keep.start()

        def finish(last=spread[-1], keep=keep):
            last()
            keep.wait()

        parts.append(sums[:-1] + [join] + spread[1:-1] + [finish])
    return parts


def middle_kernel(
    part_ref, x_ref, gain_ref, length_ref, alt_own, middle_ref, second_ref, alt_ref, slots, own,
    send, recv, local,
):
    place = tensor_places()
    data_place, core_mate = data_places()
    greet(tensor_near(place) + data_near(data_place, core_mate))
    wires, moves = Wires(send, recv), Moves(local)

    def done(start, length, mixed):
        rows = pl.ds(start, length)
        live = live_rows(length_ref, start, length, own.shape[0])
        middle = x_ref[rows, :].astype(f32) + live * mixed
        middle_ref[rows, :] = middle
        own[rows, :] = (middle * rms_rows(middle) * gain_ref[...]).astype(bf16)

    parts = flow(wires, moves, place, part_ref, slots, own, second_ref, done,
                 scatter_tensor, gather_ring)
    weights = gather_data(wires, data_place, core_mate, alt_own, alt_ref)
    keep = moves.plan(alt_own, block(alt_ref, data_place[ME], alt_own.shape[0]))

    def nothing():
        pass

    together(*parts, weights[:1] + [keep.start] + weights[1:-1] + [nothing, weights[-1]])
    keep.wait()
    wires.flush()


def turn_kernel(
    part_ref, middle_ref, cot_ref, gain_ref, length_ref, second_any, fed_any, acts_any,
    hidden_any, ffn_any, alt_acts_any, alt_hidden_any, alt_any,
    grad_ref, mixed_ref, gain_grad_ref, ffn_part_any, early_out,
    slots, own, gain_acc, second, fed, acts, hidden, ffn, alt_acts, alt_hidden, alt, ffn_part,
    wgrad, alt_wgrad, given, added, data_slots, alt_given, alt_added, alt_slots, alt_out,
    swap_own, swap_slot, send, recv, local,
):
    place = tensor_places()
    data_place, core_mate = data_places()
    greet(tensor_near(place) + data_near(data_place, core_mate))
    wires, moves = Wires(send, recv), Moves(local)
    gain_acc[...] = jnp.zeros_like(gain_acc)

    def done(start, length, second_in):
        rows = pl.ds(start, length)
        middle = middle_ref[rows, :]
        scale = rms_rows(middle)
        gain_acc[0:1, :] += jnp.sum(second_in * middle * scale, axis=0, keepdims=True)
        grad = cot_ref[rows, :].astype(f32) + rms_back(middle, scale, gain_ref[...], second_in)
        grad_ref[rows, :] = grad
        own[rows, :] = (live_rows(length_ref, start, length, own.shape[0]) * grad).astype(bf16)

    parts = flow(wires, moves, place, part_ref, slots, own, mixed_ref, done,
                 scatter_ring, gather_tensor)
    mine = scatter_data(
        wires, data_place, core_mate, wgrad, given, added, data_slots, early_out
    )
    other = scatter_data(
        wires, data_place, core_mate, alt_wgrad, alt_given, alt_added, alt_slots, alt_out
    )
    swap = wires.plan(swap_own, swap_slot, on_tensor(place[MATE]))
    loads = [
        moves.plan(source, target)
        for source, target in (
            (second_any, second), (alt_acts_any, alt_acts), (fed_any, fed),
            (alt_hidden_any, alt_hidden), (acts_any, acts), (hidden_any, hidden), (ffn_any, ffn),
            (alt_any, alt),
        )
    ]
    store = moves.plan(ffn_part, ffn_part_any)
    ff = hidden.shape[1]
    tile = 256

    def weight_work(target, acts_side, hidden_side, i):
        at = pl.ds(i * tile, tile)
        target[at, : 2 * ff] = mm(second[:, at], acts_side[...], 0, 0).astype(bf16)
        target[at, 2 * ff :] = mm(fed[:, at], hidden_side[...], 0, 0).astype(bf16)

    def everywhere(i):
        for stages in parts:
            stages[i]()

    everywhere(0)
    start_all(loads)
    for copy in loads[:4]:
        copy.wait()
    tiles = D // tile
    for i in range(tiles):
        weight_work(alt_wgrad, alt_acts, alt_hidden, i)
    other[0]()
    for copy in loads[4:6]:
        copy.wait()
    weight_work(wgrad, acts, hidden, 0)
    everywhere(1)
    other[1]()
    for i in range(1, tiles):
        weight_work(wgrad, acts, hidden, i)
    mine[0]()
    other[2]()
    parts[0][2]()
    mine[1]()
    parts[1][2]()
    mine[2]()
    for copy in loads[6:]:
        copy.wait()
    for i in range(ffn_part.shape[0] // tile):
        at = pl.ds(i * tile, tile)
        terms = mm(hidden[at, :], ffn[:, 2 * ff :], 1, 1)
        terms = terms + mm(alt_hidden[at, :], alt[:, 2 * ff :], 1, 1)
        ffn_part[at, :] = terms.astype(bf16)
    store.start()
    everywhere(3)
    everywhere(4)
    other[3]()
    everywhere(5)
    mine[3]()
    everywhere(6)
    everywhere(7)
    other[4]()
    everywhere(8)
    mine[4]()
    other[5]()
    other[6]()
    swap_own[...] = alt_out[...].astype(bf16)
    swap.start()
    mine[5]()
    mine[6]()
    everywhere(9)
    fold(gain_grad_ref, 0, gain_acc[0:1, :])
    swap.wait_recv()
    early_out[...] += swap_slot[...].astype(f32)
    wires.flush()
    store.wait()


def ffn_kernel(
    second_ref, fed_ref, ffn_ref, alt_ref, part_ref, acts_ref, hidden_ref, alt_acts_ref,
    alt_hidden_ref,
):
    ff = hidden_ref.shape[1]
    total = None
    for weights, acts_out, hidden_out in (
        (ffn_ref, acts_ref, hidden_ref), (alt_ref, alt_acts_ref, alt_hidden_ref),
    ):
        acts = mm(second_ref[...], weights[:, : 2 * ff])
        gate, up = acts[:, :ff], acts[:, ff:]
        hidden_grad = mm(fed_ref[...], weights[:, 2 * ff :])
        sig = jax.nn.sigmoid(gate)
        act = gate * sig
        hidden_out[...] = (act * up).astype(bf16)
        acts_out[:, :ff] = (hidden_grad * up * sig * (1.0 + gate * (1.0 - sig))).astype(bf16)
        acts_out[:, ff:] = (hidden_grad * act).astype(bf16)
        part = mm(acts_out[...], weights[:, : 2 * ff], 1, 1)
        total = part if total is None else total + part
    part_ref[...] = total.astype(bf16)


def end_kernel(
    part_ref, x_ref, grad_ref, gain_ref, ffn_gain_ref, small_ref, head_ref, first_any, pre_any, mixed_grad_any, mixed_any,
    input_ref, late_out, gains_out, head_out,
    slots, first, pre, mixed_grad, mixed, part, late, late_given, late_added, late_slots, gain_acc, gain_own, gain_slots, wide_own, wide_slots,
    head_slots, send, recv, local,
):
    place = tensor_places()
    data_place, core_mate = data_places()
    me, data_me = place[ME], data_place[ME]
    others = [lax.rem(me + i, TENSOR) for i in range(1, TENSOR)]
    data_others = [lax.rem(data_me + i, DATA) for i in range(1, DATA)]
    greet([on_tensor(i) for i in others] + [on_data(i) for i in data_others])
    wires, moves = Wires(send, recv), Moves(local)
    gain_acc[...] = jnp.zeros_like(gain_acc)
    length = x_ref.shape[0] // SPLIT

    def done(start, length, first_in):
        rows = pl.ds(start, length)
        x = x_ref[rows, :].astype(f32)
        scale = rms_rows(x)
        input_ref[rows, :] = grad_ref[rows, :] + rms_back(x, scale, gain_ref[...], first_in)

    flows = [
        scatter_tensor(wires, moves, place, part_ref, slots, i * length, length, done)
        for i in range(SPLIT)
    ]
    later = scatter_data(
        wires, data_place, core_mate, late, late_given, late_added, late_slots, late_out
    )
    heads = [
        wires.plan(head_ref, head_slots.at[i], on_data(to)) for i, to in enumerate(data_others)
    ]
    near = [
        wires.plan(gain_own, gain_slots.at[i], on_tensor(to)) for i, to in enumerate(others)
    ]
    wide_ones = [
        wires.plan(wide_own, wide_slots.at[i], on_data(to)) for i, to in enumerate(data_others)
    ]
    loads = [
        moves.plan(source, target)
        for source, target in (
            (pre_any, pre), (first_any, first), (mixed_any, mixed), (mixed_grad_any, mixed_grad),
            (part_ref, part),
        )
    ]

    def everywhere(i):
        for stages in flows:
            stages[i]()

    everywhere(0)
    start_all(loads)
    tile = 256

    def make_late(i):
        at = pl.ds(i * tile, tile)
        late[at, :PRE] = mm(first[:, at], pre[...], 0, 0).astype(bf16)
        late[at, PRE:] = mm(mixed_grad[:, at], mixed[...], 0, 0).astype(bf16)

    for copy in loads:
        copy.wait()
    make_late(0)
    make_late(1)
    everywhere(1)
    make_late(2)
    make_late(3)
    later[0]()
    start_all(heads)
    everywhere(2)
    later[1]()
    later[2]()
    for i in range(first.shape[0] // 256):
        at = pl.ds(i * 256, 256)
        normed = first[at, :].astype(f32) * part[at, :].astype(f32)
        gain_acc[0:1, :] += jnp.sum(normed, axis=0, keepdims=True)
    gain_own[...] = jnp.zeros_like(gain_own)
    fold(gain_own, 0, gain_acc[0:1, :] / gain_ref[...])
    gain_own[8:16, :] = ffn_gain_ref[...]
    fold(gain_own, 16, small_ref[0:1, :])
    start_all(near)
    everywhere(3)
    later[3]()
    await_all(near)
    total = gain_own[...]
    for i in range(TENSOR - 1):
        total = total + gain_slots[i]
    wide_own[...] = total
    start_all(wide_ones)
    await_all(heads)
    total = head_ref[...]
    for i in range(DATA - 1):
        total = total + head_slots[i]
    head_out[...] = total
    later[4]()
    await_all(wide_ones)
    total = wide_own[...]
    for i in range(DATA - 1):
        total = total + wide_slots[i]
    gains_out[...] = total
    later[5]()
    everywhere(4)
    later[6]()
    wires.flush()


END_COPIES = SCATTER_TENSOR * SPLIT + SCATTER_DATA + TENSOR - 1 + 2 * (DATA - 1)
GAINS = 24


def finish_kernel(
    output_ref, input_ref, early_ref, late_ref, gains_ref, head_ref,
    output, input_grad, mixer_gain, query, key, value, gate, decay, query_conv, key_conv,
    value_conv, decay_log, decay_bias, head_gain, out_weight, ffn_gain, ffn_gate, ffn_up,
    ffn_down,
):
    output[...] = output_ref[...]
    input_grad[...] = input_ref[...]
    mixer_gain[...] = gains_ref[0:8, :]
    ffn_gain[...] = gains_ref[8:16, :]
    head_gain[...] = gains_ref[16:18, :]
    query[...] = late_ref[:, :DK]
    key[...] = late_ref[:, DK : 2 * DK]
    value[...] = late_ref[:, 2 * DK : QKV]
    gate[...] = late_ref[:, QKV:GATE_END]
    decay[...] = jnp.transpose(late_ref[:, GATE_END:PRE])[0:2, :]
    out_weight[...] = late_ref[:, PRE:MIX]
    ff = ffn_gate.shape[1]
    ffn_gate[...] = early_ref[:, :ff]
    ffn_up[...] = early_ref[:, ff : 2 * ff]
    ffn_down[...] = early_ref[:, 2 * ff :]
    query_conv[...] = head_ref[0:4, :DK]
    key_conv[...] = head_ref[0:4, DK : 2 * DK]
    value_conv[...] = head_ref[0:4, 2 * DK :]
    decay_log[...] = head_ref[4:5, 0:1]
    decay_bias[...] = head_ref[5:6, 0:1]


V, H, S = "vmem", "any", "smem"
SPECS = {
    V: lambda: pl.BlockSpec(memory_space=pltpu.VMEM),
    H: lambda: pl.BlockSpec(memory_space=pl.ANY),
    S: lambda: pl.BlockSpec(memory_space=pltpu.SMEM),
}


def communicate(kernel, number, ins, outs, scratch, copies, moves, name):
    sems = [pltpu.SemaphoreType.DMA((count,)) for count in (copies, copies, moves)]
    return pl.pallas_call(
        kernel,
        out_shape=[jax.ShapeDtypeStruct(shape, kind) for shape, kind, _ in outs],
        in_specs=[SPECS[space]() for _, space in ins],
        out_specs=[SPECS[space]() for _, _, space in outs],
        scratch_shapes=[pltpu.VMEM(shape, kind) for shape, kind in scratch] + sems,
        compiler_params=pltpu.CompilerParams(
            collective_id=number, has_side_effects=True, vmem_limit_bytes=58 * 1024 * 1024
        ),
        name=name,
    )(*[item for item, _ in ins])


def call_ffn(second_rows, fed_rows, ffn_full, alt_full):
    rows = second_rows.shape[0]
    ff = ffn_full.shape[1] // 3
    step = 256
    tall = lambda width: pl.BlockSpec((step, width), lambda i: (i, 0))
    fixed = pl.BlockSpec(ffn_full.shape, lambda i: (0, 0))
    made = lambda width: jax.ShapeDtypeStruct((rows, width), bf16)
    return pl.pallas_call(
        ffn_kernel,
        grid=(rows // step,),
        in_specs=[tall(D), tall(D), fixed, fixed],
        out_specs=[tall(D), tall(2 * ff), tall(ff), tall(2 * ff), tall(ff)],
        out_shape=[made(D), made(2 * ff), made(ff), made(2 * ff), made(ff)],
        compiler_params=pltpu.CompilerParams(
            dimension_semantics=(ARBITRARY,), vmem_limit_bytes=58 * 1024 * 1024
        ),
        name=FFN,
    )(second_rows, fed_rows, ffn_full, alt_full)


def shards(
    block_input, out_cotangent, lengths, mixer_gain, query_weight, key_weight, value_weight,
    output_gate_weight, decay_weight, query_conv, key_conv, value_conv, decay_log, decay_bias,
    head_gain, out_weight, ffn_gain, ffn_gate, ffn_up, ffn_down,
):
    size = block_input.shape[0]
    rows = size * TENSOR
    depth = query_weight.shape[0]
    ff = ffn_gate.shape[1]
    line = lambda item: item.reshape(1, -1)
    vmem = lambda *items: [(item, V) for item in items]
    hbm = lambda *items: [(item, H) for item in items]
    length = [(lengths, S)]
    slots = ((SLOTS, size, D), bf16)
    own = ((size, D), bf16)
    first_rows, full, fed_own, ffn_own, alt_own, conv, dec = communicate(
        start_kernel, 1,
        length + vmem(
            block_input, out_cotangent, line(mixer_gain), query_weight, key_weight, value_weight,
            output_gate_weight, decay_weight.reshape(depth, 2).T, out_weight.T, ffn_gate, ffn_up,
            ffn_down.T, query_conv, key_conv, value_conv, line(decay_log), line(decay_bias),
        ),
        [((rows, D), bf16, H), ((D, MIX), bf16, H), ((size, D), bf16, V),
         ((depth, 3 * ff), bf16, V), ((depth, 3 * ff), bf16, V), ((8, QKV), f32, V),
         ((8, DK), f32, V)],
        [own, ((depth, MIX), bf16)], GATHER_TENSOR * SPLIT + GATHER_DATA + 1, 2, "start_gathers",
    )
    hg = line(head_gain)
    forward = call_forward(first_rows, full, conv, dec, hg, fed_own, ffn_own)
    proj, mixed_part, mixed_rows, o, t, u, qe, a, s, tails, fed_rows, ffn_full = forward
    middle, second_rows, alt_full = communicate(
        middle_kernel, 2,
        hbm(mixed_part) + vmem(block_input, line(ffn_gain)) + length + hbm(alt_own),
        [((size, D), f32, V), ((rows // 2, D), bf16, H), ((D, 3 * ff), bf16, H)],
        [slots, own], (GATHER_RING + SCATTER_TENSOR) * SPLIT + GATHER_DATA,
        (len(HELD) + 1) * SPLIT + 1, "middle_sums",
    )
    second_part, acts, hidden, alt_acts, alt_hidden = call_ffn(
        second_rows, fed_rows, ffn_full, alt_full
    )
    block_rows = D // DATA
    half_rows = rows // 2
    early_block, late_block = ((8, block_rows, 3 * ff), bf16), ((8, block_rows, MIX), bf16)
    early_row, early_all = (block_rows, 3 * ff), ((D, 3 * ff), bf16)
    middle_grad, mixed_grad, ffn_gain_grad, ffn_part, early = communicate(
        turn_kernel, 3,
        hbm(second_part) + vmem(middle, out_cotangent, line(ffn_gain)) + length
        + hbm(second_rows, fed_rows, acts, hidden, ffn_full, alt_acts, alt_hidden, alt_full),
        [((size, D), f32, V), ((rows, D), bf16, H), ((8, DK), f32, V),
         ((half_rows, D), bf16, H), (early_row, f32, V)],
        [((RING_SLOTS, size, D), bf16), own, ((8, D), f32)] + [((half_rows, D), bf16)] * 2
        + [((half_rows, 2 * ff), bf16), ((half_rows, ff), bf16), early_all] * 2
        + [((half_rows, D), bf16), early_all, early_all] + [early_block] * 6
        + [(early_row, f32), (early_row, bf16), (early_row, bf16)],
        (GATHER_TENSOR + SCATTER_RING) * SPLIT + 2 * SCATTER_DATA + 1, 4 * SPLIT + 9,
        "turn_sums",
    )
    pre_grads, first_part, head_grads, small, block_output = call_backward(
        mixed_grad, full, (proj, o, t, u, qe, a, s, tails), conv, dec, hg, ffn_part, middle,
        lengths,
    )
    input_grad, late, gains, heads = communicate(
        end_kernel, 4,
        hbm(first_part)
        + vmem(block_input, middle_grad, line(mixer_gain), ffn_gain_grad, small, head_grads)
        + hbm(first_rows, pre_grads, mixed_grad, mixed_rows),
        [((size, D), f32, V), ((block_rows, MIX), f32, V), ((GAINS, DK), f32, V),
         ((8, QKV), f32, V)],
        [slots, ((rows, D), bf16), ((rows, PRE), bf16), ((rows, D), bf16), ((rows, DV), bf16),
         ((rows, D), bf16), ((D, MIX), bf16)] + [late_block] * 3
        + [((8, D), f32), ((GAINS, DK), f32), ((TENSOR - 1, GAINS, DK), f32),
           ((GAINS, DK), f32), ((DATA - 1, GAINS, DK), f32), ((DATA - 1, 8, QKV), f32)],
        END_COPIES, len(HELD) * SPLIT + 5, "end_sums",
    )
    made = lambda *shape: jax.ShapeDtypeStruct(shape, f32)
    whole = lambda count: [pl.BlockSpec(memory_space=pltpu.VMEM)] * count
    outs = pl.pallas_call(
        finish_kernel,
        in_specs=whole(6),
        out_specs=whole(19),
        out_shape=[
            jax.ShapeDtypeStruct((size, D), bf16), made(size, D), made(8, DK), made(depth, DK),
            made(depth, DK), made(depth, DV), made(depth, DV), made(2, depth), made(4, DK),
            made(4, DK), made(4, DV), made(1, 1), made(1, 1), made(2, DK), made(depth, DV),
            made(8, DK), made(depth, ff), made(depth, ff), made(depth, ff),
        ],
        compiler_params=pltpu.CompilerParams(vmem_limit_bytes=58 * 1024 * 1024),
        name="finish",
    )(block_output, input_grad, early, late, gains, heads)
    outs = [item.T if i in (7, 14, 18) else item for i, item in enumerate(outs)]
    shapes = {2: (D,), 7: (depth, 1, 2), 11: (1,), 12: (1,), 13: (DV,), 15: (D,)}
    return tuple(
        item.reshape(shapes[i]) if i in shapes else item for i, item in enumerate(outs)
    )


def solution(mesh):
    rows = P((DP, AT_TENSOR), None)
    tile = P(DP, AT_TENSOR)
    taps = P(None, AT_TENSOR)
    turned = P(AT_TENSOR, DP)
    decay = P(DP, AT_TENSOR, None)
    head = P(AT_TENSOR)
    return jax.shard_map(
        shards,
        mesh=mesh,
        in_specs=(
            rows, rows, P(DP), P(), tile, tile, tile, tile, decay, taps, taps, taps, head, head,
            P(), turned, P(), tile, tile, turned,
        ),
        out_specs=(
            rows, rows, P(), tile, tile, tile, tile, decay, taps, taps, taps, head, head,
            P(), turned, P(), tile, tile, turned,
        ),
        check_vma=False,
    )
```
